32 devices in a mesh: dp: 8 (over z, x), mp: 4 (over y, core).
Axes of the slice: x: 2, y: 2, z: 4, core: 2. Of those that a mesh axis runs over, the one named last changes fastest.
Arguments:
- inputs: bfloat16 [20224, 512], P(('dp', 'mp')), may hold values from -6 to 6
- segments: int32 [8, 2528], P('dp'), may hold values from 0 to 5, never falling along the last dimension, each value on 1 to 842 neighbouring positions
- cotangent: bfloat16 [20224, 512], P(('dp', 'mp')), may hold values from -6 to 6
- inner_first: float32 [512, 2048], P(None, 'mp'), may hold values from -0.25 to 0.25
- outer_first: float32 [2048, 512], P('mp'), may hold values from -0.25 to 0.25
- mixer_input: float32 [512, 2, 512], P(None, None, 'mp'), may hold values from -0.25 to 0.25
- mixer_output: float32 [512, 512], P('mp'), may hold values from -0.5 to 0.5
- inner_second: float32 [512, 2048], P(None, 'mp'), may hold values from -0.25 to 0.25
- outer_second: float32 [2048, 512], P('mp'), may hold values from -0.25 to 0.25
- norm_params: float32 [5, 2, 512], replicated, may hold values from -0.5 to 1.6, as said below
- conv_taps: float32 [15, 512], replicated, may hold values from -1.5 to 1.5
- state_maps: float32 [8, 2, 32, 64], P('mp'), may hold values from -0.75 to 0.75
- state_rates: float32 [8, 32], P('mp'), may hold values from -8.5 to -3
- inner_first_moment: float32 [512, 2048], P(None, 'mp'), may hold values from -160 to 160
- outer_first_moment: float32 [2048, 512], P('mp'), may hold values from -160 to 160
- mixer_input_moment: float32 [512, 2, 512], P(None, None, 'mp'), may hold values from -160 to 160
- mixer_output_moment: float32 [512, 512], P('mp'), may hold values from -160 to 160
- inner_second_moment: float32 [512, 2048], P(None, 'mp'), may hold values from -160 to 160
- outer_second_moment: float32 [2048, 512], P('mp'), may hold values from -160 to 160
- norm_params_moment: float32 [5, 2, 512], replicated, may hold values from -256 to 256
- conv_taps_moment: float32 [15, 512], replicated, may hold values from -256 to 256
- state_maps_moment: float32 [8, 2, 32, 64], P('mp'), may hold values from -256 to 256
- state_rates_moment: float32 [8, 32], P('mp'), may hold values from -256 to 256
Outputs:
- layer_output: bfloat16 [20224, 512], P(('dp', 'mp'))
- input_grad: float32 [20224, 512], P(('dp', 'mp'))
- inner_first_grad: float32 [512, 2048], P(None, 'mp')
- inner_first_moment_new: float32 [512, 2048], P(None, 'mp')
- inner_first_new: float32 [512, 2048], P(None, 'mp')
- outer_first_grad: float32 [2048, 512], P('mp')
- outer_first_moment_new: float32 [2048, 512], P('mp')
- outer_first_new: float32 [2048, 512], P('mp')
- mixer_input_grad: float32 [512, 2, 512], P(None, None, 'mp')
- mixer_input_moment_new: float32 [512, 2, 512], P(None, None, 'mp')
- mixer_input_new: float32 [512, 2, 512], P(None, None, 'mp')
- mixer_output_grad: float32 [512, 512], P('mp')
- mixer_output_moment_new: float32 [512, 512], P('mp')
- mixer_output_new: float32 [512, 512], P('mp')
- inner_second_grad: float32 [512, 2048], P(None, 'mp')
- inner_second_moment_new: float32 [512, 2048], P(None, 'mp')
- inner_second_new: float32 [512, 2048], P(None, 'mp')
- outer_second_grad: float32 [2048, 512], P('mp')
- outer_second_moment_new: float32 [2048, 512], P('mp')
- outer_second_new: float32 [2048, 512], P('mp')
- norm_params_grad: float32 [5, 2, 512], replicated
- norm_params_moment_new: float32 [5, 2, 512], replicated
- norm_params_new: float32 [5, 2, 512], replicated
- conv_taps_grad: float32 [15, 512], replicated
- conv_taps_moment_new: float32 [15, 512], replicated
- conv_taps_new: float32 [15, 512], replicated
- state_maps_grad: float32 [8, 2, 32, 64], P('mp')
- state_maps_moment_new: float32 [8, 2, 32, 64], P('mp')
- state_maps_new: float32 [8, 2, 32, 64], P('mp')
- state_rates_grad: float32 [8, 32], P('mp')
- state_rates_moment_new: float32 [8, 32], P('mp')
- state_rates_new: float32 [8, 32], P('mp')
The draws below stay inside these ranges and needn't reach their ends.
Inputs may be any that keep to these rules, and one draw needn't show every extreme that they name: `segments`: along each row the ids never fall; each row holds 6 utterances of 1 to 842 frames, one of exactly 842. `norm_params`: row 0 of each norm holds gains, row 1 biases.
All inputs are finite; a program needn't handle non-finite values.
Results may differ from the reference program's by a relative error of at most 0.019.
Values may be sent and summed in bfloat16 or wider, within the bound.
No kernel may reach another device: no remote copies, remote signals or barrier semaphores. Data moves between devices by JAX's collectives and lax.ppermute only.
A program may use at most 256 MiB of HBM per device.

```python
import math
import jax
import jax.numpy as jnp
import numpy as np
from jax import lax

D = 512
FF = 2048
HEADS = 8
STATE = 32
KSIZE = 15
LEN = 2528
SEGS = 6
NS_STEPS = 5
HD = 64
ROWS = 8
TOKENS = 20224
N_MP = 4


def draw_norm_params(key, part):
    gain_key = jax.random.fold_in(key, 11)
    bias_key = jax.random.fold_in(key, 23)
    gains = jnp.clip(1.0 + 0.2 * jax.random.normal(gain_key, (5, 1, D), jnp.float32), 0.4, 1.6)
    biases = jnp.clip(0.15 * jax.random.normal(bias_key, (5, 1, D), jnp.float32), -0.5, 0.5)
    return jnp.concatenate([gains, biases], axis=1)


def shard_levels(own_key, dims, cuts, smallest, high):
    def one(position, parts):
        draws = jax.random.uniform(jax.random.fold_in(jax.random.fold_in(own_key, 6), position), (parts,), jnp.float32, smallest / len(cuts), high / len(cuts))
        return jnp.repeat(jnp.exp(draws), dims[position] // parts).reshape((-1,) + (1,) * (len(dims) - position - 1))

    factor_of = one(*cuts[0])
    for cut in cuts[1:]:
        factor_of = factor_of * one(*cut)
    return factor_of


def length_profile(count, total, limit, lean):
    portions = [(1 << 20) // math.isqrt(rank ** lean) + 1 for rank in range(2, count + 1)]
    surplus, counts = total - limit - (count - 1), [1] * (count - 1)
    while surplus > 0:
        candidates = [i for i in range(count - 1) if counts[i] < limit]
        whole, left = sum([portions[i] for i in candidates]), surplus
        for i in candidates:
            extra = min(limit - counts[i], max(1, left * portions[i] // whole), surplus)
            counts[i] = counts[i] + extra
            surplus = surplus - extra
    return np.array([limit] + counts)


def ragged(key, number_of, total, reach, skew):
    if number_of == 2:
        one = jax.random.randint(key, (), max(1, total - reach), min(reach, total - 1) + 1)
        return jnp.stack([one, total - one])
    lengths = jnp.asarray(length_profile(number_of, total, reach, skew), jnp.int32)
    couples = (number_of - 1) // 2
    donor, receiver = lengths[1:1 + 2 * couples:2], lengths[2:2 + 2 * couples:2]
    room = jnp.minimum(donor - 1, reach - receiver)
    shifted = jax.random.randint(jax.random.fold_in(key, 1), (couples,), 0, 1 << 20) % (room + 1)
    lengths = lengths.at[1:1 + 2 * couples:2].set(donor - shifted).at[2:2 + 2 * couples:2].set(receiver + shifted)
    return lengths[jax.random.permutation(jax.random.fold_in(key, 2), number_of)]


def gaussian(stream_key, extent, width, most, split=(), dtype=jnp.bfloat16):
    drawn = jax.random.normal(stream_key, extent, jnp.float32) * width
    if len(split) > 0:
        drawn = shard_levels(stream_key, extent, split, -0.22, 0.18) * drawn
    return jnp.clip(drawn, min=-most, max=most).astype(dtype)


def setup_inputs(seed: int = 0) -> dict:
    key_of = jax.random.split(jax.random.key(seed), 24)
    inputs = gaussian(key_of[0], (TOKENS, D), 1.0, 6.0, ((0, 32),))
    segments = jax.vmap(lambda own: jnp.searchsorted(jnp.cumsum(ragged(own, SEGS, LEN, LEN // 3, 0)), jnp.arange(LEN), side="right"))(jax.random.split(key_of[1], ROWS)).reshape((ROWS, LEN)).astype(jnp.int32)
    cotangent = gaussian(key_of[2], (TOKENS, D), 1.0, 6.0, ((0, 32),))
    inner_first = gaussian(key_of[3], (D, FF), D ** -0.5, 0.25, ((1, 4),), jnp.float32)
    outer_first = gaussian(key_of[4], (FF, D), (FF // 4) ** -0.5, 0.25, ((0, 4),), jnp.float32)
    mixer_input = gaussian(key_of[5], (D, 2, D), D ** -0.5, 0.25, ((2, 4),), jnp.float32)
    mixer_output = gaussian(key_of[6], (D, D), (D // 4) ** -0.5, 0.5, ((0, 4),), jnp.float32)
    inner_second = gaussian(key_of[7], (D, FF), D ** -0.5, 0.25, ((1, 4),), jnp.float32)
    outer_second = gaussian(key_of[8], (FF, D), (FF // 4) ** -0.5, 0.25, ((0, 4),), jnp.float32)
    norm_params = draw_norm_params(jax.random.fold_in(key_of[23], 71), 0)
    conv_taps = gaussian(key_of[10], (KSIZE, D), KSIZE ** -0.5, 1.5, (), jnp.float32)
    state_maps = gaussian(key_of[11], (HEADS, 2, STATE, HD), HD ** -0.5, 0.75, ((0, 4),), jnp.float32)
    state_rates = jnp.clip(-8.5 + 5.5 * jax.random.uniform(key_of[12], (HEADS, STATE), jnp.float32) ** shard_levels(key_of[12], (HEADS, STATE), ((0, 4),), -0.2, 0.2), -8.5, -3.0)
    inner_first_moment = gaussian(key_of[13], (D, FF), (0.2 * TOKENS ** 0.5), 160.0, ((1, 4),), jnp.float32)
    outer_first_moment = gaussian(key_of[14], (FF, D), (0.2 * TOKENS ** 0.5), 160.0, ((0, 4),), jnp.float32)
    mixer_input_moment = gaussian(key_of[15], (D, 2, D), (0.2 * TOKENS ** 0.5), 160.0, ((2, 4),), jnp.float32)
    mixer_output_moment = gaussian(key_of[16], (D, D), (0.2 * TOKENS ** 0.5), 160.0, ((0, 4),), jnp.float32)
    inner_second_moment = gaussian(key_of[17], (D, FF), (0.2 * TOKENS ** 0.5), 160.0, ((1, 4),), jnp.float32)
    outer_second_moment = gaussian(key_of[18], (FF, D), (0.2 * TOKENS ** 0.5), 160.0, ((0, 4),), jnp.float32)
    norm_params_moment = gaussian(key_of[19], (5, 2, D), (0.3 * TOKENS ** 0.5), 256.0, (), jnp.float32)
    conv_taps_moment = gaussian(key_of[20], (KSIZE, D), (0.3 * TOKENS ** 0.5), 256.0, (), jnp.float32)
    state_maps_moment = gaussian(key_of[21], (HEADS, 2, STATE, HD), (0.3 * TOKENS ** 0.5), 256.0, ((0, 4),), jnp.float32)
    state_rates_moment = gaussian(key_of[22], (HEADS, STATE), (0.3 * TOKENS ** 0.5), 256.0, ((0, 4),), jnp.float32)
    return dict(inputs=inputs, segments=segments, cotangent=cotangent, inner_first=inner_first, outer_first=outer_first, mixer_input=mixer_input, mixer_output=mixer_output, inner_second=inner_second, outer_second=outer_second, norm_params=norm_params, conv_taps=conv_taps, state_maps=state_maps, state_rates=state_rates, inner_first_moment=inner_first_moment, outer_first_moment=outer_first_moment, mixer_input_moment=mixer_input_moment, mixer_output_moment=mixer_output_moment, inner_second_moment=inner_second_moment, outer_second_moment=outer_second_moment, norm_params_moment=norm_params_moment, conv_taps_moment=conv_taps_moment, state_maps_moment=state_maps_moment, state_rates_moment=state_rates_moment)


HIGH = lax.Precision.HIGHEST
COEF_A = 3.4445
COEF_B = -4.775
COEF_C = 2.0315
NORM_EPS = 1e-05
SMALL_FACTORS = (0.2, 0.2, 0.2, 4.0)

@jax.custom_vjp
def low(v):
    return lax.optimization_barrier(v.astype(jnp.bfloat16)).astype(jnp.float32)

@jax.custom_vjp
def low_back(v):
    return v

def low_keep(v):
    return (low(v), None)

def low_pass(kept, grad):
    return (grad,)

def back_keep(v):
    return (v, None)

def back_low(kept, grad):
    return (low(grad),)
low.defvjp(low_keep, low_pass)
low_back.defvjp(back_keep, back_low)

def matmul(left, right):
    return jnp.dot(left, right, precision=HIGH, preferred_element_type=jnp.float32)

def layer_norm(values, gain_row, bias_row):
    middle = lax.optimization_barrier(jnp.mean(values, axis=-1, keepdims=True))
    centred = values - middle
    spread = lax.optimization_barrier(jnp.mean(centred * centred, axis=-1, keepdims=True))
    return centred * lax.rsqrt(spread + NORM_EPS) * gain_row + bias_row

def swish(values):
    return values * jax.nn.sigmoid(values)

def combine(earlier, latter):
    return (earlier[0] * latter[0], latter[0] * earlier[1] + latter[1])

def mixer_core(signal, gate_part, state_maps, state_rates, boundary):
    decays = jnp.exp(-jnp.exp(state_rates))
    input_gain = jnp.sqrt(1.0 - decays * decays)
    driven = jnp.einsum('thc,hnc->thn', signal, state_maps[:, 0], precision=HIGH) * input_gain
    retain = (1.0 - boundary)[:, None, None] * decays
    states = lax.associative_scan(combine, (retain, driven), axis=0)[1]
    result = jnp.einsum('thn,hnc->thc', states, state_maps[:, 1], precision=HIGH)
    gated = result * swish(gate_part)
    return gated.reshape(gated.shape[0], -1)

def half_ffn(activation, up_weight, down_weight):
    pre_hidden = low_back(matmul(activation, low(up_weight)))
    gated = low(swish(pre_hidden))
    return low_back(matmul(gated, low(down_weight)))

def row_forward(params, inputs_row, segment_row):
    inner_first, outer_first, mixer_input, mixer_output, inner_second, outer_second, norm_params, conv_taps, state_maps, state_rates = params
    length = inputs_row.shape[0]
    margin = (KSIZE - 1) // 2
    boundary = jnp.concatenate([jnp.ones((1,), jnp.float32), (segment_row[1:] != segment_row[:-1]).astype(jnp.float32)])
    act_one = low(layer_norm(inputs_row, norm_params[0, 0], norm_params[0, 1]))
    stream_one = inputs_row + 0.5 * half_ffn(act_one, inner_first, outer_first)
    act_two = low(layer_norm(stream_one, norm_params[1, 0], norm_params[1, 1]))
    projected = low_back(matmul(act_two, low(mixer_input.reshape(D, 2 * D)))).reshape(length, 2, HEADS, HD)
    mixer_value = low(mixer_core(projected[:, 0], projected[:, 1], state_maps, state_rates, boundary))
    stream_two = stream_one + low_back(matmul(mixer_value, low(mixer_output)))
    act_three = low(layer_norm(stream_two, norm_params[2, 0], norm_params[2, 1]))
    padded_segment = jnp.pad(segment_row, (margin, margin), constant_values=-1)
    framed = jnp.pad(act_three, ((margin, margin), (0, 0)))
    pre_conv = jnp.zeros((length, D), jnp.float32)
    for offset in range(KSIZE):
        same_mask = (padded_segment[offset:offset + length] == segment_row).astype(jnp.float32)
        pre_conv = pre_conv + conv_taps[offset] * same_mask[:, None] * framed[offset:offset + length]
    pre_conv = low_back(pre_conv)
    stream_three = stream_two + swish(pre_conv)
    act_four = low(layer_norm(stream_three, norm_params[3, 0], norm_params[3, 1]))
    stream_four = stream_three + 0.5 * half_ffn(act_four, inner_second, outer_second)
    return layer_norm(stream_four, norm_params[4, 0], norm_params[4, 1])

def forward(params, inputs, segments):
    rows_in = inputs.reshape(ROWS, LEN, D)
    one_row = jax.checkpoint(lambda row_pair: row_forward(params, row_pair[0], row_pair[1]))
    return lax.map(one_row, (rows_in, segments)).reshape(ROWS * LEN, D)

def newton_schulz(blocks):
    squared = jnp.sum(blocks * blocks)
    current = blocks / (jnp.sqrt(squared) + 1e-07)
    for iteration in range(NS_STEPS):
        partials = low(jnp.einsum('jkd,jke->jde', current, current, precision=HIGH))
        gram_sum = lax.optimization_barrier(jnp.sum(partials, axis=0))
        polynomial = COEF_B * gram_sum + COEF_C * jnp.dot(gram_sum, gram_sum, precision=HIGH)
        current = COEF_A * current + jnp.einsum('jkd,de->jke', current, polynomial, precision=HIGH)
    return current

def column_blocks(matrix):
    return jnp.transpose(matrix.reshape(matrix.shape[0], N_MP, -1), (1, 2, 0))

def column_restore(blocks):
    return jnp.transpose(blocks, (2, 0, 1)).reshape(blocks.shape[2], -1)

def row_blocks(matrix):
    return matrix.reshape(N_MP, -1, matrix.shape[1])

def row_restore(blocks):
    return blocks.reshape(-1, blocks.shape[2])

def mixer_blocks(matrix):
    divided = matrix.reshape(D, 2, N_MP, D // N_MP)
    return jnp.transpose(divided, (2, 1, 3, 0)).reshape(N_MP, -1, D)

def mixer_restore(blocks):
    divided = blocks.reshape(N_MP, 2, D // N_MP, D)
    return jnp.transpose(divided, (3, 1, 0, 2)).reshape(D, 2, D)

def reference(inputs, segments, cotangent, inner_first, outer_first, mixer_input, mixer_output, inner_second, outer_second, norm_params, conv_taps, state_maps, state_rates, inner_first_moment, outer_first_moment, mixer_input_moment, mixer_output_moment, inner_second_moment, outer_second_moment, norm_params_moment, conv_taps_moment, state_maps_moment, state_rates_moment):
    params = (inner_first, outer_first, mixer_input, mixer_output, inner_second, outer_second, norm_params, conv_taps, state_maps, state_rates)
    moments = (inner_first_moment, outer_first_moment, mixer_input_moment, mixer_output_moment, inner_second_moment, outer_second_moment, norm_params_moment, conv_taps_moment, state_maps_moment, state_rates_moment)

    def whole_layer(param_set, values):
        return forward(param_set, values, segments)
    layer_out, pullback = jax.vjp(whole_layer, params, inputs.astype(jnp.float32))
    param_grads, input_grad = pullback(cotangent.astype(jnp.float32))
    first_scale = 0.5 * math.sqrt(max(D, FF) / D)
    second_scale = 0.5 * math.sqrt(max(D, FF) / FF)
    shapers = ((column_blocks, column_restore, first_scale), (row_blocks, row_restore, second_scale), (mixer_blocks, mixer_restore, 0.5 * math.sqrt(2.0)), (row_blocks, row_restore, 0.5), (column_blocks, column_restore, first_scale), (row_blocks, row_restore, second_scale))
    results = [layer_out.astype(jnp.bfloat16), input_grad]
    for index in range(10):
        moment_new = 0.5 * moments[index] + param_grads[index]
        if index < 6:
            to_blocks, from_blocks, step_scale = shapers[index]
            updated = params[index] - step_scale * from_blocks(newton_schulz(to_blocks(moment_new)))
        else:
            small_rate = SMALL_FACTORS[index - 6] / math.sqrt(TOKENS)
            updated = params[index] - small_rate * moment_new
        results = results + [param_grads[index], moment_new, updated]
    return (results[0], results[1], results[2], results[3], results[4], results[5], results[6], results[7], results[8], results[9], results[10], results[11], results[12], results[13], results[14], results[15], results[16], results[17], results[18], results[19], results[20], results[21], results[22], results[23], results[24], results[25], results[26], results[27], results[28], results[29], results[30], results[31])
```

```python
import math

import jax
import jax.numpy as jnp
from jax import lax
from jax.experimental import pallas as pl
from jax.experimental.pallas import tpu as pltpu
from jax.sharding import PartitionSpec as P

D = 512
FF = 2048
HEADS = 8
STATE = 32
HD = 64
KSIZE = 15
MARGIN = (KSIZE - 1) // 2
NS_STEPS = 5
N_MP = 4
BF = jnp.bfloat16
F32 = jnp.float32

COEF_A = 3.4445
COEF_B = -4.775
COEF_C = 2.0315
NORM_EPS = 1e-05
SMALL_FACTORS = (0.2, 0.2, 0.2, 4.0)
VMEM_LIMIT = 48 * 1024 * 1024


def dot(left, right, dims):
    return lax.dot_general(left, right, ((dims[0], dims[1]), ((), ())), preferred_element_type=F32)


def dot_nn(left, right):
    return dot(left, right, ((1,), (0,)))


def dot_tn(left, right):
    return dot(left, right, ((0,), (0,)))


def dot_nt(left, right):
    return dot(left, right, ((1,), (1,)))


def split_low(values):
    high = values.astype(BF)
    return high, (values - high.astype(F32)).astype(BF)


def dot3(left, right, kind):
    lh, ll = left
    rh, rl = right
    return kind(lh, rh) + (kind(lh, rl) + kind(ll, rh))


def swap_core(values):
    return lax.ppermute(values, "mp", [(i, i ^ 1) for i in range(N_MP)])


def swap_y(values):
    return lax.ppermute(values, "mp", [(i, i ^ 2) for i in range(N_MP)])


def swap_dp(values, bit):
    count = lax.axis_size("dp")
    return lax.ppermute(values, "dp", [(i, i ^ bit) for i in range(count)])


def dp_bits():
    count = lax.axis_size("dp")
    bits = []
    bit = 1
    while bit < count:
        bits.append(bit)
        bit *= 2
    return bits


def add_low(left, right):
    return (left.astype(F32) + right.astype(F32)).astype(BF)


def dp_sum(block):
    me = lax.axis_index("dp")
    bits = dp_bits()
    for bit in bits:
        half = block.shape[0] // 2
        upper = (me & bit) != 0
        low, high = block[:half], block[half:]
        got = swap_dp(jnp.where(upper, low, high), bit)
        block = add_low(jnp.where(upper, high, low), got)
    for bit in reversed(bits):
        upper = (me & bit) != 0
        got = swap_dp(block, bit)
        block = jnp.concatenate(
            [jnp.where(upper, got, block), jnp.where(upper, block, got)], axis=0
        )
    return block


def all_sum(values):
    values = values + swap_core(values)
    values = values + swap_y(values)
    for bit in dp_bits():
        values = values + swap_dp(values, bit)
    return values


def layer_norm(values, gain_row, bias_row):
    middle = jnp.mean(values, axis=-1, keepdims=True)
    centred = values - middle
    spread = jnp.mean(centred * centred, axis=-1, keepdims=True)
    return centred * lax.rsqrt(spread + NORM_EPS) * gain_row + bias_row


def swish(values):
    return values * jax.nn.sigmoid(values)


def swish_slope(values):
    sigmoid_value = jax.nn.sigmoid(values)
    return sigmoid_value * (1.0 + values * (1.0 - sigmoid_value))


def scan_kernel(backward, values_ref, reach_ref, rate_ref, out_ref):
    frames = values_ref.shape[0]
    rate = rate_ref[...]
    states = values_ref[...]
    reach = jnp.concatenate([reach_ref[...]] * (values_ref.shape[1] // 128), axis=1)
    step = 1
    while step < frames:
        moved = pltpu.roll(states, frames - step if backward else step, 0)
        factor = jnp.exp(-float(step) * rate)
        states = states + jnp.where(reach >= step, moved * factor, 0.0)
        step *= 2
    out_ref[...] = states


def local_scan(values, reach, rate, backward):
    spec = pl.BlockSpec(memory_space=pltpu.VMEM)
    return pl.pallas_call(
        lambda *refs: scan_kernel(backward, *refs),
        out_shape=jax.ShapeDtypeStruct(values.shape, F32),
        in_specs=[spec] * 3,
        out_specs=spec,
        compiler_params=pltpu.CompilerParams(vmem_limit_bytes=VMEM_LIMIT),
        cost_estimate=pl.CostEstimate(flops=30 * values.size, bytes_accessed=8 * values.size, transcendentals=0),
    )(values, reach, rate)


def polynomial_kernel(gram_ref, out_ref, a_ref):
    rows = lax.broadcasted_iota(jnp.int32, (D, D), 0)
    columns = lax.broadcasted_iota(jnp.int32, (D, D), 1)
    eye = jnp.where(rows == columns, 1.0, 0.0).astype(F32)
    gram = gram_ref[...]
    total = jnp.sum(gram * eye)
    inverse = 1.0 / (jnp.sqrt(jnp.full((1, 1), total, F32)) + 1e-07)
    a_ref[...] = gram * (inverse * inverse)
    out_ref[...] = eye * inverse

    def polynomial():
        a = a_ref[...]
        pair = split_low(a)
        return COEF_A * eye + COEF_B * a + COEF_C * dot3(pair, pair, dot_nn), pair

    def step(index, carry):
        poly, pair = polynomial()
        poly_pair = split_low(poly)
        out_ref[...] = dot3(split_low(out_ref[...]), poly_pair, dot_nn)
        half = split_low(dot3(pair, poly_pair, dot_nn))
        a_ref[...] = dot3(poly_pair, half, dot_nn)
        return carry

    lax.fori_loop(0, NS_STEPS - 1, step, 0)
    poly, _ = polynomial()
    out_ref[...] = dot3(split_low(out_ref[...]), split_low(poly), dot_nn)


def newton_factor(gram):
    spec = pl.BlockSpec(memory_space=pltpu.VMEM)
    return pl.pallas_call(
        polynomial_kernel,
        out_shape=jax.ShapeDtypeStruct((D, D), F32),
        in_specs=[spec],
        out_specs=spec,
        scratch_shapes=[pltpu.VMEM((D, D), F32)],
        compiler_params=pltpu.CompilerParams(vmem_limit_bytes=VMEM_LIMIT),
        cost_estimate=pl.CostEstimate(flops=108 * D * D * D, bytes_accessed=8 * D * D, transcendentals=0),
    )(gram)


def muon_pair(rows_first, columns_second):
    core = lax.axis_index("mp") % 2
    first = split_low(rows_first)
    second = split_low(columns_second)
    gram_first = dot3(first, first, dot_tn)
    gram_second = dot3(second, second, dot_nt)
    own = jnp.where(core == 0, gram_first, gram_second)
    other = jnp.where(core == 0, gram_second, gram_first)
    own = own + swap_core(other)
    own = own + swap_y(own)
    factor = newton_factor(own)
    got = swap_core(factor)
    factor_first = split_low(jnp.where(core == 0, factor, got))
    factor_second = split_low(jnp.where(core == 0, got, factor))
    return dot3(first, factor_first, dot_nn), dot3(factor_second, second, dot_nn)


def block_diagonal(left_dim_first):
    heads, rows, columns = left_dim_first.shape
    eye = jnp.eye(heads, dtype=left_dim_first.dtype)
    return (left_dim_first[:, :, None, :] * eye[:, None, :, None]).reshape(heads * rows, heads * columns)


def diagonal_blocks(matrix, heads):
    rows, columns = matrix.shape[0] // heads, matrix.shape[1] // heads
    shaped = matrix.reshape(heads, rows, heads, columns)
    return jnp.stack([shaped[h, :, h, :] for h in range(heads)])


def gather_weights(own):
    from_y = swap_y(own)
    both = jnp.stack([own, from_y])
    return jnp.concatenate([both, swap_core(both)], axis=0)


def core_sum(keep, send):
    return add_low(keep, swap_core(send))


def ffn_forward(act, up, down):
    pre = dot_nn(act, up)
    gated = swish(pre).astype(BF)
    return pre, gated, dot_nn(gated, down)


def ffn_backward(grad_stream, act, pre, gated, up, down):
    back = (0.5 * grad_stream).astype(BF)
    grad_gated = dot_nt(back, down)
    grad_down = dot_tn(gated, back).astype(BF)
    grad_pre = (grad_gated * swish_slope(pre)).astype(BF)
    grad_up = dot_tn(act, grad_pre).astype(BF)
    return dot_nt(grad_pre, up), grad_up, grad_down


def reduce_ffn(grad_up, grad_down):
    half = FF // 2
    quarter = FF // N_MP
    down = core_sum(grad_down[:half], grad_down[half:])
    up = core_sum(grad_up[:, :half], grad_up[:, half:])
    own = jnp.concatenate([up[:, :quarter], down[:quarter]], axis=0)
    away = jnp.concatenate([up[:, quarter:], down[quarter:]], axis=0)
    own = dp_sum(add_low(own, swap_y(away)))
    return own[:D].astype(F32), own[D:].astype(F32)


def edges(block, width):
    low = lax.ppermute(block[block.shape[0] - width :], "mp", [(i, i + 1) for i in range(N_MP - 1)])
    high = lax.ppermute(block[:width], "mp", [(i + 1, i) for i in range(N_MP - 1)])
    return jnp.concatenate([low, block, high], axis=0)


def body(
    inputs,
    segments,
    cotangent,
    inner_first,
    outer_first,
    mixer_input,
    mixer_output,
    inner_second,
    outer_second,
    norm_params,
    conv_taps,
    state_maps,
    state_rates,
    inner_first_moment,
    outer_first_moment,
    mixer_input_moment,
    mixer_output_moment,
    inner_second_moment,
    outer_second_moment,
    norm_params_moment,
    conv_taps_moment,
    state_maps_moment,
    state_rates_moment,
):
    frames = inputs.shape[0]
    me = lax.axis_index("mp")
    own_heads = HEADS // N_MP
    own_states = own_heads * STATE
    own_width = own_heads * HD
    quarter = FF // N_MP

    up_one = gather_weights(inner_first.astype(BF))
    down_one = gather_weights(outer_first.astype(BF))
    wide = 2 * own_width
    in_own = mixer_input.astype(BF).reshape(D, wide)
    out_own = mixer_output.astype(BF)
    out_own = jnp.concatenate([out_own[:, :wide], out_own[:, wide:]], axis=0)
    maps_own = state_maps.astype(BF).reshape(-1, wide)
    rate_one = state_rates.astype(BF)
    rate_rest = state_rates - rate_one.astype(F32)
    rate_two = rate_rest.astype(BF)
    rate_three = (rate_rest - rate_two.astype(F32)).astype(BF)
    rate_rows = jnp.stack([r.reshape(-1) for r in (rate_one, rate_two, rate_three)])
    rate_rows = jnp.pad(rate_rows, ((0, 13), (0, wide - own_states)))
    mixer_pack = jnp.concatenate([in_own, out_own, maps_own, rate_rows], axis=0)
    mixer_all = gather_weights(mixer_pack)
    up_two = gather_weights(inner_second.astype(BF))
    down_two = gather_weights(outer_second.astype(BF))
    up_one, up_two = (jnp.concatenate([w[k] for k in range(N_MP)], axis=1) for w in (up_one, up_two))
    down_one, down_two = (w.reshape(FF, D) for w in (down_one, down_two))
    out_rows = 2 * out_own.shape[0] // 2
    maps_rows = maps_own.shape[0]
    in_all = mixer_all[:, :D]
    out_half = out_rows // 2
    out_all = jnp.concatenate(
        [mixer_all[:, D : D + out_half], mixer_all[:, D + out_half : D + out_rows]], axis=2
    ).reshape(D, D)
    maps_all = mixer_all[:, D + out_rows : D + out_rows + maps_rows].reshape(HEADS, 2, STATE, HD)
    rate_parts = mixer_all[:, D + out_rows + maps_rows : D + out_rows + maps_rows + 3, :own_states].astype(F32)
    rates_all = (rate_parts[:, 0] + rate_parts[:, 1] + rate_parts[:, 2]).reshape(1, HEADS * STATE)
    in_signal = jnp.concatenate([in_all[k][:, :own_width] for k in range(N_MP)], axis=1)
    in_gate = jnp.concatenate([in_all[k][:, own_width:] for k in range(N_MP)], axis=1)
    in_both = jnp.concatenate([in_signal, in_gate], axis=1)
    maps_in = block_diagonal(jnp.transpose(maps_all[:, 0], (0, 2, 1)))
    maps_out = block_diagonal(maps_all[:, 1])
    rate = jnp.exp(rates_all)
    decays = jnp.exp(-rate)
    state_gain = jnp.sqrt(1.0 - decays * decays)

    row = segments.reshape(-1)
    start = me * frames
    here = lax.dynamic_slice_in_dim(row, start, frames, 0)
    before = jnp.sum((row[None, :] < here[:, None]).astype(jnp.int32), axis=1)
    until = jnp.sum((row[None, :] <= here[:, None]).astype(jnp.int32), axis=1)
    local = jnp.arange(frames, dtype=jnp.int32)
    past = local + start - before
    future = until - 1 - local - start
    past_reach = jnp.broadcast_to(jnp.minimum(past, local)[:, None], (frames, 128))
    future_reach = jnp.broadcast_to(jnp.minimum(future, frames - 1 - local)[:, None], (frames, 128))
    from_before = jnp.where(past > local, local + 1, 0).astype(F32)[:, None]
    from_after = jnp.where(future > frames - 1 - local, frames - local, 0).astype(F32)[:, None]
    firsts = jnp.stack([row[k * frames] for k in range(N_MP)])
    lasts = jnp.stack([row[(k + 1) * frames - 1] for k in range(N_MP)])
    joined = [jnp.bool_(False)] + [row[k * frames - 1] == row[k * frames] for k in range(1, N_MP)]
    whole_past = [joined[k] & (firsts[k] == lasts[k]) for k in range(N_MP)]
    taps_open = []
    for offset in range(KSIZE):
        shift = offset - MARGIN
        taps_open.append((past >= -shift if shift < 0 else future >= shift).astype(F32)[:, None])

    def to_absolute(vector):
        blocks = vector.reshape(N_MP, own_states)
        y, core = me // 2, me % 2
        order = [0, 2, 1, 3]
        blocks = jnp.stack([blocks[order[k]] for k in range(N_MP)])
        blocks = jnp.where(core == 1, jnp.stack([blocks[k ^ 1] for k in range(N_MP)]), blocks)
        return jnp.where(y == 1, jnp.stack([blocks[k ^ 2] for k in range(N_MP)]), blocks)

    def from_absolute(blocks):
        y, core = me // 2, me % 2
        blocks = jnp.where(y == 1, jnp.stack([blocks[k ^ 2] for k in range(N_MP)]), blocks)
        blocks = jnp.where(core == 1, jnp.stack([blocks[k ^ 1] for k in range(N_MP)]), blocks)
        order = [0, 2, 1, 3]
        return jnp.stack([blocks[order[k]] for k in range(N_MP)]).reshape(1, -1)

    across = jnp.exp(-float(frames) * to_absolute(rate))

    stream_zero = inputs.astype(F32)
    act_one, pull_one = jax.vjp(layer_norm, stream_zero, norm_params[0, 0], norm_params[0, 1])
    act_one = act_one.astype(BF)
    pre_one, gated_one, out_one = ffn_forward(act_one, up_one, down_one)
    stream_one = stream_zero + 0.5 * out_one

    act_two, pull_two = jax.vjp(layer_norm, stream_one, norm_params[1, 0], norm_params[1, 1])
    act_two = act_two.astype(BF)
    projected = dot_nn(act_two, in_both)
    signal, gate = projected[:, :D].astype(BF), projected[:, D:]
    driven = dot_nn(signal, maps_in) * state_gain
    states = local_scan(driven, past_reach, rate, False)
    finals = lax.all_gather(to_absolute(states[frames - 1 :]), "mp", axis=0, tiled=False)
    carry = jnp.zeros((N_MP, own_states), F32)
    carries = []
    for k in range(N_MP):
        carries.append(carry)
        carry = finals[k] + jnp.where(whole_past[k], across, 0.0) * carry
    carry_in = from_absolute(lax.dynamic_index_in_dim(jnp.stack(carries), me, 0, keepdims=False))
    states = states + jnp.where(from_before > 0.0, jnp.exp(-rate * from_before) * carry_in, 0.0)
    states_low = states.astype(BF)
    result = dot_nn(states_low, maps_out)
    gate_value = swish(gate)
    mixed = (result * gate_value).astype(BF)
    stream_two = stream_one + dot_nn(mixed, out_all)

    act_three, pull_three = jax.vjp(layer_norm, stream_two, norm_params[2, 0], norm_params[2, 1])
    framed = edges(act_three.astype(BF), MARGIN).astype(F32)
    pre_conv = jnp.zeros((frames, D), F32)
    for offset in range(KSIZE):
        pre_conv = pre_conv + conv_taps[offset] * taps_open[offset] * framed[offset : offset + frames]
    stream_three = stream_two + swish(pre_conv)

    act_four, pull_four = jax.vjp(layer_norm, stream_three, norm_params[3, 0], norm_params[3, 1])
    act_four = act_four.astype(BF)
    pre_four, gated_four, out_four = ffn_forward(act_four, up_two, down_two)
    stream_four = stream_three + 0.5 * out_four
    normed_out, pull_five = jax.vjp(layer_norm, stream_four, norm_params[4, 0], norm_params[4, 1])
    layer_output = normed_out.astype(BF)

    grad_four, gain_five, bias_five = pull_five(cotangent.astype(F32))
    grad_act_four, up_two_grad, down_two_grad = ffn_backward(
        grad_four, act_four, pre_four, gated_four, up_two, down_two
    )
    grad_part, gain_four, bias_four = pull_four(grad_act_four)
    grad_three = grad_four + grad_part
    grad_conv = (grad_three * swish_slope(pre_conv)).astype(BF)
    framed_grad = edges(grad_conv, MARGIN).astype(F32)
    grad_conv_wide = grad_conv.astype(F32)
    grad_act_three = jnp.zeros((frames, D), F32)
    taps_rows = []
    for offset in range(KSIZE):
        grad_act_three = (
            grad_act_three
            + conv_taps[KSIZE - 1 - offset] * taps_open[offset] * framed_grad[offset : offset + frames]
        )
        taps_rows.append(jnp.sum(grad_conv_wide * taps_open[offset] * framed[offset : offset + frames], axis=0))
    taps_grad = jnp.stack(taps_rows)
    grad_part, gain_three, bias_three = pull_three(grad_act_three)
    grad_two = grad_three + grad_part
    back_two = grad_two.astype(BF)
    grad_mixed = dot_nt(back_two, out_all)
    out_grad = dot_tn(mixed, back_two)
    grad_result = (grad_mixed * gate_value).astype(BF)
    grad_gate = grad_mixed * result * swish_slope(gate)
    maps_out_grad = dot_tn(states_low, grad_result)
    grad_states = dot_nt(grad_result, maps_out)
    adjoint = local_scan(grad_states, future_reach, rate, True)
    firsts_in = lax.all_gather(to_absolute(adjoint[:1]), "mp", axis=0, tiled=False)
    carry = jnp.zeros((N_MP, own_states), F32)
    carries = [carry] * N_MP
    for k in reversed(range(N_MP)):
        carry = jnp.where(joined[k + 1], carry, 0.0) if k + 1 < N_MP else carry
        carries[k] = carry
        carry = firsts_in[k] + jnp.where(firsts[k] == lasts[k], across, 0.0) * carry
    carry_back = from_absolute(lax.dynamic_index_in_dim(jnp.stack(carries), me, 0, keepdims=False))
    adjoint = adjoint + jnp.where(from_after > 0.0, jnp.exp(-rate * from_after) * carry_back, 0.0)
    earlier = jnp.concatenate([carry_in, states[:-1]], axis=0)
    decay_grad = jnp.sum(jnp.where((past >= 1)[:, None], earlier, 0.0) * adjoint, axis=0)
    gain_grad = jnp.sum(adjoint * driven, axis=0) / state_gain[0]
    decay_grad = decay_grad - gain_grad * decays[0] / state_gain[0]
    rates_grad = decay_grad * decays[0] * -rate[0]
    adjoint_low = (adjoint * state_gain).astype(BF)
    grad_signal = dot_nt(adjoint_low, maps_in)
    maps_in_grad = dot_tn(adjoint_low, signal)
    maps_grad = jnp.stack([diagonal_blocks(maps_in_grad, HEADS), diagonal_blocks(maps_out_grad, HEADS)], axis=1)
    grad_projected = jnp.concatenate([grad_signal, grad_gate], axis=1).astype(BF)
    in_grad = dot_tn(act_two, grad_projected)
    grad_act_two = dot_nt(grad_projected, in_both)
    grad_part, gain_two, bias_two = pull_two(grad_act_two)
    grad_one = grad_two + grad_part
    grad_act_one, up_one_grad, down_one_grad = ffn_backward(
        grad_one, act_one, pre_one, gated_one, up_one, down_one
    )
    grad_part, gain_one, bias_one = pull_one(grad_act_one)
    input_grad = grad_one + grad_part

    up_two_sum, down_two_sum = reduce_ffn(up_two_grad, down_two_grad)
    pack_parts = []
    for k in range(N_MP):
        columns = slice(k * own_width, (k + 1) * own_width)
        shifted = slice(D + k * own_width, D + (k + 1) * own_width)
        out_block = out_grad[columns]
        pack_parts.append(
            jnp.concatenate(
                [
                    jnp.concatenate([in_grad[:, columns], in_grad[:, shifted]], axis=1),
                    out_block[:, :wide],
                    out_block[:, wide:],
                    maps_grad[k * own_heads : (k + 1) * own_heads].reshape(-1, wide),
                    jnp.pad(
                        rates_grad[None, k * own_states : (k + 1) * own_states],
                        ((0, 95), (0, wide - own_states)),
                    ),
                ],
                axis=0,
            ).astype(BF)
        )
    kept = core_sum(jnp.stack(pack_parts[:2]), jnp.stack(pack_parts[2:]))
    mixer_sum = dp_sum(add_low(kept[0], swap_y(kept[1]))).astype(F32)
    in_sum = mixer_sum[:D]
    out_sum = jnp.concatenate([mixer_sum[D : D + out_half], mixer_sum[D + out_half : D + out_rows]], axis=1)
    maps_sum = mixer_sum[D + out_rows : D + out_rows + maps_rows].reshape(state_maps.shape)
    rates_sum = mixer_sum[D + out_rows + maps_rows, :own_states].reshape(state_rates.shape)
    up_one_sum, down_one_sum = reduce_ffn(up_one_grad, down_one_grad)
    small = jnp.concatenate(
        [
            jnp.stack(
                [
                    gain_one,
                    bias_one,
                    gain_two,
                    bias_two,
                    gain_three,
                    bias_three,
                    gain_four,
                    bias_four,
                    gain_five,
                    bias_five,
                ]
            ),
            taps_grad,
            jnp.zeros((7, D), F32),
        ]
    )
    small = all_sum(small)
    norm_sum = small[:10].reshape(norm_params.shape)
    taps_sum = small[10 : 10 + KSIZE]

    matrices = [inner_first, outer_first, mixer_input, mixer_output, inner_second, outer_second]
    matrix_moments = [
        inner_first_moment,
        outer_first_moment,
        mixer_input_moment,
        mixer_output_moment,
        inner_second_moment,
        outer_second_moment,
    ]
    matrix_grads = [up_one_sum, down_one_sum, in_sum.reshape(mixer_input.shape), out_sum, up_two_sum, down_two_sum]
    moments_new = [0.5 * moment + gradient for moment, gradient in zip(matrix_moments, matrix_grads)]
    x_down_two, x_up_two = muon_pair(moments_new[5], moments_new[4])
    x_out, x_in = muon_pair(moments_new[3], moments_new[2].reshape(D, wide))
    x_down_one, x_up_one = muon_pair(moments_new[1], moments_new[0])
    restored = [x_up_one, x_down_one, x_in.reshape(mixer_input.shape), x_out, x_up_two, x_down_two]
    first_scale = 0.5 * math.sqrt(max(D, FF) / D)
    second_scale = 0.5 * math.sqrt(max(D, FF) / FF)
    step_scales = [first_scale, second_scale, 0.5 * math.sqrt(2.0), 0.5, first_scale, second_scale]
    matrices_new = [
        matrix - step_scale * change for matrix, step_scale, change in zip(matrices, step_scales, restored)
    ]
    tokens_all = frames * lax.axis_size("dp") * lax.axis_size("mp")
    small_rates = [factor / math.sqrt(tokens_all) for factor in SMALL_FACTORS]
    small_params = [norm_params, conv_taps, state_maps, state_rates]
    small_moments = [norm_params_moment, conv_taps_moment, state_maps_moment, state_rates_moment]
    small_grads = [norm_sum, taps_sum, maps_sum, rates_sum]
    small_moments_new = [0.5 * moment + gradient for moment, gradient in zip(small_moments, small_grads)]
    small_new = [
        current_value - rate_value * moment
        for current_value, rate_value, moment in zip(small_params, small_rates, small_moments_new)
    ]
    results = [layer_output, input_grad]
    for grads, moments, params in (
        (matrix_grads, moments_new, matrices_new),
        (small_grads, small_moments_new, small_new),
    ):
        for triple in zip(grads, moments, params):
            results.extend(triple)
    return tuple(results)


def solution(mesh):
    in_specs = (
        P(("dp", "mp"), None),
        P("dp", None),
        P(("dp", "mp"), None),
        P(None, "mp"),
        P("mp", None),
        P(None, None, "mp"),
        P("mp", None),
        P(None, "mp"),
        P("mp", None),
        P(),
        P(),
        P("mp", None, None, None),
        P("mp", None),
        P(None, "mp"),
        P("mp", None),
        P(None, None, "mp"),
        P("mp", None),
        P(None, "mp"),
        P("mp", None),
        P(),
        P(),
        P("mp", None, None, None),
        P("mp", None),
    )
    out_specs = (
        P(("dp", "mp"), None),
        P(("dp", "mp"), None),
        P(None, "mp"),
        P(None, "mp"),
        P(None, "mp"),
        P("mp", None),
        P("mp", None),
        P("mp", None),
        P(None, None, "mp"),
        P(None, None, "mp"),
        P(None, None, "mp"),
        P("mp", None),
        P("mp", None),
        P("mp", None),
        P(None, "mp"),
        P(None, "mp"),
        P(None, "mp"),
        P("mp", None),
        P("mp", None),
        P("mp", None),
        P(),
        P(),
        P(),
        P(),
        P(),
        P(),
        P("mp", None, None, None),
        P("mp", None, None, None),
        P("mp", None, None, None),
        P("mp", None),
        P("mp", None),
        P("mp", None),
    )
    return jax.shard_map(body, mesh=mesh, in_specs=in_specs, out_specs=out_specs, check_vma=False)
```

```python
import math

import jax
import jax.numpy as jnp
from jax import lax
from jax.experimental import pallas as pl
from jax.experimental.pallas import tpu as pltpu
from jax.sharding import PartitionSpec as P

D = 512
FF = 2048
HEADS = 8
STATE = 32
HD = 64
KSIZE = 15
MARGIN = (KSIZE - 1) // 2
NS_STEPS = 5
N_MP = 4
BF = jnp.bfloat16
F32 = jnp.float32

COEF_A = 3.4445
COEF_B = -4.775
COEF_C = 2.0315
NORM_EPS = 1e-05
SMALL_FACTORS = (0.2, 0.2, 0.2, 4.0)
VMEM_LIMIT = 24 * 1024 * 1024
ROW_CHUNK = 320
CONV_CHUNK = 64
MAPS_AT = D + 256
RATES_AT = MAPS_AT + STATE
SEGS = 6
FLOPS_PER_US = 1.0e9


def dot(left, right, dims):
    return lax.dot_general(left, right, ((dims[0], dims[1]), ((), ())), preferred_element_type=F32)


def dot_nn(left, right):
    return dot(left, right, ((1,), (0,)))


def dot_tn(left, right):
    return dot(left, right, ((0,), (0,)))


def dot_nt(left, right):
    return dot(left, right, ((1,), (1,)))


def split_low(values):
    high = values.astype(BF)
    return high, (values - high.astype(F32)).astype(BF)


def dot3(left, right, kind):
    lh, ll = left
    rh, rl = right
    return kind(lh, rh) + (kind(lh, rl) + kind(ll, rh))


def swap_core(values):
    return lax.ppermute(values, "mp", [(i, i ^ 1) for i in range(N_MP)])


def swap_y(values):
    return lax.ppermute(values, "mp", [(i, i ^ 2) for i in range(N_MP)])


def swap_dp(values, bit):
    count = lax.axis_size("dp")
    return lax.ppermute(values, "dp", [(i, i ^ bit) for i in range(count)])


def dp_bits():
    count = lax.axis_size("dp")
    bits = []
    bit = 1
    while bit < count:
        bits.append(bit)
        bit *= 2
    return bits


def add_low(left, right):
    return (left.astype(F32) + right.astype(F32)).astype(BF)


def all_sum(values):
    values = values + swap_core(values)
    values = values + swap_y(values)
    for bit in dp_bits():
        values = values + swap_dp(values, bit)
    return values


def swish_parts(values):
    gate = 0.5 * jnp.tanh(0.5 * values) + 0.5
    active = values * gate
    return active, gate + active * (1.0 - gate)


def normed(values):
    middle = jnp.mean(values, axis=-1, keepdims=True)
    centred = values - middle
    spread = jnp.mean(centred * centred, axis=-1, keepdims=True)
    scale = lax.rsqrt(spread + NORM_EPS)
    return centred * scale, scale


def norm_forward(values, norm_ref, index):
    unit, _ = normed(values)
    return unit * norm_ref[2 * index : 2 * index + 1, :] + norm_ref[2 * index + 1 : 2 * index + 2, :]


def fold(values):
    return jnp.sum(values.reshape(values.shape[0] // 8, 8, values.shape[1]), axis=0)


def norm_backward(values, grad, norm_ref, index):
    unit, scale = normed(values)
    wide = grad * norm_ref[2 * index : 2 * index + 1, :]
    mean_one = jnp.mean(wide, axis=-1, keepdims=True)
    mean_two = jnp.mean(wide * unit, axis=-1, keepdims=True)
    return scale * (wide - mean_one - unit * mean_two), fold(grad * unit), fold(grad)


def for_rows(total, size, fn):
    def step(index, carry):
        fn(pl.ds(pl.multiple_of(index * size, size), size))
        return carry

    lax.fori_loop(0, total // size, step, 0)


def lanes(column, width):
    return jnp.concatenate([column] * (width // 128), axis=1)


def after(value, *others):
    return lax.optimization_barrier((value, *others))[0]


def call(kernel, outs, args, scratch=(), smem=(), us=1.0):
    in_specs = [pl.BlockSpec(memory_space=pltpu.SMEM if i in smem else pltpu.VMEM) for i in range(len(args))]
    return pl.pallas_call(
        kernel,
        out_shape=tuple(jax.ShapeDtypeStruct(shape, dtype) for shape, dtype in outs),
        in_specs=in_specs,
        out_specs=tuple(pl.BlockSpec(memory_space=pltpu.VMEM) for _ in outs),
        scratch_shapes=list(scratch),
        compiler_params=pltpu.CompilerParams(vmem_limit_bytes=VMEM_LIMIT),
        cost_estimate=pl.CostEstimate(flops=int(us * FLOPS_PER_US), bytes_accessed=1 << 16, transcendentals=0),
    )(*args)


def block_place(block, me):
    mask = block ^ me
    return (mask & 1) * 2 + (mask >> 1)


def first_kernel(x_ref, norm_ref, u0, d0, u1, d1, u2, d2, u3, d3, act_ref, gated_ref, slope_ref, stream_ref):
    def chunk(rows):
        x = x_ref[rows, :].astype(F32)
        act = norm_forward(x, norm_ref, 0).astype(BF)
        act_ref[rows, :] = act
        total = jnp.zeros(x.shape, F32)
        for k, (up, down) in enumerate(((u0, d0), (u1, d1), (u2, d2), (u3, d3))):
            active, slope = swish_parts(dot_nn(act, up[...]))
            active = active.astype(BF)
            gated_ref[rows, k * D : (k + 1) * D] = active
            slope_ref[rows, k * D : (k + 1) * D] = slope.astype(BF)
            total = total + dot_nn(active, down[...])
        stream_ref[rows, :] = x + 0.5 * total

    for_rows(x_ref.shape[0], ROW_CHUNK, chunk)


def fill_maps(me, wm_ref, map_ref, side):
    map_ref[...] = jnp.zeros(map_ref.shape, BF)
    lane = lax.broadcasted_iota(jnp.int32, (STATE, 128), 1)
    for block in range(N_MP):
        tile = wm_ref[block_place(block, me), MAPS_AT : MAPS_AT + STATE, side * 128 : (side + 1) * 128]
        for j in range(2):
            head = 2 * block + j
            keep = jnp.where((lane >= HD) == (j == 1), tile.astype(F32), 0.0)
            map_ref[head * STATE : (head + 1) * STATE, block * 128 : (block + 1) * 128] = keep.astype(BF)


def rates_of(me, wm_ref):
    lane = lax.broadcasted_iota(jnp.int32, (1, HEADS * STATE), 1)
    own_states = HEADS // N_MP * STATE
    total = jnp.zeros((1, HEADS * STATE), F32)
    for block in range(N_MP):
        parts = wm_ref[block_place(block, me), RATES_AT : RATES_AT + 16, :].astype(F32)
        here = (lane >= block * own_states) & (lane < (block + 1) * own_states)
        total = jnp.where(here, parts[0:1] + parts[1:2] + parts[2:3], total)
    rate = jnp.exp(total)
    decays = jnp.exp(-rate)
    return rate, decays, jnp.sqrt(1.0 - decays * decays)


def no_start(bounds_ref, low, high):
    free = jnp.ones((1, 1), F32)
    for v in range(SEGS - 1):
        bound = bounds_ref[v : v + 1, :1]
        free = jnp.where((bound >= low) & (bound <= high), 0.0, free)
    return free


def place_kernel(info_ref, frames, segments_ref, past_ref, future_ref, bounds_ref):
    row = segments_ref[...]
    length = row.shape[1]
    frame = lax.broadcasted_iota(jnp.int32, past_ref.shape, 0)
    real = frame < frames
    frame = frame + info_ref[0] * frames
    begin = jnp.zeros(past_ref.shape, jnp.int32)
    end = jnp.full(past_ref.shape, length, jnp.int32)
    bounds_ref[...] = jnp.zeros(bounds_ref.shape, jnp.int32)
    for v in range(1, SEGS):
        bound = jnp.sum((row < v).astype(F32), axis=1, keepdims=True).astype(jnp.int32)
        bounds_ref[v - 1 : v, :] = jnp.broadcast_to(bound, (1, 128))
        begin = jnp.where(bound <= frame, jnp.maximum(begin, bound), begin)
        end = jnp.where(bound > frame, jnp.minimum(end, bound), end)
    past_ref[...] = jnp.where(real, frame - begin, -1)
    future_ref[...] = jnp.where(real, end - 1 - frame, -1)


def scan_steps(states_ref, reach, rate, backward):
    frames = states_ref.shape[0]
    wide = lanes(reach, states_ref.shape[1])
    states = states_ref[...]
    step = 1
    while step < frames:
        moved = pltpu.roll(states, frames - step if backward else step, 0)
        factor = jnp.exp(-float(step) * rate)
        states = states + jnp.where(wide >= step, moved * factor, 0.0)
        step *= 2
    states_ref[...] = states


def mixer_in_kernel(
    frames, info_ref, stream_ref, norm_ref, wm_ref, past_ref,
    act_ref, signal_ref, gate_ref, driven_ref, states_ref, final_ref, map_ref,
):
    me = info_ref[0]
    rate, _, gain = rates_of(me, wm_ref)
    fill_maps(me, wm_ref, map_ref, 0)

    def chunk(rows):
        act = norm_forward(stream_ref[rows, :], norm_ref, 1).astype(BF)
        act_ref[rows, :] = act
        for block in range(N_MP):
            both = dot_nn(act, wm_ref[block_place(block, me), :D, :])
            signal_ref[rows, block * 128 : (block + 1) * 128] = both[:, :128].astype(BF)
            gate_ref[rows, block * 128 : (block + 1) * 128] = both[:, 128:]
        driven = dot_nt(signal_ref[rows, :], map_ref[...]) * gain
        driven_ref[rows, :] = driven
        states_ref[rows, :] = driven

    for_rows(stream_ref.shape[0], ROW_CHUNK, chunk)
    local = lax.broadcasted_iota(jnp.int32, past_ref.shape, 0)
    scan_steps(states_ref, jnp.minimum(past_ref[...], local), rate, False)
    final_ref[...] = states_ref[frames - 8 : frames, :]


def fill_out(me, wm_ref, out_ref):
    for block in range(N_MP):
        for half in range(2):
            out_ref[block * 128 : (block + 1) * 128, half * 256 : (half + 1) * 256] = wm_ref[
                block_place(block, me), D + half * 128 : D + (half + 1) * 128, :
            ]


def mixer_out_kernel(
    frames, info_ref, states_in_ref, finals_ref, past_ref, bounds_ref, wm_ref, gate_ref, stream_ref, norm_ref,
    states_ref, carry_ref, result_ref, mixed_ref, stream_two_ref, act_ref, low_ref, high_ref, map_ref, out_ref,
):
    me = info_ref[0]
    fill_maps(me, wm_ref, map_ref, 1)
    fill_out(me, wm_ref, out_ref)
    rate, _, _ = rates_of(me, wm_ref)
    across = jnp.exp(-float(frames) * rate)
    carry = jnp.zeros(rate.shape, F32)
    mine = carry
    for k in range(N_MP):
        mine = jnp.where(me == k, carry, mine)
        whole = no_start(bounds_ref, k * frames, (k + 1) * frames - 1)
        carry = finals_ref[8 * k + 7 : 8 * k + 8, :] + whole * across * carry
    carry_ref[...] = jnp.broadcast_to(mine, carry_ref.shape)

    def chunk(rows):
        past = past_ref[rows, :]
        local = lax.broadcasted_iota(jnp.int32, past.shape, 0) + rows.start
        reach = lanes(jnp.where(past > local, local + 1, 0).astype(F32), rate.shape[1])
        states = states_in_ref[rows, :] + jnp.where(reach > 0.0, jnp.exp(-rate * reach) * mine, 0.0)
        states_ref[rows, :] = states
        result = dot_nn(states.astype(BF), map_ref[...])
        result_ref[rows, :] = result
        mixed = (result * swish_parts(gate_ref[rows, :])[0]).astype(BF)
        mixed_ref[rows, :] = mixed
        stream = stream_ref[rows, :] + dot_nn(mixed, out_ref[...])
        stream_two_ref[rows, :] = stream
        act_ref[rows, :] = norm_forward(stream, norm_ref, 2).astype(BF).astype(F32)

    for_rows(stream_ref.shape[0], ROW_CHUNK, chunk)
    low_ref[...] = act_ref[:16, :].astype(BF)
    high_ref[...] = act_ref[frames - 16 : frames, :].astype(BF)


def fill_frame(frames, frame_ref, own_ref, before_ref, after_ref):
    frame_ref[:8, :] = before_ref[8:, :].astype(F32)
    frame_ref[8 : 8 + frames, :] = own_ref[:frames, :]
    frame_ref[8 + frames : 24 + frames, :] = after_ref[...].astype(F32)


def open_taps(past, future, offset):
    shift = offset - MARGIN
    return past >= -shift if shift < 0 else future >= shift


def conv_rows(frame_ref, taps_ref, past_ref, future_ref, start, flip):
    rows = pl.ds(start, CONV_CHUNK)
    past, future = past_ref[rows, :], future_ref[rows, :]
    total = jnp.zeros((CONV_CHUNK, D), F32)
    block = frame_ref[pl.ds(start, CONV_CHUNK + 16), :]
    for offset in range(KSIZE):
        tap = KSIZE - 1 - offset if flip else offset
        here = block[offset + 1 : offset + 1 + CONV_CHUNK, :]
        term = here * taps_ref[tap : tap + 1, :]
        if offset != MARGIN:
            term = jnp.where(lanes(open_taps(past, future, offset), D), term, 0.0)
        total = total + term
    if flip:
        total = jnp.where(lanes(past >= 0, D), total, 0.0)
    return total


def second_kernel(
    frames, act_three_ref, before_ref, after_ref, past_ref, future_ref, taps_ref, stream_two_ref, norm_ref,
    u0, d0, u1, d1, u2, d2, u3, d3, cot_ref,
    output_ref, act_ref, gated_ref, grad_pre_ref, back_ref, grad_three_ref, grad_conv_ref, low_ref, high_ref, norm_grad_ref,
    frame_ref, pre_ref, slope_ref, out_ref,
):
    fill_frame(frames, frame_ref, act_three_ref, before_ref, after_ref)
    norm_grad_ref[...] = jnp.zeros(norm_grad_ref.shape, F32)
    weights = ((u0, d0), (u1, d1), (u2, d2), (u3, d3))

    def conv(index, carry):
        start = pl.multiple_of(index * CONV_CHUNK, CONV_CHUNK)
        pre_ref[pl.ds(start, CONV_CHUNK), :] = conv_rows(frame_ref, taps_ref, past_ref, future_ref, start, False)
        return carry

    lax.fori_loop(0, pre_ref.shape[0] // CONV_CHUNK, conv, 0)

    def chunk(rows):
        active, conv_slope = swish_parts(pre_ref[rows, :])
        stream_three = stream_two_ref[rows, :] + active
        act = norm_forward(stream_three, norm_ref, 3).astype(BF)
        act_ref[rows, :] = act
        total = jnp.zeros(active.shape, F32)
        for k, (up, down) in enumerate(weights):
            hidden, slope = swish_parts(dot_nn(act, up[...]))
            hidden = hidden.astype(BF)
            gated_ref[rows, k * D : (k + 1) * D] = hidden
            slope_ref[rows, k * D : (k + 1) * D] = slope.astype(BF)
            total = total + dot_nn(hidden, down[...])
        stream_four = stream_three + 0.5 * total
        out_ref[rows, :] = norm_forward(stream_four, norm_ref, 4).astype(BF)
        grad_four, gain, bias = norm_backward(stream_four, cot_ref[rows, :].astype(F32), norm_ref, 4)
        norm_grad_ref[16:24, :] += gain
        norm_grad_ref[24:32, :] += bias
        back = (0.5 * grad_four).astype(BF)
        back_ref[rows, :] = back
        grad_act = jnp.zeros(active.shape, F32)
        for k, (up, down) in enumerate(weights):
            grad_gated = dot_nt(back, down[...])
            grad_pre = (grad_gated * slope_ref[rows, k * D : (k + 1) * D].astype(F32)).astype(BF)
            grad_pre_ref[rows, k * D : (k + 1) * D] = grad_pre
            grad_act = grad_act + dot_nt(grad_pre, up[...])
        grad_part, gain, bias = norm_backward(stream_three, grad_act, norm_ref, 3)
        norm_grad_ref[:8, :] += gain
        norm_grad_ref[8:16, :] += bias
        grad_three = grad_four + grad_part
        grad_three_ref[rows, :] = grad_three
        grad_conv_ref[rows, :] = (grad_three * conv_slope).astype(BF).astype(F32)

    for_rows(pre_ref.shape[0], ROW_CHUNK, chunk)
    output_ref[...] = out_ref[:frames, :]
    low_ref[...] = grad_conv_ref[:16, :].astype(BF)
    high_ref[...] = grad_conv_ref[frames - 16 : frames, :].astype(BF)


def weight_grad_kernel(first, act_ref, gated_ref, grad_pre_ref, back_ref, *out_refs):
    for k, g in enumerate(out_refs):
        columns = slice((first + k) * D, (first + k + 1) * D)
        g[:D, :] = dot_tn(act_ref[...], grad_pre_ref[:, columns]).astype(BF)
        g[D:, :] = dot_tn(gated_ref[:, columns], back_ref[...]).astype(BF)


def weight_grads(first, act, gated, grad_pre, back):
    return call(
        lambda *refs: weight_grad_kernel(first, *refs), [((2 * D, D), BF)] * 2, (act, gated, grad_pre, back), us=4.0
    )


def conv_back_kernel(
    frames, info_ref, act_three_ref, act_before_ref, act_after_ref, grad_conv_ref, before_ref, after_ref,
    past_ref, future_ref, taps_ref, grad_three_ref, stream_two_ref, norm_ref, wm_ref, gate_ref, result_ref,
    grad_two_ref, back_ref, grad_result_ref, grad_gate_ref, adjoint_ref, first_ref, taps_grad_ref, norm_grad_ref,
    act_frame_ref, frame_ref, grad_act_ref, map_ref, out_ref,
):
    me = info_ref[0]
    fill_frame(frames, act_frame_ref, act_three_ref, act_before_ref, act_after_ref)
    fill_frame(frames, frame_ref, grad_conv_ref, before_ref, after_ref)
    fill_maps(me, wm_ref, map_ref, 1)
    fill_out(me, wm_ref, out_ref)
    taps_grad_ref[...] = jnp.zeros(taps_grad_ref.shape, F32)
    norm_grad_ref[...] = jnp.zeros(norm_grad_ref.shape, F32)

    def conv(index, carry):
        start = pl.multiple_of(index * CONV_CHUNK, CONV_CHUNK)
        rows = pl.ds(start, CONV_CHUNK)
        grad_act_ref[rows, :] = conv_rows(frame_ref, taps_ref, past_ref, future_ref, start, True)
        past, future = past_ref[rows, :], future_ref[rows, :]
        block = act_frame_ref[pl.ds(start, CONV_CHUNK + 16), :]
        grad = grad_conv_ref[rows, :]
        for offset in range(KSIZE):
            term = grad * block[offset + 1 : offset + 1 + CONV_CHUNK, :]
            if offset != MARGIN:
                term = jnp.where(lanes(open_taps(past, future, offset), D), term, 0.0)
            taps_grad_ref[8 * offset : 8 * offset + 8, :] += fold(term)
        return carry

    lax.fori_loop(0, grad_act_ref.shape[0] // CONV_CHUNK, conv, 0)

    def chunk(rows):
        grad_part, gain, bias = norm_backward(stream_two_ref[rows, :], grad_act_ref[rows, :], norm_ref, 2)
        norm_grad_ref[:8, :] += gain
        norm_grad_ref[8:16, :] += bias
        grad_two = grad_three_ref[rows, :] + grad_part
        grad_two_ref[rows, :] = grad_two
        back = grad_two.astype(BF)
        back_ref[rows, :] = back
        grad_mixed = dot_nt(back, out_ref[...])
        active, slope = swish_parts(gate_ref[rows, :])
        grad_result = (grad_mixed * active).astype(BF)
        grad_result_ref[rows, :] = grad_result
        grad_gate_ref[rows, :] = (grad_mixed * result_ref[rows, :] * slope).astype(BF)
        adjoint_ref[rows, :] = dot_nt(grad_result, map_ref[...])

    for_rows(grad_act_ref.shape[0], ROW_CHUNK, chunk)
    local = lax.broadcasted_iota(jnp.int32, future_ref.shape, 0)
    reach = jnp.where(local < frames, jnp.minimum(future_ref[...], frames - 1 - local), 0)
    scan_steps(adjoint_ref, reach, rates_of(me, wm_ref)[0], True)
    first_ref[...] = adjoint_ref[:8, :]


def mixer_back_kernel(
    frames, info_ref, adjoint_in_ref, firsts_ref, past_ref, future_ref, bounds_ref, states_ref, carry_ref,
    driven_ref, wm_ref, signal_ref, grad_gate_ref, act_ref, stream_ref, norm_ref, grad_two_ref,
    mixed_ref, back_ref, grad_result_ref,
    grad_one_ref, pack_ref, rates_ref, norm_grad_ref, low_ref, map_ref, grad_signal_ref,
):
    me = info_ref[0]
    rate, decays, gain = rates_of(me, wm_ref)
    fill_maps(me, wm_ref, map_ref, 0)
    norm_grad_ref[...] = jnp.zeros(norm_grad_ref.shape, F32)
    low_ref[...] = states_ref[...].astype(BF)
    out_grad = dot_tn(mixed_ref[...], back_ref[...])
    maps_out = dot_tn(low_ref[...], grad_result_ref[...])
    across = jnp.exp(-float(frames) * rate)
    carry = jnp.zeros(rate.shape, F32)
    mine = carry
    for k in reversed(range(N_MP)):
        mine = jnp.where(me == k, carry, mine)
        whole = no_start(bounds_ref, k * frames + 1, (k + 1) * frames) if k + 1 < N_MP else 0.0
        carry = firsts_ref[8 * k : 8 * k + 1, :] + whole * across * carry
    rows_all = adjoint_in_ref.shape[0]
    local = lax.broadcasted_iota(jnp.int32, future_ref.shape, 0)
    reach = jnp.where((local < frames) & (future_ref[...] > frames - 1 - local), frames - local, 0).astype(F32)
    reach = lanes(reach, rate.shape[1])
    adjoint = adjoint_in_ref[...] + jnp.where(reach > 0.0, jnp.exp(-rate * reach) * mine, 0.0)
    low_ref[...] = (adjoint * gain).astype(BF)
    earlier = pltpu.roll(states_ref[...], 1, 0)
    place = lax.broadcasted_iota(jnp.int32, earlier.shape, 0)
    earlier = jnp.where(place == 0, carry_ref[:1, :], earlier)
    open_past = lanes(past_ref[...], rate.shape[1]) >= 1
    decay_grad = jnp.sum(jnp.where(open_past, earlier * adjoint, 0.0), axis=0, keepdims=True)
    gain_grad = jnp.sum(adjoint * driven_ref[...], axis=0, keepdims=True) / gain
    decay_grad = decay_grad - gain_grad * decays / gain
    rates_ref[...] = jnp.broadcast_to(decay_grad * decays * -rate, rates_ref.shape)
    maps = dot_tn(low_ref[...], signal_ref[...])
    lane = lax.broadcasted_iota(jnp.int32, (STATE, 128), 1)
    for block in range(N_MP):
        place_k = block_place(block, me)
        columns = slice(block * 128, (block + 1) * 128)
        for half in range(2):
            pack_ref[place_k, D + half * 128 : D + (half + 1) * 128, :] = out_grad[
                columns, half * 256 : (half + 1) * 256
            ].astype(BF)
        for side, grads in enumerate((maps, maps_out)):
            one = grads[2 * block * STATE : (2 * block + 1) * STATE, columns]
            two = grads[(2 * block + 1) * STATE : (2 * block + 2) * STATE, columns]
            pack_ref[place_k, MAPS_AT : MAPS_AT + STATE, side * 128 : (side + 1) * 128] = jnp.where(lane < HD, one, two).astype(BF)
        pack_ref[place_k, RATES_AT:, :] = jnp.zeros((pack_ref.shape[1] - RATES_AT, 256), BF)

    def chunk(rows):
        grad_signal_ref[rows, :] = dot_nn(low_ref[rows, :], map_ref[...]).astype(BF)
        grad_act = jnp.zeros((ROW_CHUNK, D), F32)
        for block in range(N_MP):
            columns = slice(block * 128, (block + 1) * 128)
            both = jnp.concatenate([grad_signal_ref[rows, columns], grad_gate_ref[rows, columns]], axis=1)
            grad_act = grad_act + dot_nt(both, wm_ref[block_place(block, me), :D, :])
        grad_part, gain_sum, bias_sum = norm_backward(stream_ref[rows, :], grad_act, norm_ref, 1)
        norm_grad_ref[:8, :] += gain_sum
        norm_grad_ref[8:16, :] += bias_sum
        grad_one_ref[rows, :] = grad_two_ref[rows, :] + grad_part

    for_rows(rows_all, ROW_CHUNK, chunk)
    for block in range(N_MP):
        columns = slice(block * 128, (block + 1) * 128)
        both = jnp.concatenate([grad_signal_ref[:, columns], grad_gate_ref[:, columns]], axis=1)
        pack_ref[block_place(block, me), :D, :] = dot_tn(act_ref[...], both).astype(BF)


def first_back_kernel(grad_one_ref, slope_ref, u0, d0, u1, d1, u2, d2, u3, d3, grad_pre_ref, back_ref, grad_act_ref):
    def chunk(rows):
        back = (0.5 * grad_one_ref[rows, :]).astype(BF)
        back_ref[rows, :] = back
        grad_act = jnp.zeros((ROW_CHUNK, D), F32)
        for k, (up, down) in enumerate(((u0, d0), (u1, d1), (u2, d2), (u3, d3))):
            grad_gated = dot_nt(back, down[...])
            grad_pre = (grad_gated * slope_ref[rows, k * D : (k + 1) * D].astype(F32)).astype(BF)
            grad_pre_ref[rows, k * D : (k + 1) * D] = grad_pre
            grad_act = grad_act + dot_nt(grad_pre, up[...])
        grad_act_ref[rows, :] = grad_act

    for_rows(grad_one_ref.shape[0], ROW_CHUNK, chunk)


def input_grad_kernel(
    frames, x_ref, grad_act_ref, norm_ref, grad_one_ref, norm_one_ref, norm_two_ref, norm_high_ref, taps_ref, rates_ref,
    grad_ref, small_ref, sum_ref, norm_grad_ref,
):
    norm_grad_ref[...] = jnp.zeros(norm_grad_ref.shape, F32)

    def chunk(rows):
        grad_part, gain, bias = norm_backward(x_ref[rows, :].astype(F32), grad_act_ref[rows, :], norm_ref, 0)
        norm_grad_ref[:8, :] += gain
        norm_grad_ref[8:16, :] += bias
        sum_ref[rows, :] = grad_one_ref[rows, :] + grad_part

    for_rows(x_ref.shape[0], ROW_CHUNK, chunk)
    grad_ref[...] = sum_ref[:frames, :]
    small_ref[...] = jnp.zeros(small_ref.shape, F32)
    row = 0
    for ref in (norm_grad_ref, norm_one_ref, norm_two_ref, norm_high_ref, taps_ref):
        for part in range(ref.shape[0] // 8):
            small_ref[row : row + 1, :] = jnp.sum(ref[8 * part : 8 * part + 8, :], axis=0, keepdims=True)
            row += 1
    small_ref[row : row + 1, : HEADS * STATE] = rates_ref[:1, :]


def triangle():
    count = D // 128
    return [(i, j) for i in range(count) for j in range(i, count)]


def put_triangle(matrix, out_ref):
    for k, (i, j) in enumerate(triangle()):
        out_ref[k * 128 : (k + 1) * 128, :] = matrix[i * 128 : (i + 1) * 128, j * 128 : (j + 1) * 128]


def get_triangle(near_ref, far_ref, out_ref):
    for k, (i, j) in enumerate(triangle()):
        block = near_ref[k * 128 : (k + 1) * 128, :] + far_ref[k * 128 : (k + 1) * 128, :]
        out_ref[i * 128 : (i + 1) * 128, j * 128 : (j + 1) * 128] = block
        if i != j:
            out_ref[j * 128 : (j + 1) * 128, i * 128 : (i + 1) * 128] = block.T


def moment_kernel(
    split, info_ref, mine_ref, near_ref, across_ref, across_near_ref, first_moment_ref, second_moment_ref,
    first_grad_ref, second_grad_ref, first_new_ref, second_new_ref, own_ref, other_ref, *more_refs,
):
    block_ref = more_refs[-1]
    part = mine_ref.shape[0]
    x, z = info_ref[2], info_ref[3]
    for ref, side, half in (
        (mine_ref, z, x), (near_ref, 1 - z, x), (across_ref, z, 1 - x), (across_near_ref, 1 - z, 1 - x)
    ):
        block_ref[pl.ds(pl.multiple_of(side * 2 * part + half * part, part), part), :] = ref[...]
    first_grad, second_grad = split(block_ref, *more_refs[:-1])
    first_grad_ref[...] = first_grad
    second_grad_ref[...] = second_grad
    first = 0.5 * first_moment_ref[...] + first_grad
    second = 0.5 * second_moment_ref[...] + second_grad
    first_new_ref[...] = first
    second_new_ref[...] = second
    first_pair = split_low(first)
    second_pair = split_low(second)
    gram_first = dot3(first_pair, first_pair, dot_tn)
    gram_second = dot3(second_pair, second_pair, dot_nt)
    is_zero = info_ref[1] == 0

    @pl.when(is_zero)
    def _():
        put_triangle(gram_first, own_ref)
        put_triangle(gram_second, other_ref)

    @pl.when(jnp.logical_not(is_zero))
    def _():
        put_triangle(gram_second, own_ref)
        put_triangle(gram_first, other_ref)


def update_kernel(scales, info_ref, own_ref, other_ref, first_new_ref, second_new_ref, first_ref, second_ref, first_out, second_out):
    is_zero = info_ref[1] == 0
    own, other = own_ref[...], other_ref[...]
    factor_first = split_low(jnp.where(is_zero, own, other))
    factor_second = split_low(jnp.where(is_zero, other, own))
    first_out[...] = first_ref[...] - scales[0] * dot3(split_low(first_new_ref[...]), factor_first, dot_nn)
    second_out[...] = second_ref[...] - scales[1] * dot3(factor_second, split_low(second_new_ref[...]), dot_nn)


def newton_poly(a):
    pair = split_low(a)
    return split_low(COEF_B * a + COEF_C * dot3(pair, pair, dot_nn)), pair


def newton_gram(a, pair, poly):
    half = COEF_A * a + dot3(pair, poly, dot_nn)
    return COEF_A * half + dot3(poly, split_low(half), dot_nn)


def newton_start(near_ref, far_ref, a_ref, q_ref):
    get_triangle(near_ref, far_ref, a_ref)
    rows = lax.broadcasted_iota(jnp.int32, (D, D), 0)
    columns = lax.broadcasted_iota(jnp.int32, (D, D), 1)
    gram = a_ref[...]
    trace = jnp.sum(jnp.where(rows == columns, gram, 0.0))
    inverse = 1.0 / (jnp.sqrt(jnp.full((1, 1), trace, F32)) + 1e-07)
    a = gram * (inverse * inverse)
    poly, pair = newton_poly(a)
    q_ref[...] = (jnp.where(rows == columns, COEF_A, 0.0) + poly[0].astype(F32) + poly[1].astype(F32)) * inverse
    a_ref[...] = newton_gram(a, pair, poly)


def newton_step(a_ref, q_ref, last, a_out, q_out):
    a, q = a_ref[...], q_ref[...]
    poly, pair = newton_poly(a)
    if not last:
        a_out[...] = newton_gram(a, pair, poly)
    q_out[...] = COEF_A * q + dot3(split_low(q), poly, dot_nn)


def newton_kernel(near_ref, far_ref, q_ref, a_ref):
    newton_start(near_ref, far_ref, a_ref, q_ref)

    def step(index, carry):
        newton_step(a_ref, q_ref, False, a_ref, q_ref)
        return carry

    lax.fori_loop(0, NS_STEPS - 2, step, 0)
    newton_step(a_ref, q_ref, True, None, q_ref)


def newton_factor(near, far, whole):
    square = ((D, D), F32)
    if whole:
        return call(newton_kernel, [square], (near, far), scratch=[pltpu.VMEM((D, D), F32)], us=17.0)[0]
    gram, factor = call(newton_start, [square] * 2, (near, far), us=3.5)
    for _ in range(NS_STEPS - 2):
        gram, factor = call(
            lambda a, q, a_out, q_out: newton_step(a, q, False, a_out, q_out), [square] * 2, (gram, factor), us=3.7
        )
    return call(lambda a, q, q_out: newton_step(a, q, True, None, q_out), [square], (gram, factor), us=3.0)[0]


class Muon:
    def __init__(self, info, parts, split, moments, extra=()):
        self.info = info
        shapes = [(moment.shape, F32) for moment in moments]
        packed = ((len(triangle()) * 128, 128), F32)
        outs = call(
            lambda *refs: moment_kernel(split, *refs),
            shapes * 2 + [packed] * 2 + list(extra),
            (info, *parts, *moments),
            scratch=[pltpu.VMEM((4 * parts[0].shape[0], parts[0].shape[1]), BF)],
            smem=(0,),
            us=4.5,
        )
        self.grads, self.news, own, other = outs[:2], outs[2:4], outs[4], outs[5]
        self.extra = outs[6:]
        self.own, self.got = own, swap_core(other)
        self.moment_out = own

    def exchange(self, *others):
        self.near = self.own + after(self.got, *others)
        self.far = swap_y(self.near)
        return self.near

    def factor(self, whole, *others):
        self.q = newton_factor(self.near, after(self.far, *others), whole)
        self.other_q = swap_core(self.q)
        return self.q

    def update(self, scales, params, *others):
        news = call(
            lambda *refs: update_kernel(scales, *refs),
            [(param.shape, F32) for param in params],
            (self.info, self.q, after(self.other_q, *others), *self.news, *params),
            smem=(0,),
            us=4.5,
        )
        return [list(triple) for triple in zip(self.grads, self.news, news)]


def bit_rows(info_ref, index, half, other=False):
    bit = info_ref[2 + index]
    return pl.ds(pl.multiple_of((1 - bit if other else bit) * half, half), half)


def add_refs(one, two):
    return (one.astype(F32) + two.astype(F32)).astype(BF)


def sum_start_kernel(info_ref, own_ref, got_own_ref, away_ref, got_away_ref, own_a, away_a, keep_b, send_b):
    half = own_a.shape[0]
    own_a[...] = add_refs(own_ref[:half, :], got_own_ref[:half, :])
    away_a[...] = add_refs(away_ref[:half, :], got_away_ref[:half, :])
    quarter = half // 2
    for out, other in ((keep_b, False), (send_b, True)):
        rows = bit_rows(info_ref, 0, quarter, other)
        rows = pl.ds(pl.multiple_of(half + rows.start, quarter), quarter)
        out[:quarter, :] = add_refs(own_ref[rows, :], got_own_ref[rows, :])
        out[quarter:, :] = add_refs(away_ref[rows, :], got_away_ref[rows, :])


def sum_second_kernel(info_ref, own_a, got_a, keep_b, got_b, keep_a, send_a, own_b, away_b):
    quarter = keep_a.shape[0]
    for out, other in ((keep_a, False), (send_a, True)):
        rows = bit_rows(info_ref, 0, quarter, other)
        out[...] = add_refs(own_a[rows, :], got_a[rows, :])
    own_b[...] = add_refs(keep_b[:quarter, :], got_b[:quarter, :])
    away_b[...] = add_refs(keep_b[quarter:, :], got_b[quarter:, :])


def sum_third_kernel(info_ref, keep_a, got_a, own_b, got_b, keep, send):
    first = info_ref[3] == 0
    a = add_refs(keep_a[...], got_a[...])
    b = add_refs(own_b[...], got_b[...])

    @pl.when(first)
    def _():
        keep[...] = a
        send[...] = b

    @pl.when(jnp.logical_not(first))
    def _():
        keep[...] = b
        send[...] = a


def sum_more_kernel(index, info_ref, keep_in, got, keep, send):
    half = keep.shape[0]
    for out, other in ((keep, False), (send, True)):
        rows = bit_rows(info_ref, index, half, other)
        out[...] = add_refs(keep_in[rows, :], got[rows, :])


def sum_join_kernel(index, info_ref, own, got, out):
    half = own.shape[0]
    out[bit_rows(info_ref, index, half), :] = own[...]
    out[bit_rows(info_ref, index, half, True), :] = got[...]


class Sum:
    def __init__(self, info, own, got_own, away, got_away):
        self.info = info
        self.inputs = (own, got_own, away, got_away)
        self.rows, self.width = own.shape
        self.bits = dp_bits()

    def run(self, kernel, rows, args):
        return call(kernel, [((count, self.width), BF) for count in rows], (self.info, *args), smem=(0,), us=0.8)

    def start(self):
        half = self.rows // 2
        self.own_a, away_a, self.keep_b, send_b = self.run(sum_start_kernel, [half] * 4, self.inputs)
        self.got = (swap_y(away_a), swap_dp(send_b, self.bits[0]))
        return (away_a,)

    def second(self, *others):
        quarter = self.rows // 4
        got_a, got_b = (after(value, *others) for value in self.got)
        self.keep_a, send_a, self.own_b, away_b = self.run(
            sum_second_kernel, [quarter] * 4, (self.own_a, got_a, self.keep_b, got_b)
        )
        self.got = (swap_dp(send_a, self.bits[0]), swap_y(away_b))
        return (send_a,)

    def third(self, *others):
        quarter = self.rows // 4
        got_a, got_b = (after(value, *others) for value in self.got)
        self.keep, send = self.run(sum_third_kernel, [quarter] * 2, (self.keep_a, got_a, self.own_b, got_b))
        self.got = swap_dp(send, self.bits[1])
        self.count = quarter
        self.index = 2
        return (send,)

    def more(self, *others):
        got = after(self.got, *others)
        if self.index < len(self.bits):
            self.count //= 2
            index = self.index
            self.keep, send = self.run(
                lambda *refs: sum_more_kernel(index, *refs), [self.count] * 2, (self.keep, got)
            )
            self.got = swap_dp(send, self.bits[index])
            self.index += 1
            return (send,)
        self.block = add_low(self.keep, got)
        self.gather_start()
        return (self.block,)

    def gather_start(self):
        self.index -= 1
        if self.index >= 2:
            self.got = swap_dp(self.block, self.bits[self.index])
        else:
            self.near = swap_dp(self.block, self.bits[1])
            self.across = swap_dp(self.block, self.bits[0])

    def gather(self, *others):
        got = after(self.got, *others)
        index = self.index
        self.count *= 2
        (self.block,) = self.run(lambda *refs: sum_join_kernel(index, *refs), [self.count], (self.block, got))
        self.gather_start()
        return (self.block,)

    def finish(self, *others):
        near = after(self.near, *others)
        self.parts = (self.block, near, self.across, swap_dp(near, self.bits[0]))
        return (near,)


def halo(low, high):
    before = lax.ppermute(high, "mp", [(i, i + 1) for i in range(N_MP - 1)])
    after = lax.ppermute(low, "mp", [(i + 1, i) for i in range(N_MP - 1)])
    return before, after


def body(
    inputs,
    segments,
    cotangent,
    inner_first,
    outer_first,
    mixer_input,
    mixer_output,
    inner_second,
    outer_second,
    norm_params,
    conv_taps,
    state_maps,
    state_rates,
    inner_first_moment,
    outer_first_moment,
    mixer_input_moment,
    mixer_output_moment,
    inner_second_moment,
    outer_second_moment,
    norm_params_moment,
    conv_taps_moment,
    state_maps_moment,
    state_rates_moment,
):
    frames = inputs.shape[0]
    padded = -(-frames // ROW_CHUNK) * ROW_CHUNK
    more = padded - frames
    me = lax.axis_index("mp")
    own_states = HEADS // N_MP * STATE
    n_states = HEADS * STATE
    wide = 256
    bits = dp_bits()
    dp = lax.axis_index("dp")
    info = jnp.stack([me, me % 2] + [(dp // bit) % 2 for bit in bits])
    x_upper = dp % 2 == 1
    unit = 16 * lax.axis_size("dp")
    pack_rows = -(-(RATES_AT + 16) // unit) * unit

    own_one = [inner_first.astype(BF), outer_first.astype(BF)]
    y_halves = [
        swap_y(jnp.where(x_upper, value[D // 2 :], value[: D // 2])) for value in own_one
    ]
    core_one = [swap_core(value) for value in own_one]
    own_two = [inner_second.astype(BF), outer_second.astype(BF)]
    maps_tile = jnp.transpose(state_maps, (2, 1, 0, 3)).reshape(STATE, wide)
    rates_row = jnp.tile(state_rates.reshape(1, own_states), (1, N_MP))
    rates_one = rates_row.astype(BF)
    rates_rest = rates_row - rates_one.astype(F32)
    rates_two = rates_rest.astype(BF)
    rates_three = (rates_rest - rates_two.astype(F32)).astype(BF)
    rates_tile = jnp.pad(
        jnp.concatenate([rates_one, rates_two, rates_three], axis=0), ((0, pack_rows - RATES_AT - 3), (0, 0))
    )
    own_mixer = jnp.concatenate(
        [
            mixer_input.reshape(D, wide).astype(BF),
            mixer_output[:, :wide].astype(BF),
            mixer_output[:, wide:].astype(BF),
            maps_tile.astype(BF),
            rates_tile,
        ],
        axis=0,
    )
    norm_rows = norm_params.reshape(10, D)
    x = jnp.pad(inputs, ((0, more), (0, 0)))
    cot = jnp.pad(cotangent, ((0, more), (0, 0)))
    taps = jnp.pad(conv_taps, ((0, 1), (0, 0)))
    past, future, bounds = call(
        lambda info_ref, *refs: place_kernel(info_ref, frames, *refs),
        [((padded, 128), jnp.int32), ((padded, 128), jnp.int32), ((8, 128), jnp.int32)],
        (info, segments),
        smem=(0,),
    )
    y_halves[0] = after(y_halves[0], own_mixer, *own_two, norm_rows, x, past)
    y_one = []
    for half in y_halves:
        across = swap_dp(half, 1)
        y_one.append(
            jnp.concatenate([jnp.where(x_upper, across, half), jnp.where(x_upper, half, across)], axis=0)
        )
    both_one = [swap_core(value) for value in y_one]
    one_refs = []
    for group in (own_one, y_one, core_one, both_one):
        one_refs.extend(group)
    own_mixer = after(own_mixer, y_halves[1])
    half = pack_rows // 2
    mixer_half = swap_y(jnp.where(x_upper, own_mixer[half:], own_mixer[:half]))
    core_mixer = swap_core(own_mixer)
    send_half = after(jnp.where(x_upper, own_two[1], own_two[0]), mixer_half)
    two_half = swap_y(send_half)
    core_two = [swap_core(after(value, mixer_half)) for value in own_two]
    mixer_across = swap_dp(mixer_half, 1)

    frame_shape = (padded, D)
    hidden_shape = (padded, FF)
    state_shape = (padded, n_states)
    edge = ((16, D), BF)
    frame_scratch = pltpu.VMEM((padded + 32, D), F32)
    map_scratch = pltpu.VMEM((n_states, D), BF)
    out_scratch = pltpu.VMEM((D, D), BF)

    act_one, gated_one, slope_one, stream_one = call(
        first_kernel,
        [(frame_shape, BF), (hidden_shape, BF), (hidden_shape, BF), (frame_shape, F32)],
        (after(x, send_half), norm_rows, *one_refs),
        us=6.6,
    )
    mixer_across = after(mixer_across, stream_one)
    y_mixer = jnp.concatenate(
        [jnp.where(x_upper, mixer_across, mixer_half), jnp.where(x_upper, mixer_half, mixer_across)], axis=0
    )
    wm = jnp.stack([own_mixer, y_mixer, core_mixer, swap_core(y_mixer)])
    two_half = after(two_half, stream_one, y_mixer)
    two_across = swap_dp(two_half, 1)
    act_two, signal, gate, driven, states_local, final = call(
        lambda *refs: mixer_in_kernel(frames, *refs),
        [(frame_shape, BF), (frame_shape, BF), (frame_shape, F32), (state_shape, F32), (state_shape, F32), ((8, n_states), F32)],
        (info, after(stream_one, two_half), norm_rows, wm, past),
        scratch=[map_scratch],
        smem=(0,),
        us=4.2,
    )
    finals = lax.all_gather(final, "mp", axis=0, tiled=True)
    states, carry_in, result, mixed, stream_two, act_three, low, high = call(
        lambda *refs: mixer_out_kernel(frames, *refs),
        [(state_shape, F32), ((8, n_states), F32), (frame_shape, F32), (frame_shape, BF), (frame_shape, F32), (frame_shape, F32), edge, edge],
        (info, states_local, finals, past, bounds, wm, gate, stream_one, norm_rows),
        scratch=[map_scratch, out_scratch],
        smem=(0,),
        us=2.1,
    )
    act_before, act_after = halo(low, high)
    two_across = after(two_across, stream_two)
    y_two = [jnp.where(x_upper, two_across, two_half), jnp.where(x_upper, two_half, two_across)]
    both_two = [swap_core(value) for value in y_two]
    two_refs = []
    for group in (own_two, y_two, core_two, both_two):
        two_refs.extend(group)
    layer_output, act_four, gated_four, grad_pre_four, back_four, grad_three, grad_conv, low, high, norm_high = call(
        lambda *refs: second_kernel(frames, *refs),
        [
            ((frames, D), BF), (frame_shape, BF), (hidden_shape, BF), (hidden_shape, BF), (frame_shape, BF),
            (frame_shape, F32), (frame_shape, F32), edge, edge, ((32, D), F32),
        ],
        (act_three, act_before, act_after, past, future, taps, stream_two, norm_rows, *two_refs, cot),
        scratch=[frame_scratch, pltpu.VMEM(frame_shape, F32), pltpu.VMEM(hidden_shape, BF), pltpu.VMEM(frame_shape, BF)],
        us=16.6,
    )
    grad_before, grad_after = halo(low, high)
    send_two = weight_grads(2, act_four, gated_four, grad_pre_four, back_four)
    keep_two = weight_grads(0, act_four, gated_four, grad_pre_four, back_four)
    got_two = [swap_core(value) for value in send_two]

    grad_two, back_two, grad_result, grad_gate, adjoint, first, taps_part, norm_two = call(
        lambda *refs: conv_back_kernel(frames, *refs),
        [
            (frame_shape, F32), (frame_shape, BF), (frame_shape, BF), (frame_shape, BF), (state_shape, F32),
            ((8, n_states), F32), ((8 * KSIZE, D), F32), ((16, D), F32),
        ],
        (
            info, act_three, act_before, act_after, grad_conv, grad_before, grad_after, past, future, taps,
            after(grad_three, *keep_two, *send_two), stream_two, norm_rows, wm, gate, result,
        ),
        scratch=[frame_scratch, frame_scratch, pltpu.VMEM(frame_shape, F32), map_scratch, out_scratch],
        smem=(0,),
        us=11.8,
    )
    firsts = lax.all_gather(first, "mp", axis=0, tiled=True)
    sum_two = Sum(info, keep_two[0], after(got_two[0], firsts), keep_two[1], got_two[1])
    started = sum_two.start()
    grad_one, mixer_pack, rates_part, norm_one = call(
        lambda *refs: mixer_back_kernel(frames, *refs),
        [(frame_shape, F32), ((N_MP, pack_rows, wide), BF), ((8, n_states), F32), ((16, D), F32)],
        (
            info, adjoint, firsts, past, future, bounds, states, carry_in, driven, wm, signal, grad_gate,
            act_two, stream_one, norm_rows, after(grad_two, *started), mixed, back_two, grad_result,
        ),
        scratch=[pltpu.VMEM(state_shape, BF), map_scratch, pltpu.VMEM(frame_shape, BF)],
        smem=(0,),
        us=5.5,
    )
    got_mixer = [swap_core(mixer_pack[k]) for k in (2, 3)]
    grad_pre_one, back_one, grad_act_one = call(
        first_back_kernel,
        [(hidden_shape, BF), (frame_shape, BF), (frame_shape, F32)],
        (grad_one, slope_one, *one_refs),
        us=5.4,
    )
    started = sum_two.second(back_one)
    send_one = weight_grads(2, act_one, gated_one, grad_pre_one, after(back_one, *started))
    got_one = [swap_core(value) for value in send_one]
    sum_mixer = Sum(info, mixer_pack[0], after(got_mixer[0], *send_one), mixer_pack[1], got_mixer[1])
    started = sum_mixer.start()
    keep_one = weight_grads(0, act_one, gated_one, grad_pre_one, after(back_one, *started))
    started = sum_two.third(*keep_one)
    sum_one = Sum(info, keep_one[0], after(got_one[0], *started), keep_one[1], got_one[1])
    started = sum_one.start()
    input_grad, small = call(
        lambda *refs: input_grad_kernel(frames, *refs),
        [((frames, D), F32), ((32, D), F32)],
        (x, after(grad_act_one, *started), norm_rows, grad_one, norm_one, norm_two, norm_high, taps_part, rates_part),
        scratch=[pltpu.VMEM(frame_shape, F32), pltpu.VMEM((16, D), F32)],
        us=2.4,
    )
    extra_bits = len(bits) - 2
    started = sum_mixer.second(input_grad)
    started = sum_two.more(*started)
    started = sum_one.second(*started)
    started = sum_mixer.third(*started)
    started = sum_two.more(*started) if extra_bits else started
    started = sum_one.third(*started)
    for _ in range(extra_bits - 1):
        started = sum_two.more(*started)
    for _ in range(extra_bits):
        started = sum_mixer.more(*started)
        started = sum_two.gather(*started)
        started = sum_one.more(*started)
    started = sum_two.finish(*started)
    started = sum_mixer.more(*started)
    started = sum_one.more(*started)

    first_scale = 0.5 * math.sqrt(max(D, FF) / D)
    second_scale = 0.5 * math.sqrt(max(D, FF) / FF)
    split_ffn = lambda block_ref: (block_ref[D:, :].astype(F32), block_ref[:D, :].astype(F32))
    muon_two = Muon(info, tuple(after(v, *started) for v in sum_two.parts), split_ffn, (outer_second_moment, inner_second_moment))
    for _ in range(extra_bits):
        started = sum_one.gather(*started)
        started = sum_mixer.gather(*started)
    started = sum_one.finish(muon_two.moment_out)
    near_two = muon_two.exchange(*started)
    started = sum_mixer.finish(near_two)
    muon_one = Muon(info, tuple(after(v, *started) for v in sum_one.parts), split_ffn, (outer_first_moment, inner_first_moment))

    def split_mixer(block_ref, maps_ref):
        maps_ref[...] = block_ref[MAPS_AT : MAPS_AT + STATE, :].astype(F32)
        out = jnp.concatenate([block_ref[D : D + 128, :], block_ref[D + 128 : MAPS_AT, :]], axis=1)
        return out.astype(F32), block_ref[:D, :].astype(F32)

    q_two = muon_two.factor(False, muon_one.moment_out)
    near_one = muon_one.exchange(muon_one.moment_out)
    muon_mixer = Muon(
        info, tuple(after(v, near_one) for v in sum_mixer.parts), split_mixer,
        (mixer_output_moment, mixer_input_moment.reshape(D, wide)), extra=[((STATE, wide), F32)],
    )
    near_mixer = muon_mixer.exchange(muon_mixer.moment_out)
    muon_one.factor(True)
    muon_mixer.factor(False)
    down_two, up_two = muon_two.update((second_scale, first_scale), (outer_second, inner_second))
    out_triple, in_triple = muon_mixer.update(
        (0.5, 0.5 * math.sqrt(2.0)), (mixer_output, mixer_input.reshape(D, wide))
    )
    in_triple = [value.reshape(mixer_input.shape) for value in in_triple]
    down_one, up_one = muon_one.update((second_scale, first_scale), (outer_first, inner_first))
    small = all_sum(small)

    norm_sum = small[:10].reshape(norm_params.shape)
    taps_sum = small[10 : 10 + KSIZE]
    rates_sum = lax.dynamic_slice_in_dim(small[10 + KSIZE], me * own_states, own_states, 0).reshape(state_rates.shape)
    maps_sum = muon_mixer.extra[0].reshape(STATE, 2, HEADS // N_MP, HD)
    maps_sum = jnp.transpose(maps_sum, (2, 1, 0, 3))
    tokens_all = frames * lax.axis_size("dp") * lax.axis_size("mp")
    results = [layer_output, input_grad]
    for triple in (up_one, down_one, in_triple, out_triple, up_two, down_two):
        results.extend(triple)
    for factor, grad, moment, param in (
        (SMALL_FACTORS[0], norm_sum, norm_params_moment, norm_params),
        (SMALL_FACTORS[1], taps_sum, conv_taps_moment, conv_taps),
        (SMALL_FACTORS[2], maps_sum, state_maps_moment, state_maps),
        (SMALL_FACTORS[3], rates_sum, state_rates_moment, state_rates),
    ):
        moment_new = 0.5 * moment + grad
        results.extend((grad, moment_new, param - factor / math.sqrt(tokens_all) * moment_new))
    return tuple(results)


def solution(mesh):
    in_specs = (
        P(("dp", "mp"), None),
        P("dp", None),
        P(("dp", "mp"), None),
        P(None, "mp"),
        P("mp", None),
        P(None, None, "mp"),
        P("mp", None),
        P(None, "mp"),
        P("mp", None),
        P(),
        P(),
        P("mp", None, None, None),
        P("mp", None),
        P(None, "mp"),
        P("mp", None),
        P(None, None, "mp"),
        P("mp", None),
        P(None, "mp"),
        P("mp", None),
        P(),
        P(),
        P("mp", None, None, None),
        P("mp", None),
    )
    out_specs = (
        P(("dp", "mp"), None),
        P(("dp", "mp"), None),
        P(None, "mp"),
        P(None, "mp"),
        P(None, "mp"),
        P("mp", None),
        P("mp", None),
        P("mp", None),
        P(None, None, "mp"),
        P(None, None, "mp"),
        P(None, None, "mp"),
        P("mp", None),
        P("mp", None),
        P("mp", None),
        P(None, "mp"),
        P(None, "mp"),
        P(None, "mp"),
        P("mp", None),
        P("mp", None),
        P("mp", None),
        P(),
        P(),
        P(),
        P(),
        P(),
        P(),
        P("mp", None, None, None),
        P("mp", None, None, None),
        P("mp", None, None, None),
        P("mp", None),
        P("mp", None),
        P("mp", None),
    )
    return jax.shard_map(body, mesh=mesh, in_specs=in_specs, out_specs=out_specs, check_vma=False)
```

```python
import math

import jax
import jax.numpy as jnp
from jax import lax
from jax.experimental import pallas as pl
from jax.experimental.pallas import tpu as pltpu
from jax.sharding import PartitionSpec as P

D = 512
FF = 2048
HEADS = 8
STATE = 32
HD = 64
KSIZE = 15
MARGIN = (KSIZE - 1) // 2
NS_STEPS = 5
N_MP = 4
BF = jnp.bfloat16
F32 = jnp.float32

COEF_A = 3.4445
COEF_B = -4.775
COEF_C = 2.0315
NORM_EPS = 1e-05
SMALL_FACTORS = (0.2, 0.2, 0.2, 4.0)
VMEM_LIMIT = 24 * 1024 * 1024
ROW_CHUNK = 320
CONV_CHUNK = 64
MAPS_AT = D + 256
RATES_AT = MAPS_AT + STATE
SEGS = 6
SQUARES = (1, 3, 3, 3, 3)
ORDER = "otomtoomstomstomtostmsotmsomsmmooomopmotm"
OUT_AT = 256
TILE_AT = OUT_AT + 128
FLOPS_PER_US = 1.0e9


def dot(left, right, dims):
    return lax.dot_general(left, right, ((dims[0], dims[1]), ((), ())), preferred_element_type=F32)


def dot_nn(left, right):
    return dot(left, right, ((1,), (0,)))


def dot_tn(left, right):
    return dot(left, right, ((0,), (0,)))


def dot_nt(left, right):
    return dot(left, right, ((1,), (1,)))


def split_low(values):
    high = values.astype(BF)
    return high, (values - high.astype(F32)).astype(BF)


def dot3(left, right, kind):
    lh, ll = left
    rh, rl = right
    return kind(lh, rh) + (kind(lh, rl) + kind(ll, rh))


def swap_core(values):
    return lax.ppermute(values, "mp", [(i, i ^ 1) for i in range(N_MP)])


def swap_y(values):
    return lax.ppermute(values, "mp", [(i, i ^ 2) for i in range(N_MP)])


def swap_dp(values, bit):
    count = lax.axis_size("dp")
    return lax.ppermute(values, "dp", [(i, i ^ bit) for i in range(count)])


def dp_bits():
    count = lax.axis_size("dp")
    bits = []
    bit = 1
    while bit < count:
        bits.append(bit)
        bit *= 2
    return bits


def add_low(left, right):
    return (left.astype(F32) + right.astype(F32)).astype(BF)


def swish_parts(values):
    gate = 0.5 * jnp.tanh(0.5 * values) + 0.5
    active = values * gate
    return active, gate + active * (1.0 - gate)


def normed(values):
    middle = jnp.mean(values, axis=-1, keepdims=True)
    centred = values - middle
    spread = jnp.mean(centred * centred, axis=-1, keepdims=True)
    scale = lax.rsqrt(spread + NORM_EPS)
    return centred * scale, scale


def norm_forward(values, norm_ref, index):
    unit, _ = normed(values)
    return unit * norm_ref[2 * index : 2 * index + 1, :] + norm_ref[2 * index + 1 : 2 * index + 2, :]


def fold(values):
    return jnp.sum(values.reshape(values.shape[0] // 8, 8, values.shape[1]), axis=0)


def norm_backward(values, grad, norm_ref, index):
    unit, scale = normed(values)
    wide = grad * norm_ref[2 * index : 2 * index + 1, :]
    mean_one = jnp.mean(wide, axis=-1, keepdims=True)
    mean_two = jnp.mean(wide * unit, axis=-1, keepdims=True)
    return scale * (wide - mean_one - unit * mean_two), fold(grad * unit), fold(grad)


def for_rows(total, size, fn):
    def step(index, carry):
        fn(pl.ds(pl.multiple_of(index * size, size), size))
        return carry

    lax.fori_loop(0, total // size, step, 0)


def lanes(column, width):
    return jnp.concatenate([column] * (width // 128), axis=1)


def after(value, *others):
    return lax.optimization_barrier((value, *others))[0]


def together(*values):
    return lax.optimization_barrier(values)


def call(kernel, outs, args, scratch=(), smem=(), us=1.0):
    in_specs = [pl.BlockSpec(memory_space=pltpu.SMEM if i in smem else pltpu.VMEM) for i in range(len(args))]
    return pl.pallas_call(
        kernel,
        out_shape=tuple(jax.ShapeDtypeStruct(shape, dtype) for shape, dtype in outs),
        in_specs=in_specs,
        out_specs=tuple(pl.BlockSpec(memory_space=pltpu.VMEM) for _ in outs),
        scratch_shapes=list(scratch),
        compiler_params=pltpu.CompilerParams(vmem_limit_bytes=VMEM_LIMIT),
        cost_estimate=pl.CostEstimate(flops=int(us * FLOPS_PER_US), bytes_accessed=1 << 16, transcendentals=0),
    )(*args)


def block_place(block, me):
    mask = block ^ me
    return (mask & 1) * 2 + (mask >> 1)


def first_kernel(x_ref, norm_ref, u0, d0, u1, d1, u2, d2, u3, d3, act_ref, gated_ref, slope_ref, stream_ref):
    def chunk(rows):
        x = x_ref[rows, :].astype(F32)
        act = norm_forward(x, norm_ref, 0).astype(BF)
        act_ref[rows, :] = act
        total = jnp.zeros(x.shape, F32)
        for k, (up, down) in enumerate(((u0, d0), (u1, d1), (u2, d2), (u3, d3))):
            active, slope = swish_parts(dot_nn(act, up[...]))
            active = active.astype(BF)
            gated_ref[rows, k * D : (k + 1) * D] = active
            slope_ref[rows, k * D : (k + 1) * D] = slope.astype(BF)
            total = total + dot_nn(active, down[...])
        stream_ref[rows, :] = x + 0.5 * total

    for_rows(x_ref.shape[0], ROW_CHUNK, chunk)


def fill_maps(me, wm_ref, map_ref, side):
    map_ref[...] = jnp.zeros(map_ref.shape, BF)
    lane = lax.broadcasted_iota(jnp.int32, (STATE, 128), 1)
    for block in range(N_MP):
        tile = wm_ref[block_place(block, me), MAPS_AT : MAPS_AT + STATE, side * 128 : (side + 1) * 128]
        for j in range(2):
            head = 2 * block + j
            keep = jnp.where((lane >= HD) == (j == 1), tile.astype(F32), 0.0)
            map_ref[head * STATE : (head + 1) * STATE, block * 128 : (block + 1) * 128] = keep.astype(BF)


def rates_of(me, wm_ref):
    lane = lax.broadcasted_iota(jnp.int32, (1, HEADS * STATE), 1)
    own_states = HEADS // N_MP * STATE
    total = jnp.zeros((1, HEADS * STATE), F32)
    for block in range(N_MP):
        parts = wm_ref[block_place(block, me), RATES_AT : RATES_AT + 16, :].astype(F32)
        here = (lane >= block * own_states) & (lane < (block + 1) * own_states)
        total = jnp.where(here, parts[0:1] + parts[1:2] + parts[2:3], total)
    rate = jnp.exp(total)
    decays = jnp.exp(-rate)
    return rate, decays, jnp.sqrt(1.0 - decays * decays)


def no_start(bounds_ref, low, high):
    free = jnp.ones((1, 1), F32)
    for v in range(SEGS - 1):
        bound = bounds_ref[v : v + 1, :1]
        free = jnp.where((bound >= low) & (bound <= high), 0.0, free)
    return free


def place_kernel(info_ref, frames, segments_ref, past_ref, future_ref, bounds_ref):
    row = segments_ref[...]
    length = row.shape[1]
    frame = lax.broadcasted_iota(jnp.int32, past_ref.shape, 0)
    real = frame < frames
    frame = frame + info_ref[0] * frames
    begin = jnp.zeros(past_ref.shape, jnp.int32)
    end = jnp.full(past_ref.shape, length, jnp.int32)
    bounds_ref[...] = jnp.zeros(bounds_ref.shape, jnp.int32)
    for v in range(1, SEGS):
        bound = jnp.sum((row < v).astype(F32), axis=1, keepdims=True).astype(jnp.int32)
        bounds_ref[v - 1 : v, :] = jnp.broadcast_to(bound, (1, 128))
        begin = jnp.where(bound <= frame, jnp.maximum(begin, bound), begin)
        end = jnp.where(bound > frame, jnp.minimum(end, bound), end)
    past_ref[...] = jnp.where(real, frame - begin, -1)
    future_ref[...] = jnp.where(real, end - 1 - frame, -1)


def scan_steps(states_ref, reach, rate, backward):
    frames = states_ref.shape[0]
    wide = lanes(reach, states_ref.shape[1])
    states = states_ref[...]
    step = 1
    while step < frames:
        moved = pltpu.roll(states, frames - step if backward else step, 0)
        factor = jnp.exp(-float(step) * rate)
        states = states + jnp.where(wide >= step, moved * factor, 0.0)
        step *= 2
    states_ref[...] = states


def mixer_in_kernel(
    frames, info_ref, stream_ref, norm_ref, wm_ref, past_ref,
    act_ref, signal_ref, gate_ref, driven_ref, states_ref, final_ref, map_ref,
):
    me = info_ref[0]
    rate, _, gain = rates_of(me, wm_ref)
    fill_maps(me, wm_ref, map_ref, 0)

    def chunk(rows):
        act = norm_forward(stream_ref[rows, :], norm_ref, 1).astype(BF)
        act_ref[rows, :] = act
        for block in range(N_MP):
            both = dot_nn(act, wm_ref[block_place(block, me), :D, :])
            signal_ref[rows, block * 128 : (block + 1) * 128] = both[:, :128].astype(BF)
            gate_ref[rows, block * 128 : (block + 1) * 128] = both[:, 128:]
        driven = dot_nt(signal_ref[rows, :], map_ref[...]) * gain
        driven_ref[rows, :] = driven
        states_ref[rows, :] = driven

    for_rows(stream_ref.shape[0], ROW_CHUNK, chunk)
    local = lax.broadcasted_iota(jnp.int32, past_ref.shape, 0)
    scan_steps(states_ref, jnp.minimum(past_ref[...], local), rate, False)
    final_ref[...] = states_ref[frames - 8 : frames, :]


def fill_out(me, wm_ref, out_ref):
    for block in range(N_MP):
        for half in range(2):
            out_ref[block * 128 : (block + 1) * 128, half * 256 : (half + 1) * 256] = wm_ref[
                block_place(block, me), D + half * 128 : D + (half + 1) * 128, :
            ]


def mixer_out_kernel(
    frames, info_ref, states_in_ref, finals_ref, past_ref, bounds_ref, wm_ref, gate_ref, stream_ref, norm_ref,
    states_ref, carry_ref, result_ref, mixed_ref, stream_two_ref, act_ref, low_ref, high_ref, map_ref, out_ref,
):
    me = info_ref[0]
    fill_maps(me, wm_ref, map_ref, 1)
    fill_out(me, wm_ref, out_ref)
    rate, _, _ = rates_of(me, wm_ref)
    across = jnp.exp(-float(frames) * rate)
    carry = jnp.zeros(rate.shape, F32)
    mine = carry
    for k in range(N_MP):
        mine = jnp.where(me == k, carry, mine)
        whole = no_start(bounds_ref, k * frames, (k + 1) * frames - 1)
        carry = finals_ref[8 * k + 7 : 8 * k + 8, :] + whole * across * carry
    carry_ref[...] = jnp.broadcast_to(mine, carry_ref.shape)

    def chunk(rows):
        past = past_ref[rows, :]
        local = lax.broadcasted_iota(jnp.int32, past.shape, 0) + rows.start
        reach = lanes(jnp.where(past > local, local + 1, 0).astype(F32), rate.shape[1])
        states = states_in_ref[rows, :] + jnp.where(reach > 0.0, jnp.exp(-rate * reach) * mine, 0.0)
        states_ref[rows, :] = states
        result = dot_nn(states.astype(BF), map_ref[...])
        result_ref[rows, :] = result
        mixed = (result * swish_parts(gate_ref[rows, :])[0]).astype(BF)
        mixed_ref[rows, :] = mixed
        stream = stream_ref[rows, :] + dot_nn(mixed, out_ref[...])
        stream_two_ref[rows, :] = stream
        act_ref[rows, :] = norm_forward(stream, norm_ref, 2).astype(BF).astype(F32)

    for_rows(stream_ref.shape[0], ROW_CHUNK, chunk)
    low_ref[...] = act_ref[:16, :].astype(BF)
    high_ref[...] = act_ref[frames - 16 : frames, :].astype(BF)


def fill_frame(frames, frame_ref, own_ref, before_ref, after_ref):
    frame_ref[:8, :] = before_ref[8:, :].astype(F32)
    frame_ref[8 : 8 + frames, :] = own_ref[:frames, :]
    frame_ref[8 + frames : 24 + frames, :] = after_ref[...].astype(F32)


def open_taps(past, future, offset):
    shift = offset - MARGIN
    return past >= -shift if shift < 0 else future >= shift


def conv_rows(frame_ref, taps_ref, past_ref, future_ref, start, flip):
    rows = pl.ds(start, CONV_CHUNK)
    past, future = past_ref[rows, :], future_ref[rows, :]
    total = jnp.zeros((CONV_CHUNK, D), F32)
    block = frame_ref[pl.ds(start, CONV_CHUNK + 16), :]
    for offset in range(KSIZE):
        tap = KSIZE - 1 - offset if flip else offset
        here = block[offset + 1 : offset + 1 + CONV_CHUNK, :]
        term = here * taps_ref[tap : tap + 1, :]
        if offset != MARGIN:
            term = jnp.where(lanes(open_taps(past, future, offset), D), term, 0.0)
        total = total + term
    if flip:
        total = jnp.where(lanes(past >= 0, D), total, 0.0)
    return total


def second_kernel(
    frames, act_three_ref, before_ref, after_ref, past_ref, future_ref, taps_ref, stream_two_ref, norm_ref,
    u0, d0, u1, d1, u2, d2, u3, d3, cot_ref,
    output_ref, act_ref, gated_ref, grad_pre_ref, back_ref, grad_three_ref, grad_conv_ref, low_ref, high_ref, norm_grad_ref,
    frame_ref, pre_ref, slope_ref, out_ref,
):
    fill_frame(frames, frame_ref, act_three_ref, before_ref, after_ref)
    norm_grad_ref[...] = jnp.zeros(norm_grad_ref.shape, F32)
    weights = ((u0, d0), (u1, d1), (u2, d2), (u3, d3))

    def conv(index, carry):
        start = pl.multiple_of(index * CONV_CHUNK, CONV_CHUNK)
        pre_ref[pl.ds(start, CONV_CHUNK), :] = conv_rows(frame_ref, taps_ref, past_ref, future_ref, start, False)
        return carry

    lax.fori_loop(0, pre_ref.shape[0] // CONV_CHUNK, conv, 0)

    def chunk(rows):
        active, conv_slope = swish_parts(pre_ref[rows, :])
        stream_three = stream_two_ref[rows, :] + active
        act = norm_forward(stream_three, norm_ref, 3).astype(BF)
        act_ref[rows, :] = act
        total = jnp.zeros(active.shape, F32)
        for k, (up, down) in enumerate(weights):
            hidden, slope = swish_parts(dot_nn(act, up[...]))
            hidden = hidden.astype(BF)
            gated_ref[rows, k * D : (k + 1) * D] = hidden
            slope_ref[rows, k * D : (k + 1) * D] = slope.astype(BF)
            total = total + dot_nn(hidden, down[...])
        stream_four = stream_three + 0.5 * total
        out_ref[rows, :] = norm_forward(stream_four, norm_ref, 4).astype(BF)
        grad_four, gain, bias = norm_backward(stream_four, cot_ref[rows, :].astype(F32), norm_ref, 4)
        norm_grad_ref[16:24, :] += gain
        norm_grad_ref[24:32, :] += bias
        back = (0.5 * grad_four).astype(BF)
        back_ref[rows, :] = back
        grad_act = jnp.zeros(active.shape, F32)
        for k, (up, down) in enumerate(weights):
            grad_gated = dot_nt(back, down[...])
            grad_pre = (grad_gated * slope_ref[rows, k * D : (k + 1) * D].astype(F32)).astype(BF)
            grad_pre_ref[rows, k * D : (k + 1) * D] = grad_pre
            grad_act = grad_act + dot_nt(grad_pre, up[...])
        grad_part, gain, bias = norm_backward(stream_three, grad_act, norm_ref, 3)
        norm_grad_ref[:8, :] += gain
        norm_grad_ref[8:16, :] += bias
        grad_three = grad_four + grad_part
        grad_three_ref[rows, :] = grad_three
        grad_conv_ref[rows, :] = (grad_three * conv_slope).astype(BF).astype(F32)

    for_rows(pre_ref.shape[0], ROW_CHUNK, chunk)
    output_ref[...] = out_ref[:frames, :]
    low_ref[...] = grad_conv_ref[:16, :].astype(BF)
    high_ref[...] = grad_conv_ref[frames - 16 : frames, :].astype(BF)


def weight_grad_kernel(first, act_ref, gated_ref, grad_pre_ref, back_ref, out_ref):
    for k in range(2):
        columns = slice((first + k) * D, (first + k + 1) * D)
        out_ref[2 * k * D : (2 * k + 1) * D, :] = dot_tn(act_ref[...], grad_pre_ref[:, columns]).astype(BF)
        out_ref[(2 * k + 1) * D : (2 * k + 2) * D, :] = dot_tn(gated_ref[:, columns], back_ref[...]).astype(BF)


def weight_grads(first, act, gated, grad_pre, back):
    return call(
        lambda *refs: weight_grad_kernel(first, *refs), [((4 * D, D), BF)], (act, gated, grad_pre, back), us=2.0
    )[0]


def conv_back_kernel(
    frames, info_ref, act_three_ref, act_before_ref, act_after_ref, grad_conv_ref, before_ref, after_ref,
    past_ref, future_ref, taps_ref, grad_three_ref, stream_two_ref, norm_ref, wm_ref, gate_ref, result_ref,
    grad_two_ref, back_ref, grad_result_ref, grad_gate_ref, adjoint_ref, first_ref, taps_grad_ref, norm_grad_ref,
    act_frame_ref, frame_ref, grad_act_ref, map_ref, out_ref,
):
    me = info_ref[0]
    fill_frame(frames, act_frame_ref, act_three_ref, act_before_ref, act_after_ref)
    fill_frame(frames, frame_ref, grad_conv_ref, before_ref, after_ref)
    fill_maps(me, wm_ref, map_ref, 1)
    fill_out(me, wm_ref, out_ref)
    taps_grad_ref[...] = jnp.zeros(taps_grad_ref.shape, F32)
    norm_grad_ref[...] = jnp.zeros(norm_grad_ref.shape, F32)

    def conv(index, carry):
        start = pl.multiple_of(index * CONV_CHUNK, CONV_CHUNK)
        rows = pl.ds(start, CONV_CHUNK)
        grad_act_ref[rows, :] = conv_rows(frame_ref, taps_ref, past_ref, future_ref, start, True)
        past, future = past_ref[rows, :], future_ref[rows, :]
        block = act_frame_ref[pl.ds(start, CONV_CHUNK + 16), :]
        grad = grad_conv_ref[rows, :]
        for offset in range(KSIZE):
            term = grad * block[offset + 1 : offset + 1 + CONV_CHUNK, :]
            if offset != MARGIN:
                term = jnp.where(lanes(open_taps(past, future, offset), D), term, 0.0)
            taps_grad_ref[8 * offset : 8 * offset + 8, :] += fold(term)
        return carry

    lax.fori_loop(0, grad_act_ref.shape[0] // CONV_CHUNK, conv, 0)

    def chunk(rows):
        grad_part, gain, bias = norm_backward(stream_two_ref[rows, :], grad_act_ref[rows, :], norm_ref, 2)
        norm_grad_ref[:8, :] += gain
        norm_grad_ref[8:16, :] += bias
        grad_two = grad_three_ref[rows, :] + grad_part
        grad_two_ref[rows, :] = grad_two
        back = grad_two.astype(BF)
        back_ref[rows, :] = back
        grad_mixed = dot_nt(back, out_ref[...])
        active, slope = swish_parts(gate_ref[rows, :])
        grad_result = (grad_mixed * active).astype(BF)
        grad_result_ref[rows, :] = grad_result
        grad_gate_ref[rows, :] = (grad_mixed * result_ref[rows, :] * slope).astype(BF)
        adjoint_ref[rows, :] = dot_nt(grad_result, map_ref[...])

    for_rows(grad_act_ref.shape[0], ROW_CHUNK, chunk)
    local = lax.broadcasted_iota(jnp.int32, future_ref.shape, 0)
    reach = jnp.where(local < frames, jnp.minimum(future_ref[...], frames - 1 - local), 0)
    scan_steps(adjoint_ref, reach, rates_of(me, wm_ref)[0], True)
    first_ref[...] = adjoint_ref[:8, :]


def mixer_back_kernel(
    frames, info_ref, adjoint_in_ref, firsts_ref, past_ref, future_ref, bounds_ref, states_ref, carry_ref,
    driven_ref, wm_ref, signal_ref, grad_gate_ref, act_ref, stream_ref, norm_ref, grad_two_ref,
    mixed_ref, back_ref, grad_result_ref,
    grad_one_ref, keep_ref, send_ref, rates_ref, norm_grad_ref, low_ref, map_ref, grad_signal_ref, pack_ref,
):
    me = info_ref[0]
    rate, decays, gain = rates_of(me, wm_ref)
    fill_maps(me, wm_ref, map_ref, 0)
    norm_grad_ref[...] = jnp.zeros(norm_grad_ref.shape, F32)
    low_ref[...] = states_ref[...].astype(BF)
    out_grad = dot_tn(mixed_ref[...], back_ref[...])
    maps_out = dot_tn(low_ref[...], grad_result_ref[...])
    across = jnp.exp(-float(frames) * rate)
    carry = jnp.zeros(rate.shape, F32)
    mine = carry
    for k in reversed(range(N_MP)):
        mine = jnp.where(me == k, carry, mine)
        whole = no_start(bounds_ref, k * frames + 1, (k + 1) * frames) if k + 1 < N_MP else 0.0
        carry = firsts_ref[8 * k : 8 * k + 1, :] + whole * across * carry
    rows_all = adjoint_in_ref.shape[0]
    local = lax.broadcasted_iota(jnp.int32, future_ref.shape, 0)
    reach = jnp.where((local < frames) & (future_ref[...] > frames - 1 - local), frames - local, 0).astype(F32)
    reach = lanes(reach, rate.shape[1])
    adjoint = adjoint_in_ref[...] + jnp.where(reach > 0.0, jnp.exp(-rate * reach) * mine, 0.0)
    low_ref[...] = (adjoint * gain).astype(BF)
    earlier = pltpu.roll(states_ref[...], 1, 0)
    place = lax.broadcasted_iota(jnp.int32, earlier.shape, 0)
    earlier = jnp.where(place == 0, carry_ref[:1, :], earlier)
    open_past = lanes(past_ref[...], rate.shape[1]) >= 1
    decay_grad = jnp.sum(jnp.where(open_past, earlier * adjoint, 0.0), axis=0, keepdims=True)
    gain_grad = jnp.sum(adjoint * driven_ref[...], axis=0, keepdims=True) / gain
    decay_grad = decay_grad - gain_grad * decays / gain
    rates_ref[...] = jnp.broadcast_to(decay_grad * decays * -rate, rates_ref.shape)
    maps = dot_tn(low_ref[...], signal_ref[...])
    lane = lax.broadcasted_iota(jnp.int32, (STATE, 128), 1)
    for block in range(N_MP):
        place_k = block_place(block, me)
        columns = slice(block * 128, (block + 1) * 128)
        pack_ref[place_k, OUT_AT:TILE_AT, :] = out_grad[columns, :].astype(BF)
        pack_ref[place_k, TILE_AT:, :] = jnp.zeros((pack_ref.shape[1] - TILE_AT, D), BF)
        for side, grads in enumerate((maps, maps_out)):
            one = grads[2 * block * STATE : (2 * block + 1) * STATE, columns]
            two = grads[(2 * block + 1) * STATE : (2 * block + 2) * STATE, columns]
            pack_ref[place_k, TILE_AT : TILE_AT + STATE, side * 128 : (side + 1) * 128] = jnp.where(lane < HD, one, two).astype(BF)

    def chunk(rows):
        grad_signal_ref[rows, :] = dot_nn(low_ref[rows, :], map_ref[...]).astype(BF)
        grad_act = jnp.zeros((ROW_CHUNK, D), F32)
        for block in range(N_MP):
            columns = slice(block * 128, (block + 1) * 128)
            both = jnp.concatenate([grad_signal_ref[rows, columns], grad_gate_ref[rows, columns]], axis=1)
            grad_act = grad_act + dot_nt(both, wm_ref[block_place(block, me), :D, :])
        grad_part, gain_sum, bias_sum = norm_backward(stream_ref[rows, :], grad_act, norm_ref, 1)
        norm_grad_ref[:8, :] += gain_sum
        norm_grad_ref[8:16, :] += bias_sum
        grad_one_ref[rows, :] = grad_two_ref[rows, :] + grad_part

    for_rows(rows_all, ROW_CHUNK, chunk)
    for block in range(N_MP):
        columns = slice(block * 128, (block + 1) * 128)
        both = jnp.concatenate([grad_signal_ref[:, columns], grad_gate_ref[:, columns]], axis=1)
        grad = dot_tn(act_ref[...], both).astype(BF)
        for half in range(2):
            pack_ref[block_place(block, me), :OUT_AT, half * 256 : (half + 1) * 256] = grad[half * 256 : (half + 1) * 256, :]
    rows = pack_ref.shape[1]
    for k in range(2):
        keep_ref[k * rows : (k + 1) * rows, :] = pack_ref[k]
        send_ref[k * rows : (k + 1) * rows, :] = pack_ref[2 + k]


def first_back_kernel(grad_one_ref, slope_ref, u0, d0, u1, d1, u2, d2, u3, d3, grad_pre_ref, back_ref, grad_act_ref):
    def chunk(rows):
        back = (0.5 * grad_one_ref[rows, :]).astype(BF)
        back_ref[rows, :] = back
        grad_act = jnp.zeros((ROW_CHUNK, D), F32)
        for k, (up, down) in enumerate(((u0, d0), (u1, d1), (u2, d2), (u3, d3))):
            grad_gated = dot_nt(back, down[...])
            grad_pre = (grad_gated * slope_ref[rows, k * D : (k + 1) * D].astype(F32)).astype(BF)
            grad_pre_ref[rows, k * D : (k + 1) * D] = grad_pre
            grad_act = grad_act + dot_nt(grad_pre, up[...])
        grad_act_ref[rows, :] = grad_act

    for_rows(grad_one_ref.shape[0], ROW_CHUNK, chunk)


def input_grad_kernel(
    frames, x_ref, grad_act_ref, norm_ref, grad_one_ref, norm_one_ref, norm_two_ref, norm_high_ref, taps_ref, rates_ref,
    grad_ref, small_ref, sum_ref, norm_grad_ref,
):
    norm_grad_ref[...] = jnp.zeros(norm_grad_ref.shape, F32)

    def chunk(rows):
        grad_part, gain, bias = norm_backward(x_ref[rows, :].astype(F32), grad_act_ref[rows, :], norm_ref, 0)
        norm_grad_ref[:8, :] += gain
        norm_grad_ref[8:16, :] += bias
        sum_ref[rows, :] = grad_one_ref[rows, :] + grad_part

    for_rows(x_ref.shape[0], ROW_CHUNK, chunk)
    grad_ref[...] = sum_ref[:frames, :]
    small_ref[...] = jnp.zeros(small_ref.shape, F32)
    row = 0
    for ref in (norm_grad_ref, norm_one_ref, norm_two_ref, norm_high_ref, taps_ref):
        for part in range(ref.shape[0] // 8):
            small_ref[row : row + 1, :] = jnp.sum(ref[8 * part : 8 * part + 8, :], axis=0, keepdims=True)
            row += 1
    small_ref[row : row + 1, : HEADS * STATE] = rates_ref[:1, :]


def triangle():
    count = D // 128
    return [(i, j) for i in range(count) for j in range(i, count)]


def put_triangle(matrix, out_ref):
    for k, (i, j) in enumerate(triangle()):
        out_ref[k * 128 : (k + 1) * 128, :] = matrix[i * 128 : (i + 1) * 128, j * 128 : (j + 1) * 128]


def get_triangle(ref, out_ref, more_ref=None):
    for k, (i, j) in enumerate(triangle()):
        block = ref[k * 128 : (k + 1) * 128, :]
        if more_ref is not None:
            block = block + more_ref[k * 128 : (k + 1) * 128, :]
        out_ref[i * 128 : (i + 1) * 128, j * 128 : (j + 1) * 128] = block
        if i != j:
            out_ref[j * 128 : (j + 1) * 128, i * 128 : (i + 1) * 128] = block.T


def fill_block(info_ref, part_refs, block_ref):
    x, z = info_ref[2], info_ref[3]
    part = part_refs[0].shape[0]
    for ref, side, half in zip(part_refs, (z, 1 - z, z, 1 - z), (x, x, 1 - x, 1 - x)):
        block_ref[pl.ds(pl.multiple_of(side * 2 * part + half * part, part), part), :] = ref[...]


def put_grams(info_ref, pair, own_ref, other_ref):
    first_pair, second_pair = split_low(pair[0]), split_low(pair[1])
    gram_first = dot3(first_pair, first_pair, dot_tn)
    gram_second = dot3(second_pair, second_pair, dot_nt)
    is_zero = info_ref[1] == 0

    @pl.when(is_zero)
    def _():
        put_triangle(gram_first, own_ref)
        put_triangle(gram_second, other_ref)

    @pl.when(jnp.logical_not(is_zero))
    def _():
        put_triangle(gram_second, own_ref)
        put_triangle(gram_first, other_ref)


def moment_kernel(kind, info_ref, *refs):
    parts, moments, block_ref = refs[:4], refs[4:6], refs[-1]
    refs = refs[6:-1]
    if kind == "m":
        left_refs, refs = refs[:2], refs[2:]
    grads, news, own_ref, other_ref = refs[:2], refs[2:4], refs[4], refs[5]
    fill_block(info_ref, parts, block_ref)
    if kind == "m":
        values = [
            block_ref[OUT_AT:TILE_AT, :],
            jnp.concatenate([block_ref[:OUT_AT, :256], block_ref[:OUT_AT, 256:]], axis=0),
        ]
        refs[6][...] = block_ref[TILE_AT : TILE_AT + STATE, :256].astype(F32)
    else:
        values = [block_ref[D:, :], block_ref[:D, :]]
    pair = []
    for value, moment, grad_ref, new_ref in zip(values, moments, grads, news):
        grad = value.astype(F32)
        grad_ref[...] = grad
        new = 0.5 * moment[...] + grad
        new_ref[...] = new
        pair.append(new)
    if kind == "o":
        put_grams(info_ref, pair, own_ref, other_ref)
        return
    mine = info_ref[2] == (0 if kind == "t" else 1)

    @pl.when(mine)
    def _():
        put_grams(info_ref, pair, own_ref, other_ref)

    @pl.when(jnp.logical_not(mine))
    def _():
        for k, ref in enumerate((own_ref, other_ref)):
            ref[...] = left_refs[k][...] if kind == "m" else jnp.zeros(ref.shape, F32)


def update_kernel(scales, kind, info_ref, *refs):
    count = 2 if kind == "o" else 4
    factors, (first_new, second_new, first_ref, second_ref, first_out, second_out, full_ref) = refs[:count], refs[count:]
    is_zero = info_ref[1] == 0
    own, other = factors[0][...], factors[1][...]
    if kind != "o":
        mine = info_ref[2] == (0 if kind == "t" else 1)
        own, other = jnp.where(mine, own, factors[2][...]), jnp.where(mine, other, factors[3][...])
    get_triangle(jnp.where(is_zero, own, other), full_ref)
    first_out[...] = first_ref[...] - scales[0] * dot3(split_low(first_new[...]), split_low(full_ref[...]), dot_nn)
    get_triangle(jnp.where(is_zero, other, own), full_ref)
    second_out[...] = second_ref[...] - scales[1] * dot3(split_low(full_ref[...]), split_low(second_new[...]), dot_nn)


def newton_poly(a, squares):
    pair = split_low(a)
    square = dot_nn(pair[0], pair[0]) if squares == 1 else dot3(pair, pair, dot_nn)
    return (COEF_B * a + COEF_C * square).astype(BF), pair


def newton_gram(a, pair, poly):
    half = COEF_A * a + (dot_nn(pair[0], poly) + dot_nn(pair[1], poly))
    high, rest = split_low(half)
    return COEF_A * half + (dot_nn(poly, high) + dot_nn(poly, rest))


def newton_start(near_ref, far_ref, a_ref, q_ref):
    get_triangle(near_ref, a_ref, far_ref)
    rows = lax.broadcasted_iota(jnp.int32, (D, D), 0)
    columns = lax.broadcasted_iota(jnp.int32, (D, D), 1)
    gram = a_ref[...]
    trace = jnp.sum(jnp.where(rows == columns, gram, 0.0))
    inverse = 1.0 / (jnp.sqrt(jnp.full((1, 1), trace, F32)) + 1e-07)
    a = gram * (inverse * inverse)
    poly, pair = newton_poly(a, SQUARES[0])
    q_ref[...] = (jnp.where(rows == columns, COEF_A, 0.0) + poly.astype(F32)) * inverse
    a_ref[...] = newton_gram(a, pair, poly)


def newton_step(index, a_ref, q_ref, a_out, q_out):
    a, q = a_ref[...], q_ref[...]
    poly, pair = newton_poly(a, SQUARES[index])
    if index < NS_STEPS - 1:
        a_out[...] = newton_gram(a, pair, poly)
    high, rest = split_low(q)
    q_out[...] = COEF_A * q + (dot_nn(high, poly) + dot_nn(rest, poly))


def newton_kernel(near_ref, far_ref, out_ref, a_ref, q_ref):
    newton_start(near_ref, far_ref, a_ref, q_ref)
    for index in range(1, NS_STEPS):
        newton_step(index, a_ref, q_ref, a_ref, q_ref)
    put_triangle(q_ref[...], out_ref)


class Muon:
    def __init__(self, info, parts, moments, kind, left=()):
        self.info, self.kind = info, kind
        shapes = [(moment.shape, F32) for moment in moments]
        packed = ((len(triangle()) * 128, 128), F32)
        extra = [((STATE, 256), F32)] if kind == "m" else []
        outs = call(
            lambda *refs: moment_kernel(kind, *refs),
            shapes * 2 + [packed] * 2 + extra,
            (info, *parts, *moments, *left),
            scratch=[pltpu.VMEM((4 * parts[0].shape[0], D), BF)],
            smem=(0,),
            us=4.5,
        )
        self.grads, self.news, self.own, self.other, self.extra = outs[:2], outs[2:4], outs[4], outs[5], outs[6:]
        if kind != "t":
            self.got = swap_core(self.other)

    def exchange(self, *others):
        self.near = self.own + after(self.got, *others)
        self.far = swap_y(self.near)
        return (self.near,)

    def newton(self, *others):
        far = after(self.far, *others)
        (self.q,) = call(
            newton_kernel,
            [(self.near.shape, F32)],
            (self.near, far),
            scratch=[pltpu.VMEM((D, D), F32)] * 2,
            us=13.0,
        )
        return self.send()

    def send(self):
        self.factors = [self.q, swap_core(self.q)]
        if self.kind == "m":
            self.factors.append(swap_dp(self.q, 1))
        return (self.q,)

    def share(self, *others):
        self.factors[1:3] = together(self.factors[1], self.factors[2], *others)[:2]
        self.factors.append(swap_core(self.factors[2]))
        return (self.factors[2],)

    def update(self, scales, params, factors, *others):
        kind = self.kind
        news = call(
            lambda *refs: update_kernel(scales, kind, *refs),
            [(param.shape, F32) for param in params],
            (self.info, *factors[:-1], after(factors[-1], *others), *self.news, *params),
            scratch=[pltpu.VMEM((D, D), F32)],
            smem=(0,),
            us=4.5,
        )
        return [list(triple) for triple in zip(self.grads, self.news, news)]


def bit_rows(info_ref, index, half, other=False):
    bit = info_ref[2 + index]
    return pl.ds(pl.multiple_of((1 - bit if other else bit) * half, half), half)


def add_refs(one, two):
    return (one.astype(F32) + two.astype(F32)).astype(BF)


def sum_start_kernel(info_ref, mine_ref, got_ref, own_a, away_a, keep_b, send_b):
    half, rows = own_a.shape[0], mine_ref.shape[0] // 2
    own_a[...] = add_refs(mine_ref[:half, :], got_ref[:half, :])
    away_a[...] = add_refs(mine_ref[rows : rows + half, :], got_ref[rows : rows + half, :])
    quarter = half // 2
    for out, other in ((keep_b, False), (send_b, True)):
        start = bit_rows(info_ref, 0, quarter, other).start
        for k in range(2):
            here = pl.ds(pl.multiple_of(k * rows + half + start, quarter), quarter)
            out[k * quarter : (k + 1) * quarter, :] = add_refs(mine_ref[here, :], got_ref[here, :])


def sum_second_kernel(info_ref, own_a, got_a, keep_b, got_b, keep_a, send_a, own_b, away_b):
    quarter = keep_a.shape[0]
    for out, other in ((keep_a, False), (send_a, True)):
        rows = bit_rows(info_ref, 0, quarter, other)
        out[...] = add_refs(own_a[rows, :], got_a[rows, :])
    own_b[...] = add_refs(keep_b[:quarter, :], got_b[:quarter, :])
    away_b[...] = add_refs(keep_b[quarter:, :], got_b[quarter:, :])


def sum_third_kernel(info_ref, keep_a, got_a, own_b, got_b, keep, send):
    first = info_ref[3] == 0
    a = add_refs(keep_a[...], got_a[...])
    b = add_refs(own_b[...], got_b[...])

    @pl.when(first)
    def _():
        keep[...] = a
        send[...] = b

    @pl.when(jnp.logical_not(first))
    def _():
        keep[...] = b
        send[...] = a


def sum_more_kernel(index, info_ref, keep_in, got, keep, send):
    half = keep.shape[0]
    for out, other in ((keep, False), (send, True)):
        rows = bit_rows(info_ref, index, half, other)
        out[...] = add_refs(keep_in[rows, :], got[rows, :])


def sum_join_kernel(index, info_ref, own, got, out):
    half = own.shape[0]
    out[bit_rows(info_ref, index, half), :] = own[...]
    out[bit_rows(info_ref, index, half, True), :] = got[...]


class SmallSum:
    def __init__(self, values):
        self.values = values
        self.moves = [swap_core, swap_y] + [lambda v, bit=bit: swap_dp(v, bit) for bit in dp_bits()]
        self.start()

    def start(self):
        self.got = self.moves.pop(0)(self.values)

    def step(self, *others):
        if self.got is None:
            return others
        self.values = self.values + after(self.got, *others)
        self.got = None
        if self.moves:
            self.start()
        return (self.values,)


class Sum:
    def __init__(self, info, mine, got):
        self.info = info
        self.inputs = (mine, got)
        self.rows, self.width = mine.shape[0] // 2, mine.shape[1]
        self.bits = dp_bits()

    def run(self, kernel, rows, args, scratch=()):
        outs = [((count, self.width), BF) for count in rows]
        return call(kernel, outs, (self.info, *args), scratch=scratch, smem=(0,), us=0.8)

    def start(self):
        half = self.rows // 2
        self.own_a, away_a, self.keep_b, send_b = self.run(sum_start_kernel, [half] * 4, self.inputs)
        self.got = (swap_y(away_a), swap_dp(send_b, self.bits[0]))
        return (away_a,)

    def second(self, *others):
        quarter = self.rows // 4
        got_a, got_b = (after(value, *others) for value in self.got)
        self.keep_a, send_a, self.own_b, away_b = self.run(
            sum_second_kernel, [quarter] * 4, (self.own_a, got_a, self.keep_b, got_b)
        )
        self.got = (swap_dp(send_a, self.bits[0]), swap_y(away_b))
        return (send_a,)

    def third(self, *others):
        quarter = self.rows // 4
        got_a, got_b = (after(value, *others) for value in self.got)
        self.keep, send = self.run(sum_third_kernel, [quarter] * 2, (self.keep_a, got_a, self.own_b, got_b))
        self.got = swap_dp(send, self.bits[1])
        self.count = quarter
        self.index = 2
        return (send,)

    def more(self, *others):
        got = after(self.got, *others)
        if self.index < len(self.bits):
            self.count //= 2
            index = self.index
            self.keep, send = self.run(
                lambda *refs: sum_more_kernel(index, *refs), [self.count] * 2, (self.keep, got)
            )
            self.got = swap_dp(send, self.bits[index])
            self.index += 1
            return (send,)
        self.block = add_low(self.keep, got)
        self.gather_start()
        return (self.block,)

    def gather_start(self):
        self.index -= 1
        if self.index >= 2:
            self.got = swap_dp(self.block, self.bits[self.index])
        else:
            self.near = swap_dp(self.block, self.bits[1])
            self.across = swap_dp(self.block, self.bits[0])

    def gather(self, *others):
        got = after(self.got, *others)
        index = self.index
        self.count *= 2
        (self.block,) = self.run(lambda *refs: sum_join_kernel(index, *refs), [self.count], (self.block, got))
        self.gather_start()
        return (self.block,)

    def finish(self, *others):
        near, across = together(self.near, self.across, *others)[:2]
        self.parts = (self.block, near, across, swap_dp(near, self.bits[0]))
        return (near,)


def halo(low, high):
    before = lax.ppermute(high, "mp", [(i, i + 1) for i in range(N_MP - 1)])
    after = lax.ppermute(low, "mp", [(i + 1, i) for i in range(N_MP - 1)])
    return before, after


def body(
    inputs,
    segments,
    cotangent,
    inner_first,
    outer_first,
    mixer_input,
    mixer_output,
    inner_second,
    outer_second,
    norm_params,
    conv_taps,
    state_maps,
    state_rates,
    inner_first_moment,
    outer_first_moment,
    mixer_input_moment,
    mixer_output_moment,
    inner_second_moment,
    outer_second_moment,
    norm_params_moment,
    conv_taps_moment,
    state_maps_moment,
    state_rates_moment,
):
    frames = inputs.shape[0]
    padded = -(-frames // ROW_CHUNK) * ROW_CHUNK
    more = padded - frames
    me = lax.axis_index("mp")
    own_states = HEADS // N_MP * STATE
    n_states = HEADS * STATE
    wide = 256
    bits = dp_bits()
    dp = lax.axis_index("dp")
    info = jnp.stack([me, me % 2] + [(dp // bit) % 2 for bit in bits])
    x_upper = dp % 2 == 1
    unit = 16 * lax.axis_size("dp")
    pack_rows = -(-(RATES_AT + 16) // unit) * unit
    tail_rows = -(-(2 * D + TILE_AT + STATE) // unit) * unit - 2 * D

    own_one = [inner_first.astype(BF), outer_first.astype(BF)]
    y_halves = [
        swap_y(jnp.where(x_upper, value[D // 2 :], value[: D // 2])) for value in own_one
    ]
    core_one = [swap_core(value) for value in own_one]
    own_two = [inner_second.astype(BF), outer_second.astype(BF)]
    maps_tile = jnp.transpose(state_maps, (2, 1, 0, 3)).reshape(STATE, wide)
    rates_row = jnp.tile(state_rates.reshape(1, own_states), (1, N_MP))
    rates_one = rates_row.astype(BF)
    rates_rest = rates_row - rates_one.astype(F32)
    rates_two = rates_rest.astype(BF)
    rates_three = (rates_rest - rates_two.astype(F32)).astype(BF)
    rates_tile = jnp.pad(
        jnp.concatenate([rates_one, rates_two, rates_three], axis=0), ((0, pack_rows - RATES_AT - 3), (0, 0))
    )
    own_mixer = jnp.concatenate(
        [
            mixer_input.reshape(D, wide).astype(BF),
            mixer_output[:, :wide].astype(BF),
            mixer_output[:, wide:].astype(BF),
            maps_tile.astype(BF),
            rates_tile,
        ],
        axis=0,
    )
    norm_rows = norm_params.reshape(10, D)
    x = jnp.pad(inputs, ((0, more), (0, 0)))
    cot = jnp.pad(cotangent, ((0, more), (0, 0)))
    taps = jnp.pad(conv_taps, ((0, 1), (0, 0)))
    past, future, bounds = call(
        lambda info_ref, *refs: place_kernel(info_ref, frames, *refs),
        [((padded, 128), jnp.int32), ((padded, 128), jnp.int32), ((8, 128), jnp.int32)],
        (info, segments),
        smem=(0,),
    )
    y_halves[0] = after(y_halves[0], own_mixer, *own_two, norm_rows, x, past)
    y_one = []
    for half in y_halves:
        across = swap_dp(half, 1)
        y_one.append(
            jnp.concatenate([jnp.where(x_upper, across, half), jnp.where(x_upper, half, across)], axis=0)
        )
    both_one = [swap_core(value) for value in y_one]
    one_refs = []
    for group in (own_one, y_one, core_one, both_one):
        one_refs.extend(group)
    own_mixer = after(own_mixer, y_halves[1])
    half = pack_rows // 2
    mixer_half = swap_y(jnp.where(x_upper, own_mixer[half:], own_mixer[:half]))
    core_mixer = swap_core(own_mixer)
    send_half = after(jnp.where(x_upper, own_two[1], own_two[0]), mixer_half)
    two_half = swap_y(send_half)
    core_two = [swap_core(after(value, mixer_half)) for value in own_two]
    mixer_across = swap_dp(mixer_half, 1)

    frame_shape = (padded, D)
    hidden_shape = (padded, FF)
    state_shape = (padded, n_states)
    edge = ((16, D), BF)
    frame_scratch = pltpu.VMEM((padded + 32, D), F32)
    map_scratch = pltpu.VMEM((n_states, D), BF)
    out_scratch = pltpu.VMEM((D, D), BF)

    act_one, gated_one, slope_one, stream_one = call(
        first_kernel,
        [(frame_shape, BF), (hidden_shape, BF), (hidden_shape, BF), (frame_shape, F32)],
        (after(x, send_half), norm_rows, *one_refs),
        us=6.6,
    )
    mixer_across = after(mixer_across, stream_one)
    y_mixer = jnp.concatenate(
        [jnp.where(x_upper, mixer_across, mixer_half), jnp.where(x_upper, mixer_half, mixer_across)], axis=0
    )
    wm = jnp.stack([own_mixer, y_mixer, core_mixer, swap_core(y_mixer)])
    two_half = after(two_half, stream_one, y_mixer)
    two_across = swap_dp(two_half, 1)
    act_two, signal, gate, driven, states_local, final = call(
        lambda *refs: mixer_in_kernel(frames, *refs),
        [(frame_shape, BF), (frame_shape, BF), (frame_shape, F32), (state_shape, F32), (state_shape, F32), ((8, n_states), F32)],
        (info, after(stream_one, two_half), norm_rows, wm, past),
        scratch=[map_scratch],
        smem=(0,),
        us=4.2,
    )
    finals = lax.all_gather(final, "mp", axis=0, tiled=True)
    states, carry_in, result, mixed, stream_two, act_three, low, high = call(
        lambda *refs: mixer_out_kernel(frames, *refs),
        [(state_shape, F32), ((8, n_states), F32), (frame_shape, F32), (frame_shape, BF), (frame_shape, F32), (frame_shape, F32), edge, edge],
        (info, states_local, finals, past, bounds, wm, gate, stream_one, norm_rows),
        scratch=[map_scratch, out_scratch],
        smem=(0,),
        us=2.1,
    )
    act_before, act_after = halo(low, high)
    two_across = after(two_across, stream_two)
    y_two = [jnp.where(x_upper, two_across, two_half), jnp.where(x_upper, two_half, two_across)]
    both_two = [swap_core(value) for value in y_two]
    two_refs = []
    for group in (own_two, y_two, core_two, both_two):
        two_refs.extend(group)
    layer_output, act_four, gated_four, grad_pre_four, back_four, grad_three, grad_conv, low, high, norm_high = call(
        lambda *refs: second_kernel(frames, *refs),
        [
            ((frames, D), BF), (frame_shape, BF), (hidden_shape, BF), (hidden_shape, BF), (frame_shape, BF),
            (frame_shape, F32), (frame_shape, F32), edge, edge, ((32, D), F32),
        ],
        (act_three, act_before, act_after, past, future, taps, stream_two, norm_rows, *two_refs, cot),
        scratch=[frame_scratch, pltpu.VMEM(frame_shape, F32), pltpu.VMEM(hidden_shape, BF), pltpu.VMEM(frame_shape, BF)],
        us=16.6,
    )
    grad_before, grad_after = halo(low, high)
    send_two = weight_grads(2, act_four, gated_four, grad_pre_four, back_four)
    keep_two = weight_grads(0, act_four, gated_four, grad_pre_four, back_four)
    got_two = swap_core(send_two)

    grad_two, back_two, grad_result, grad_gate, adjoint, first, taps_part, norm_two = call(
        lambda *refs: conv_back_kernel(frames, *refs),
        [
            (frame_shape, F32), (frame_shape, BF), (frame_shape, BF), (frame_shape, BF), (state_shape, F32),
            ((8, n_states), F32), ((8 * KSIZE, D), F32), ((16, D), F32),
        ],
        (
            info, act_three, act_before, act_after, grad_conv, grad_before, grad_after, past, future, taps,
            after(grad_three, keep_two, send_two), stream_two, norm_rows, wm, gate, result,
        ),
        scratch=[frame_scratch, frame_scratch, pltpu.VMEM(frame_shape, F32), map_scratch, out_scratch],
        smem=(0,),
        us=11.8,
    )
    firsts = lax.all_gather(first, "mp", axis=0, tiled=True)
    sum_two = Sum(info, keep_two, after(got_two, firsts))
    started = sum_two.start()
    grad_one, keep_mixer, send_mixer, rates_part, norm_one = call(
        lambda *refs: mixer_back_kernel(frames, *refs),
        [(frame_shape, F32), ((2 * tail_rows, D), BF), ((2 * tail_rows, D), BF), ((8, n_states), F32), ((16, D), F32)],
        (
            info, adjoint, firsts, past, future, bounds, states, carry_in, driven, wm, signal, grad_gate,
            act_two, stream_one, norm_rows, after(grad_two, *started), mixed, back_two, grad_result,
        ),
        scratch=[
            pltpu.VMEM(state_shape, BF), map_scratch, pltpu.VMEM(frame_shape, BF), pltpu.VMEM((N_MP, tail_rows, D), BF)
        ],
        smem=(0,),
        us=5.5,
    )
    got_mixer = swap_core(send_mixer)
    extra_bits = len(bits) - 2
    wide_shape = mixer_input.shape
    first_scale = 0.5 * math.sqrt(max(D, FF) / D)
    second_scale = 0.5 * math.sqrt(max(D, FF) / FF)
    made = {}

    def first_back(*others):
        made["pre"], made["back"], made["act"] = call(
            first_back_kernel,
            [(hidden_shape, BF), (frame_shape, BF), (frame_shape, F32)],
            (after(grad_one, *others), slope_one, *one_refs),
            us=5.4,
        )
        return (made["back"],)

    def first_send(*others):
        made["send"] = weight_grads(2, act_one, gated_one, made["pre"], after(made["back"], *others))
        made["got"] = swap_core(made["send"])
        return (made["send"],)

    def first_keep(*others):
        made["keep"] = weight_grads(0, act_one, gated_one, made["pre"], after(made["back"], *others))
        return (made["keep"],)

    def first_start(*others):
        made["o"] = Sum(info, made["keep"], after(made["got"], *others))
        return made["o"].start()

    def mixer_start(*others):
        made["m"] = Sum(info, keep_mixer, after(got_mixer, *others))
        return made["m"].start()

    made["t"] = sum_two

    def steps_of(chain, moments, scales, params):
        def step(name):
            return lambda *others: getattr(made[chain], name)(*others)

        def several(name):
            def run(*others):
                for _ in range(extra_bits - 1):
                    others = getattr(made[chain], name)(*others)
                return getattr(made[chain], name)(*others)

            return run

        def moment(*others):
            parts = tuple(after(v, *others) for v in made[chain].parts)
            left = (made["tx"].own, made["tx"].other) if chain == "m" else ()
            made[chain + "x"] = Muon(info, parts, moments, chain, left)
            return (made[chain + "x"].own,)

        def muon(name):
            return lambda *others: getattr(made[chain + "x"], name)(*others)

        def update(*others):
            factors = made["ox" if chain == "o" else "mx"].factors
            made[chain + "r"] = made[chain + "x"].update(scales, params, factors, *others)
            return (made[chain + "r"][0][2],)

        head = [
            step("second"), step("third"), several("more"), step("more"), several("gather"), step("finish"), moment
        ]
        middle = {"t": [], "o": ["exchange", "newton"], "m": ["exchange", "newton", "share"]}[chain]
        return head + [muon(name) for name in middle] + [update]

    def input_step(*others):
        input_grad, small = call(
            lambda *refs: input_grad_kernel(frames, *refs),
            [((frames, D), F32), ((32, D), F32)],
            (x, after(made["act"], *others), norm_rows, grad_one, norm_one, norm_two, norm_high, taps_part, rates_part),
            scratch=[pltpu.VMEM(frame_shape, F32), pltpu.VMEM((16, D), F32)],
            us=2.4,
        )
        made["input_grad"], made["s"] = input_grad, SmallSum(small)
        return (small,)

    def small_step(*others):
        return made["s"].step(*others)

    def small_last(*others):
        while made["s"].got is not None:
            others = made["s"].step(*others)
        return others

    def small_params(*others):
        small = after(made["s"].values, *others)
        mixer = made["mx"]
        norm_sum = small[:10].reshape(norm_params.shape)
        taps_sum = small[10 : 10 + KSIZE]
        rates_sum = lax.dynamic_slice_in_dim(small[10 + KSIZE], me * own_states, own_states, 0).reshape(state_rates.shape)
        maps_sum = jnp.transpose(mixer.extra[0].reshape(STATE, 2, HEADS // N_MP, HD), (2, 1, 0, 3))
        tokens_all = frames * lax.axis_size("dp") * lax.axis_size("mp")
        small_results = []
        for factor, grad, moment, param in (
            (SMALL_FACTORS[0], norm_sum, norm_params_moment, norm_params),
            (SMALL_FACTORS[1], taps_sum, conv_taps_moment, conv_taps),
            (SMALL_FACTORS[2], maps_sum, state_maps_moment, state_maps),
            (SMALL_FACTORS[3], rates_sum, state_rates_moment, state_rates),
        ):
            moment_new = 0.5 * moment + grad
            small_results.extend((grad, moment_new, param - factor / math.sqrt(tokens_all) * moment_new))
        made["small"] = small_results
        made["in"] = [values[1].reshape(wide_shape) for values in (mixer.grads, mixer.news)]
        return (*small_results, *made["in"])

    chains = {
        "t": steps_of("t", (outer_second_moment, inner_second_moment), (second_scale, first_scale), (outer_second, inner_second)),
        "m": [mixer_start]
        + steps_of(
            "m", (mixer_output_moment, mixer_input_moment.reshape(D, wide)), (0.5, 0.5 * math.sqrt(2.0)),
            (mixer_output, mixer_input.reshape(D, wide)),
        ),
        "o": [first_back, first_send, first_keep, first_start]
        + steps_of("o", (outer_first_moment, inner_first_moment), (second_scale, first_scale), (outer_first, inner_first)),
        "s": [input_step] + [small_step] * 4 + [small_last],
        "p": [small_params],
    }
    started = (grad_one,)
    for name in ORDER:
        started = chains[name].pop(0)(*started)
    input_grad, small_results = made["input_grad"], made["small"]
    down_two, up_two = made["tr"]
    down_one, up_one = made["or"]
    out_triple, in_triple = made["mr"]
    in_triple = [*made["in"], in_triple[2].reshape(wide_shape)]
    results = [layer_output, input_grad]
    for triple in (up_one, down_one, in_triple, out_triple, up_two, down_two):
        results.extend(triple)
    results.extend(small_results)
    return tuple(results)


def solution(mesh):
    in_specs = (
        P(("dp", "mp"), None),
        P("dp", None),
        P(("dp", "mp"), None),
        P(None, "mp"),
        P("mp", None),
        P(None, None, "mp"),
        P("mp", None),
        P(None, "mp"),
        P("mp", None),
        P(),
        P(),
        P("mp", None, None, None),
        P("mp", None),
        P(None, "mp"),
        P("mp", None),
        P(None, None, "mp"),
        P("mp", None),
        P(None, "mp"),
        P("mp", None),
        P(),
        P(),
        P("mp", None, None, None),
        P("mp", None),
    )
    out_specs = (
        P(("dp", "mp"), None),
        P(("dp", "mp"), None),
        P(None, "mp"),
        P(None, "mp"),
        P(None, "mp"),
        P("mp", None),
        P("mp", None),
        P("mp", None),
        P(None, None, "mp"),
        P(None, None, "mp"),
        P(None, None, "mp"),
        P("mp", None),
        P("mp", None),
        P("mp", None),
        P(None, "mp"),
        P(None, "mp"),
        P(None, "mp"),
        P("mp", None),
        P("mp", None),
        P("mp", None),
        P(),
        P(),
        P(),
        P(),
        P(),
        P(),
        P("mp", None, None, None),
        P("mp", None, None, None),
        P("mp", None, None, None),
        P("mp", None),
        P("mp", None),
        P("mp", None),
    )
    return jax.shard_map(body, mesh=mesh, in_specs=in_specs, out_specs=out_specs, check_vma=False)
```

```python
import math

import jax
import jax.numpy as jnp
from jax import lax
from jax.experimental import pallas as pl
from jax.experimental.pallas import tpu as pltpu
from jax.sharding import PartitionSpec as P

D = 512
FF = 2048
HEADS = 8
STATE = 32
HD = 64
KSIZE = 15
MARGIN = (KSIZE - 1) // 2
NS_STEPS = 5
N_MP = 4
BF = jnp.bfloat16
F32 = jnp.float32

COEF_A = 3.4445
COEF_B = -4.775
COEF_C = 2.0315
NORM_EPS = 1e-05
SMALL_FACTORS = (0.2, 0.2, 0.2, 4.0)
VMEM_LIMIT = 24 * 1024 * 1024
ROW_CHUNK = 320
CONV_CHUNK = 64
MAPS_AT = D + 256
RATES_AT = MAPS_AT + STATE
SEGS = 6
SQUARES = (1, 3, 3, 3, 3)
ORDER = "otomtoomstomstomtostmsotmsomsmmomoomopmotm"
OUT_AT = 256
TILE_AT = OUT_AT + 128
FLOPS_PER_US = 1.0e9


def dot(left, right, dims):
    return lax.dot_general(left, right, ((dims[0], dims[1]), ((), ())), preferred_element_type=F32)


def dot_nn(left, right):
    return dot(left, right, ((1,), (0,)))


def dot_tn(left, right):
    return dot(left, right, ((0,), (0,)))


def dot_nt(left, right):
    return dot(left, right, ((1,), (1,)))


def split_low(values):
    high = values.astype(BF)
    return high, (values - high.astype(F32)).astype(BF)


def dot3(left, right, kind):
    lh, ll = left
    rh, rl = right
    return kind(lh, rh) + (kind(lh, rl) + kind(ll, rh))


def swap_core(values):
    return lax.ppermute(values, "mp", [(i, i ^ 1) for i in range(N_MP)])


def swap_y(values):
    return lax.ppermute(values, "mp", [(i, i ^ 2) for i in range(N_MP)])


def swap_dp(values, bit):
    count = lax.axis_size("dp")
    return lax.ppermute(values, "dp", [(i, i ^ bit) for i in range(count)])


def dp_bits():
    count = lax.axis_size("dp")
    bits = []
    bit = 1
    while bit < count:
        bits.append(bit)
        bit *= 2
    return bits


def add_low(left, right):
    return (left.astype(F32) + right.astype(F32)).astype(BF)


def swish_parts(values):
    gate = 0.5 * jnp.tanh(0.5 * values) + 0.5
    active = values * gate
    return active, gate + active * (1.0 - gate)


def normed(values):
    middle = jnp.mean(values, axis=-1, keepdims=True)
    centred = values - middle
    spread = jnp.mean(centred * centred, axis=-1, keepdims=True)
    scale = lax.rsqrt(spread + NORM_EPS)
    return centred * scale, scale


def norm_forward(values, norm_ref, index):
    unit, _ = normed(values)
    return unit * norm_ref[2 * index : 2 * index + 1, :] + norm_ref[2 * index + 1 : 2 * index + 2, :]


def fold(values):
    return jnp.sum(values.reshape(values.shape[0] // 8, 8, values.shape[1]), axis=0)


def norm_backward(values, grad, norm_ref, index):
    unit, scale = normed(values)
    wide = grad * norm_ref[2 * index : 2 * index + 1, :]
    mean_one = jnp.mean(wide, axis=-1, keepdims=True)
    mean_two = jnp.mean(wide * unit, axis=-1, keepdims=True)
    return scale * (wide - mean_one - unit * mean_two), fold(grad * unit), fold(grad)


def for_rows(total, size, fn):
    def step(index, carry):
        fn(pl.ds(pl.multiple_of(index * size, size), size))
        return carry

    lax.fori_loop(0, total // size, step, 0)


def lanes(column, width):
    return jnp.concatenate([column] * (width // 128), axis=1)


def after(value, *others):
    return lax.optimization_barrier((value, *others))[0]


def together(*values):
    return lax.optimization_barrier(values)


def call(kernel, outs, args, scratch=(), smem=(), us=1.0):
    in_specs = [pl.BlockSpec(memory_space=pltpu.SMEM if i in smem else pltpu.VMEM) for i in range(len(args))]
    return pl.pallas_call(
        kernel,
        out_shape=tuple(jax.ShapeDtypeStruct(shape, dtype) for shape, dtype in outs),
        in_specs=in_specs,
        out_specs=tuple(pl.BlockSpec(memory_space=pltpu.VMEM) for _ in outs),
        scratch_shapes=list(scratch),
        compiler_params=pltpu.CompilerParams(vmem_limit_bytes=VMEM_LIMIT),
        cost_estimate=pl.CostEstimate(flops=int(us * FLOPS_PER_US), bytes_accessed=1 << 16, transcendentals=0),
    )(*args)


def block_place(block, me):
    mask = block ^ me
    return (mask & 1) * 2 + (mask >> 1)


def first_kernel(x_ref, norm_ref, u0, d0, u1, d1, u2, d2, u3, d3, act_ref, gated_ref, slope_ref, stream_ref):
    def chunk(rows):
        x = x_ref[rows, :].astype(F32)
        act = norm_forward(x, norm_ref, 0).astype(BF)
        act_ref[rows, :] = act
        total = jnp.zeros(x.shape, F32)
        for k, (up, down) in enumerate(((u0, d0), (u1, d1), (u2, d2), (u3, d3))):
            active, slope = swish_parts(dot_nn(act, up[...]))
            active = active.astype(BF)
            gated_ref[rows, k * D : (k + 1) * D] = active
            slope_ref[rows, k * D : (k + 1) * D] = slope.astype(BF)
            total = total + dot_nn(active, down[...])
        stream_ref[rows, :] = x + 0.5 * total

    for_rows(x_ref.shape[0], ROW_CHUNK, chunk)


def fill_maps(me, wm_ref, map_ref, side):
    map_ref[...] = jnp.zeros(map_ref.shape, BF)
    lane = lax.broadcasted_iota(jnp.int32, (STATE, 128), 1)
    for block in range(N_MP):
        tile = wm_ref[block_place(block, me), MAPS_AT : MAPS_AT + STATE, side * 128 : (side + 1) * 128]
        for j in range(2):
            head = 2 * block + j
            keep = jnp.where((lane >= HD) == (j == 1), tile.astype(F32), 0.0)
            map_ref[head * STATE : (head + 1) * STATE, block * 128 : (block + 1) * 128] = keep.astype(BF)


def rates_of(me, wm_ref):
    lane = lax.broadcasted_iota(jnp.int32, (1, HEADS * STATE), 1)
    own_states = HEADS // N_MP * STATE
    total = jnp.zeros((1, HEADS * STATE), F32)
    for block in range(N_MP):
        parts = wm_ref[block_place(block, me), RATES_AT : RATES_AT + 16, :].astype(F32)
        here = (lane >= block * own_states) & (lane < (block + 1) * own_states)
        total = jnp.where(here, parts[0:1] + parts[1:2] + parts[2:3], total)
    rate = jnp.exp(total)
    decays = jnp.exp(-rate)
    return rate, decays, jnp.sqrt(1.0 - decays * decays)


def no_start(bounds_ref, low, high):
    free = jnp.ones((1, 1), F32)
    for v in range(SEGS - 1):
        bound = bounds_ref[v : v + 1, :1]
        free = jnp.where((bound >= low) & (bound <= high), 0.0, free)
    return free


def place_kernel(info_ref, frames, segments_ref, past_ref, future_ref, bounds_ref):
    row = segments_ref[...]
    length = row.shape[1]
    frame = lax.broadcasted_iota(jnp.int32, past_ref.shape, 0)
    real = frame < frames
    frame = frame + info_ref[0] * frames
    begin = jnp.zeros(past_ref.shape, jnp.int32)
    end = jnp.full(past_ref.shape, length, jnp.int32)
    bounds_ref[...] = jnp.zeros(bounds_ref.shape, jnp.int32)
    for v in range(1, SEGS):
        bound = jnp.sum((row < v).astype(F32), axis=1, keepdims=True).astype(jnp.int32)
        bounds_ref[v - 1 : v, :] = jnp.broadcast_to(bound, (1, 128))
        begin = jnp.where(bound <= frame, jnp.maximum(begin, bound), begin)
        end = jnp.where(bound > frame, jnp.minimum(end, bound), end)
    past_ref[...] = jnp.where(real, frame - begin, -1)
    future_ref[...] = jnp.where(real, end - 1 - frame, -1)


def scan_steps(states_ref, reach, rate, backward):
    frames = states_ref.shape[0]
    wide = lanes(reach, states_ref.shape[1])
    states = states_ref[...]
    step = 1
    while step < frames:
        moved = pltpu.roll(states, frames - step if backward else step, 0)
        factor = jnp.exp(-float(step) * rate)
        states = states + jnp.where(wide >= step, moved * factor, 0.0)
        step *= 2
    states_ref[...] = states


def mixer_in_kernel(
    frames, info_ref, stream_ref, norm_ref, wm_ref, past_ref,
    act_ref, signal_ref, gate_ref, driven_ref, states_ref, final_ref, map_ref,
):
    me = info_ref[0]
    rate, _, gain = rates_of(me, wm_ref)
    fill_maps(me, wm_ref, map_ref, 0)

    def chunk(rows):
        act = norm_forward(stream_ref[rows, :], norm_ref, 1).astype(BF)
        act_ref[rows, :] = act
        for block in range(N_MP):
            both = dot_nn(act, wm_ref[block_place(block, me), :D, :])
            signal_ref[rows, block * 128 : (block + 1) * 128] = both[:, :128].astype(BF)
            gate_ref[rows, block * 128 : (block + 1) * 128] = both[:, 128:]
        driven = dot_nt(signal_ref[rows, :], map_ref[...]) * gain
        driven_ref[rows, :] = driven
        states_ref[rows, :] = driven

    for_rows(stream_ref.shape[0], ROW_CHUNK, chunk)
    local = lax.broadcasted_iota(jnp.int32, past_ref.shape, 0)
    scan_steps(states_ref, jnp.minimum(past_ref[...], local), rate, False)
    final_ref[...] = states_ref[frames - 8 : frames, :]


def fill_out(me, wm_ref, out_ref):
    for block in range(N_MP):
        for half in range(2):
            out_ref[block * 128 : (block + 1) * 128, half * 256 : (half + 1) * 256] = wm_ref[
                block_place(block, me), D + half * 128 : D + (half + 1) * 128, :
            ]


def mixer_out_kernel(
    frames, info_ref, states_in_ref, finals_ref, past_ref, bounds_ref, wm_ref, gate_ref, stream_ref, norm_ref,
    states_ref, carry_ref, result_ref, mixed_ref, stream_two_ref, act_ref, low_ref, high_ref, map_ref, out_ref,
):
    me = info_ref[0]
    fill_maps(me, wm_ref, map_ref, 1)
    fill_out(me, wm_ref, out_ref)
    rate, _, _ = rates_of(me, wm_ref)
    across = jnp.exp(-float(frames) * rate)
    carry = jnp.zeros(rate.shape, F32)
    mine = carry
    for k in range(N_MP):
        mine = jnp.where(me == k, carry, mine)
        whole = no_start(bounds_ref, k * frames, (k + 1) * frames - 1)
        carry = finals_ref[8 * k + 7 : 8 * k + 8, :] + whole * across * carry
    carry_ref[...] = jnp.broadcast_to(mine, carry_ref.shape)

    def chunk(rows):
        past = past_ref[rows, :]
        local = lax.broadcasted_iota(jnp.int32, past.shape, 0) + rows.start
        reach = lanes(jnp.where(past > local, local + 1, 0).astype(F32), rate.shape[1])
        states = states_in_ref[rows, :] + jnp.where(reach > 0.0, jnp.exp(-rate * reach) * mine, 0.0)
        states_ref[rows, :] = states
        result = dot_nn(states.astype(BF), map_ref[...])
        result_ref[rows, :] = result
        mixed = (result * swish_parts(gate_ref[rows, :])[0]).astype(BF)
        mixed_ref[rows, :] = mixed
        stream = stream_ref[rows, :] + dot_nn(mixed, out_ref[...])
        stream_two_ref[rows, :] = stream
        act_ref[rows, :] = norm_forward(stream, norm_ref, 2).astype(BF).astype(F32)

    for_rows(stream_ref.shape[0], ROW_CHUNK, chunk)
    low_ref[...] = act_ref[:16, :].astype(BF)
    high_ref[...] = act_ref[frames - 16 : frames, :].astype(BF)


def fill_frame(frames, frame_ref, own_ref, before_ref, after_ref):
    frame_ref[:8, :] = before_ref[8:, :].astype(F32)
    frame_ref[8 : 8 + frames, :] = own_ref[:frames, :]
    frame_ref[8 + frames : 24 + frames, :] = after_ref[...].astype(F32)


def open_taps(past, future, offset):
    shift = offset - MARGIN
    return past >= -shift if shift < 0 else future >= shift


def conv_rows(frame_ref, taps_ref, past_ref, future_ref, start, flip):
    rows = pl.ds(start, CONV_CHUNK)
    past, future = past_ref[rows, :], future_ref[rows, :]
    total = jnp.zeros((CONV_CHUNK, D), F32)
    block = frame_ref[pl.ds(start, CONV_CHUNK + 16), :]
    for offset in range(KSIZE):
        tap = KSIZE - 1 - offset if flip else offset
        here = block[offset + 1 : offset + 1 + CONV_CHUNK, :]
        term = here * taps_ref[tap : tap + 1, :]
        if offset != MARGIN:
            term = jnp.where(lanes(open_taps(past, future, offset), D), term, 0.0)
        total = total + term
    if flip:
        total = jnp.where(lanes(past >= 0, D), total, 0.0)
    return total


def second_kernel(
    frames, act_three_ref, before_ref, after_ref, past_ref, future_ref, taps_ref, stream_two_ref, norm_ref,
    u0, d0, u1, d1, u2, d2, u3, d3, cot_ref,
    output_ref, act_ref, gated_ref, grad_pre_ref, back_ref, grad_three_ref, grad_conv_ref, low_ref, high_ref, norm_grad_ref,
    frame_ref, pre_ref, slope_ref, out_ref,
):
    fill_frame(frames, frame_ref, act_three_ref, before_ref, after_ref)
    norm_grad_ref[...] = jnp.zeros(norm_grad_ref.shape, F32)
    weights = ((u0, d0), (u1, d1), (u2, d2), (u3, d3))

    def conv(index, carry):
        start = pl.multiple_of(index * CONV_CHUNK, CONV_CHUNK)
        pre_ref[pl.ds(start, CONV_CHUNK), :] = conv_rows(frame_ref, taps_ref, past_ref, future_ref, start, False)
        return carry

    lax.fori_loop(0, pre_ref.shape[0] // CONV_CHUNK, conv, 0)

    def chunk(rows):
        active, conv_slope = swish_parts(pre_ref[rows, :])
        stream_three = stream_two_ref[rows, :] + active
        act = norm_forward(stream_three, norm_ref, 3).astype(BF)
        act_ref[rows, :] = act
        total = jnp.zeros(active.shape, F32)
        for k, (up, down) in enumerate(weights):
            hidden, slope = swish_parts(dot_nn(act, up[...]))
            hidden = hidden.astype(BF)
            gated_ref[rows, k * D : (k + 1) * D] = hidden
            slope_ref[rows, k * D : (k + 1) * D] = slope.astype(BF)
            total = total + dot_nn(hidden, down[...])
        stream_four = stream_three + 0.5 * total
        out_ref[rows, :] = norm_forward(stream_four, norm_ref, 4).astype(BF)
        grad_four, gain, bias = norm_backward(stream_four, cot_ref[rows, :].astype(F32), norm_ref, 4)
        norm_grad_ref[16:24, :] += gain
        norm_grad_ref[24:32, :] += bias
        back = (0.5 * grad_four).astype(BF)
        back_ref[rows, :] = back
        grad_act = jnp.zeros(active.shape, F32)
        for k, (up, down) in enumerate(weights):
            grad_gated = dot_nt(back, down[...])
            grad_pre = (grad_gated * slope_ref[rows, k * D : (k + 1) * D].astype(F32)).astype(BF)
            grad_pre_ref[rows, k * D : (k + 1) * D] = grad_pre
            grad_act = grad_act + dot_nt(grad_pre, up[...])
        grad_part, gain, bias = norm_backward(stream_three, grad_act, norm_ref, 3)
        norm_grad_ref[:8, :] += gain
        norm_grad_ref[8:16, :] += bias
        grad_three = grad_four + grad_part
        grad_three_ref[rows, :] = grad_three
        grad_conv_ref[rows, :] = (grad_three * conv_slope).astype(BF).astype(F32)

    for_rows(pre_ref.shape[0], ROW_CHUNK, chunk)
    output_ref[...] = out_ref[:frames, :]
    low_ref[...] = grad_conv_ref[:16, :].astype(BF)
    high_ref[...] = grad_conv_ref[frames - 16 : frames, :].astype(BF)


def weight_grad_kernel(first, act_ref, gated_ref, grad_pre_ref, back_ref, out_ref):
    for k in range(2):
        columns = slice((first + k) * D, (first + k + 1) * D)
        out_ref[2 * k * D : (2 * k + 1) * D, :] = dot_tn(act_ref[...], grad_pre_ref[:, columns]).astype(BF)
        out_ref[(2 * k + 1) * D : (2 * k + 2) * D, :] = dot_tn(gated_ref[:, columns], back_ref[...]).astype(BF)


def weight_grads(first, act, gated, grad_pre, back):
    return call(
        lambda *refs: weight_grad_kernel(first, *refs), [((4 * D, D), BF)], (act, gated, grad_pre, back), us=2.0
    )[0]


def conv_back_kernel(
    frames, info_ref, act_three_ref, act_before_ref, act_after_ref, grad_conv_ref, before_ref, after_ref,
    past_ref, future_ref, taps_ref, grad_three_ref, stream_two_ref, norm_ref, wm_ref, gate_ref, result_ref,
    grad_two_ref, back_ref, grad_result_ref, grad_gate_ref, adjoint_ref, first_ref, taps_grad_ref, norm_grad_ref,
    act_frame_ref, frame_ref, grad_act_ref, map_ref, out_ref,
):
    me = info_ref[0]
    fill_frame(frames, act_frame_ref, act_three_ref, act_before_ref, act_after_ref)
    fill_frame(frames, frame_ref, grad_conv_ref, before_ref, after_ref)
    fill_maps(me, wm_ref, map_ref, 1)
    fill_out(me, wm_ref, out_ref)
    taps_grad_ref[...] = jnp.zeros(taps_grad_ref.shape, F32)
    norm_grad_ref[...] = jnp.zeros(norm_grad_ref.shape, F32)

    def conv(index, carry):
        start = pl.multiple_of(index * CONV_CHUNK, CONV_CHUNK)
        rows = pl.ds(start, CONV_CHUNK)
        grad_act_ref[rows, :] = conv_rows(frame_ref, taps_ref, past_ref, future_ref, start, True)
        past, future = past_ref[rows, :], future_ref[rows, :]
        block = act_frame_ref[pl.ds(start, CONV_CHUNK + 16), :]
        grad = grad_conv_ref[rows, :]
        for offset in range(KSIZE):
            term = grad * block[offset + 1 : offset + 1 + CONV_CHUNK, :]
            if offset != MARGIN:
                term = jnp.where(lanes(open_taps(past, future, offset), D), term, 0.0)
            taps_grad_ref[8 * offset : 8 * offset + 8, :] += fold(term)
        return carry

    lax.fori_loop(0, grad_act_ref.shape[0] // CONV_CHUNK, conv, 0)

    def chunk(rows):
        grad_part, gain, bias = norm_backward(stream_two_ref[rows, :], grad_act_ref[rows, :], norm_ref, 2)
        norm_grad_ref[:8, :] += gain
        norm_grad_ref[8:16, :] += bias
        grad_two = grad_three_ref[rows, :] + grad_part
        grad_two_ref[rows, :] = grad_two
        back = grad_two.astype(BF)
        back_ref[rows, :] = back
        grad_mixed = dot_nt(back, out_ref[...])
        active, slope = swish_parts(gate_ref[rows, :])
        grad_result = (grad_mixed * active).astype(BF)
        grad_result_ref[rows, :] = grad_result
        grad_gate_ref[rows, :] = (grad_mixed * result_ref[rows, :] * slope).astype(BF)
        adjoint_ref[rows, :] = dot_nt(grad_result, map_ref[...])

    for_rows(grad_act_ref.shape[0], ROW_CHUNK, chunk)
    local = lax.broadcasted_iota(jnp.int32, future_ref.shape, 0)
    reach = jnp.where(local < frames, jnp.minimum(future_ref[...], frames - 1 - local), 0)
    scan_steps(adjoint_ref, reach, rates_of(me, wm_ref)[0], True)
    first_ref[...] = adjoint_ref[:8, :]


def mixer_back_kernel(
    frames, info_ref, adjoint_in_ref, firsts_ref, past_ref, future_ref, bounds_ref, states_ref, carry_ref,
    driven_ref, wm_ref, signal_ref, grad_gate_ref, act_ref, stream_ref, norm_ref, grad_two_ref,
    mixed_ref, back_ref, grad_result_ref,
    grad_one_ref, keep_ref, send_ref, rates_ref, norm_grad_ref, low_ref, map_ref, grad_signal_ref, pack_ref,
):
    me = info_ref[0]
    rate, decays, gain = rates_of(me, wm_ref)
    fill_maps(me, wm_ref, map_ref, 0)
    norm_grad_ref[...] = jnp.zeros(norm_grad_ref.shape, F32)
    low_ref[...] = states_ref[...].astype(BF)
    out_grad = dot_tn(mixed_ref[...], back_ref[...])
    maps_out = dot_tn(low_ref[...], grad_result_ref[...])
    across = jnp.exp(-float(frames) * rate)
    carry = jnp.zeros(rate.shape, F32)
    mine = carry
    for k in reversed(range(N_MP)):
        mine = jnp.where(me == k, carry, mine)
        whole = no_start(bounds_ref, k * frames + 1, (k + 1) * frames) if k + 1 < N_MP else 0.0
        carry = firsts_ref[8 * k : 8 * k + 1, :] + whole * across * carry
    rows_all = adjoint_in_ref.shape[0]
    local = lax.broadcasted_iota(jnp.int32, future_ref.shape, 0)
    reach = jnp.where((local < frames) & (future_ref[...] > frames - 1 - local), frames - local, 0).astype(F32)
    reach = lanes(reach, rate.shape[1])
    adjoint = adjoint_in_ref[...] + jnp.where(reach > 0.0, jnp.exp(-rate * reach) * mine, 0.0)
    low_ref[...] = (adjoint * gain).astype(BF)
    earlier = pltpu.roll(states_ref[...], 1, 0)
    place = lax.broadcasted_iota(jnp.int32, earlier.shape, 0)
    earlier = jnp.where(place == 0, carry_ref[:1, :], earlier)
    open_past = lanes(past_ref[...], rate.shape[1]) >= 1
    decay_grad = jnp.sum(jnp.where(open_past, earlier * adjoint, 0.0), axis=0, keepdims=True)
    gain_grad = jnp.sum(adjoint * driven_ref[...], axis=0, keepdims=True) / gain
    decay_grad = decay_grad - gain_grad * decays / gain
    rates_ref[...] = jnp.broadcast_to(decay_grad * decays * -rate, rates_ref.shape)
    maps = dot_tn(low_ref[...], signal_ref[...])
    lane = lax.broadcasted_iota(jnp.int32, (STATE, 128), 1)
    for block in range(N_MP):
        place_k = block_place(block, me)
        columns = slice(block * 128, (block + 1) * 128)
        pack_ref[place_k, OUT_AT:TILE_AT, :] = out_grad[columns, :].astype(BF)
        pack_ref[place_k, TILE_AT:, :] = jnp.zeros((pack_ref.shape[1] - TILE_AT, D), BF)
        for side, grads in enumerate((maps, maps_out)):
            one = grads[2 * block * STATE : (2 * block + 1) * STATE, columns]
            two = grads[(2 * block + 1) * STATE : (2 * block + 2) * STATE, columns]
            pack_ref[place_k, TILE_AT : TILE_AT + STATE, side * 128 : (side + 1) * 128] = jnp.where(lane < HD, one, two).astype(BF)

    def chunk(rows):
        grad_signal_ref[rows, :] = dot_nn(low_ref[rows, :], map_ref[...]).astype(BF)
        grad_act = jnp.zeros((ROW_CHUNK, D), F32)
        for block in range(N_MP):
            columns = slice(block * 128, (block + 1) * 128)
            both = jnp.concatenate([grad_signal_ref[rows, columns], grad_gate_ref[rows, columns]], axis=1)
            grad_act = grad_act + dot_nt(both, wm_ref[block_place(block, me), :D, :])
        grad_part, gain_sum, bias_sum = norm_backward(stream_ref[rows, :], grad_act, norm_ref, 1)
        norm_grad_ref[:8, :] += gain_sum
        norm_grad_ref[8:16, :] += bias_sum
        grad_one_ref[rows, :] = grad_two_ref[rows, :] + grad_part

    for_rows(rows_all, ROW_CHUNK, chunk)
    for block in range(N_MP):
        columns = slice(block * 128, (block + 1) * 128)
        both = jnp.concatenate([grad_signal_ref[:, columns], grad_gate_ref[:, columns]], axis=1)
        grad = dot_tn(act_ref[...], both).astype(BF)
        for half in range(2):
            pack_ref[block_place(block, me), :OUT_AT, half * 256 : (half + 1) * 256] = grad[half * 256 : (half + 1) * 256, :]
    rows = pack_ref.shape[1]
    for k in range(2):
        keep_ref[k * rows : (k + 1) * rows, :] = pack_ref[k]
        send_ref[k * rows : (k + 1) * rows, :] = pack_ref[2 + k]


def first_back_kernel(grad_one_ref, slope_ref, u0, d0, u1, d1, u2, d2, u3, d3, grad_pre_ref, back_ref, grad_act_ref):
    def chunk(rows):
        back = (0.5 * grad_one_ref[rows, :]).astype(BF)
        back_ref[rows, :] = back
        grad_act = jnp.zeros((ROW_CHUNK, D), F32)
        for k, (up, down) in enumerate(((u0, d0), (u1, d1), (u2, d2), (u3, d3))):
            grad_gated = dot_nt(back, down[...])
            grad_pre = (grad_gated * slope_ref[rows, k * D : (k + 1) * D].astype(F32)).astype(BF)
            grad_pre_ref[rows, k * D : (k + 1) * D] = grad_pre
            grad_act = grad_act + dot_nt(grad_pre, up[...])
        grad_act_ref[rows, :] = grad_act

    for_rows(grad_one_ref.shape[0], ROW_CHUNK, chunk)


def input_grad_kernel(
    frames, x_ref, grad_act_ref, norm_ref, grad_one_ref, norm_one_ref, norm_two_ref, norm_high_ref, taps_ref, rates_ref,
    grad_ref, small_ref, sum_ref, norm_grad_ref,
):
    norm_grad_ref[...] = jnp.zeros(norm_grad_ref.shape, F32)

    def chunk(rows):
        grad_part, gain, bias = norm_backward(x_ref[rows, :].astype(F32), grad_act_ref[rows, :], norm_ref, 0)
        norm_grad_ref[:8, :] += gain
        norm_grad_ref[8:16, :] += bias
        sum_ref[rows, :] = grad_one_ref[rows, :] + grad_part

    for_rows(x_ref.shape[0], ROW_CHUNK, chunk)
    grad_ref[...] = sum_ref[:frames, :]
    small_ref[...] = jnp.zeros(small_ref.shape, F32)
    row = 0
    for ref in (norm_grad_ref, norm_one_ref, norm_two_ref, norm_high_ref, taps_ref):
        for part in range(ref.shape[0] // 8):
            small_ref[row : row + 1, :] = jnp.sum(ref[8 * part : 8 * part + 8, :], axis=0, keepdims=True)
            row += 1
    small_ref[row : row + 1, : HEADS * STATE] = rates_ref[:1, :]


def triangle():
    count = D // 128
    return [(i, j) for i in range(count) for j in range(i, count)]


def put_triangle(matrix, out_ref):
    for k, (i, j) in enumerate(triangle()):
        out_ref[k * 128 : (k + 1) * 128, :] = matrix[i * 128 : (i + 1) * 128, j * 128 : (j + 1) * 128]


def get_triangle(ref, out_ref, more_ref=None):
    for k, (i, j) in enumerate(triangle()):
        block = ref[k * 128 : (k + 1) * 128, :]
        if more_ref is not None:
            block = block + more_ref[k * 128 : (k + 1) * 128, :]
        out_ref[i * 128 : (i + 1) * 128, j * 128 : (j + 1) * 128] = block
        if i != j:
            out_ref[j * 128 : (j + 1) * 128, i * 128 : (i + 1) * 128] = block.T


def fill_block(info_ref, part_refs, block_ref):
    x, z = info_ref[2], info_ref[3]
    part = part_refs[0].shape[0]
    for ref, side, half in zip(part_refs, (z, 1 - z, z, 1 - z), (x, x, 1 - x, 1 - x)):
        block_ref[pl.ds(pl.multiple_of(side * 2 * part + half * part, part), part), :] = ref[...]


def put_grams(info_ref, pair, own_ref, other_ref):
    first_pair, second_pair = split_low(pair[0]), split_low(pair[1])
    gram_first = dot3(first_pair, first_pair, dot_tn)
    gram_second = dot3(second_pair, second_pair, dot_nt)
    is_zero = info_ref[1] == 0

    @pl.when(is_zero)
    def _():
        put_triangle(gram_first, own_ref)
        put_triangle(gram_second, other_ref)

    @pl.when(jnp.logical_not(is_zero))
    def _():
        put_triangle(gram_second, own_ref)
        put_triangle(gram_first, other_ref)


def moment_kernel(kind, info_ref, *refs):
    parts, moments, block_ref = refs[:4], refs[4:6], refs[-1]
    refs = refs[6:-1]
    if kind == "m":
        left_refs, refs = refs[:2], refs[2:]
    grads, news, own_ref, other_ref = refs[:2], refs[2:4], refs[4], refs[5]
    fill_block(info_ref, parts, block_ref)
    if kind == "m":
        values = [
            block_ref[OUT_AT:TILE_AT, :],
            jnp.concatenate([block_ref[:OUT_AT, :256], block_ref[:OUT_AT, 256:]], axis=0),
        ]
        refs[6][...] = block_ref[TILE_AT : TILE_AT + STATE, :256].astype(F32)
    else:
        values = [block_ref[D:, :], block_ref[:D, :]]
    pair = []
    for value, moment, grad_ref, new_ref in zip(values, moments, grads, news):
        grad = value.astype(F32)
        grad_ref[...] = grad
        new = 0.5 * moment[...] + grad
        new_ref[...] = new
        pair.append(new)
    if kind == "o":
        put_grams(info_ref, pair, own_ref, other_ref)
        return
    mine = info_ref[2] == (0 if kind == "t" else 1)

    @pl.when(mine)
    def _():
        put_grams(info_ref, pair, own_ref, other_ref)

    @pl.when(jnp.logical_not(mine))
    def _():
        for k, ref in enumerate((own_ref, other_ref)):
            ref[...] = left_refs[k][...] if kind == "m" else jnp.zeros(ref.shape, F32)


def update_kernel(scales, kind, info_ref, *refs):
    count = 2 if kind == "o" else 4
    factors, (first_new, second_new, first_ref, second_ref, first_out, second_out, full_ref) = refs[:count], refs[count:]
    is_zero = info_ref[1] == 0
    own, other = factors[0][...], factors[1][...]
    if kind != "o":
        mine = info_ref[2] == (0 if kind == "t" else 1)
        own, other = jnp.where(mine, own, factors[2][...]), jnp.where(mine, other, factors[3][...])
    get_triangle(jnp.where(is_zero, own, other), full_ref)
    first_out[...] = first_ref[...] - scales[0] * dot3(split_low(first_new[...]), split_low(full_ref[...]), dot_nn)
    get_triangle(jnp.where(is_zero, other, own), full_ref)
    second_out[...] = second_ref[...] - scales[1] * dot3(split_low(full_ref[...]), split_low(second_new[...]), dot_nn)


def newton_poly(a, squares):
    pair = split_low(a)
    square = dot_nn(pair[0], pair[0]) if squares == 1 else dot3(pair, pair, dot_nn)
    return (COEF_B * a + COEF_C * square).astype(BF), pair


def newton_gram(a, pair, poly):
    half = COEF_A * a + (dot_nn(pair[0], poly) + dot_nn(pair[1], poly))
    high, rest = split_low(half)
    return COEF_A * half + (dot_nn(poly, high) + dot_nn(poly, rest))


def newton_start(near_ref, far_ref, a_ref, q_ref):
    get_triangle(near_ref, a_ref, far_ref)
    rows = lax.broadcasted_iota(jnp.int32, (D, D), 0)
    columns = lax.broadcasted_iota(jnp.int32, (D, D), 1)
    gram = a_ref[...]
    trace = jnp.sum(jnp.where(rows == columns, gram, 0.0))
    inverse = 1.0 / (jnp.sqrt(jnp.full((1, 1), trace, F32)) + 1e-07)
    a = gram * (inverse * inverse)
    poly, pair = newton_poly(a, SQUARES[0])
    q_ref[...] = (jnp.where(rows == columns, COEF_A, 0.0) + poly.astype(F32)) * inverse
    a_ref[...] = newton_gram(a, pair, poly)


def newton_step(index, a_ref, q_ref, a_out, q_out):
    a, q = a_ref[...], q_ref[...]
    poly, pair = newton_poly(a, SQUARES[index])
    if index < NS_STEPS - 1:
        a_out[...] = newton_gram(a, pair, poly)
    high, rest = split_low(q)
    q_out[...] = COEF_A * q + (dot_nn(high, poly) + dot_nn(rest, poly))


def newton_kernel(near_ref, far_ref, out_ref, a_ref, q_ref):
    newton_start(near_ref, far_ref, a_ref, q_ref)
    for index in range(1, NS_STEPS):
        newton_step(index, a_ref, q_ref, a_ref, q_ref)
    put_triangle(q_ref[...], out_ref)


class Muon:
    def __init__(self, info, parts, moments, kind, left=()):
        self.info, self.kind = info, kind
        shapes = [(moment.shape, F32) for moment in moments]
        packed = ((len(triangle()) * 128, 128), F32)
        extra = [((STATE, 256), F32)] if kind == "m" else []
        outs = call(
            lambda *refs: moment_kernel(kind, *refs),
            shapes * 2 + [packed] * 2 + extra,
            (info, *parts, *moments, *left),
            scratch=[pltpu.VMEM((4 * parts[0].shape[0], D), BF)],
            smem=(0,),
            us=4.5,
        )
        self.grads, self.news, self.own, self.other, self.extra = outs[:2], outs[2:4], outs[4], outs[5], outs[6:]
        if kind != "t":
            self.got = swap_core(self.other)

    def exchange(self, *others):
        self.near = self.own + after(self.got, *others)
        self.far = swap_y(self.near)
        return (self.near,)

    def newton(self, *others):
        far = after(self.far, *others)
        (self.q,) = call(
            newton_kernel,
            [(self.near.shape, F32)],
            (self.near, far),
            scratch=[pltpu.VMEM((D, D), F32)] * 2,
            us=13.0,
        )
        return self.send()

    def arrive(self, *others):
        self.far = after(self.far, *others)
        return (self.far,)

    def send(self):
        self.factors = [self.q, swap_core(self.q)]
        if self.kind == "m":
            self.factors.append(swap_dp(self.q, 1))
        return (self.q,)

    def share(self, *others):
        self.factors[1:3] = together(self.factors[1], self.factors[2], *others)[:2]
        self.factors.append(swap_core(self.factors[2]))
        return (self.factors[2],)

    def update(self, scales, params, factors, *others):
        kind = self.kind
        news = call(
            lambda *refs: update_kernel(scales, kind, *refs),
            [(param.shape, F32) for param in params],
            (self.info, *factors[:-1], after(factors[-1], *others), *self.news, *params),
            scratch=[pltpu.VMEM((D, D), F32)],
            smem=(0,),
            us=4.5,
        )
        return [list(triple) for triple in zip(self.grads, self.news, news)]


def bit_rows(info_ref, index, half, other=False):
    bit = info_ref[2 + index]
    return pl.ds(pl.multiple_of((1 - bit if other else bit) * half, half), half)


def add_refs(one, two):
    return (one.astype(F32) + two.astype(F32)).astype(BF)


def sum_start_kernel(info_ref, mine_ref, got_ref, own_a, away_a, keep_b, send_b):
    half, rows = own_a.shape[0], mine_ref.shape[0] // 2
    own_a[...] = add_refs(mine_ref[:half, :], got_ref[:half, :])
    away_a[...] = add_refs(mine_ref[rows : rows + half, :], got_ref[rows : rows + half, :])
    quarter = half // 2
    for out, other in ((keep_b, False), (send_b, True)):
        start = bit_rows(info_ref, 0, quarter, other).start
        for k in range(2):
            here = pl.ds(pl.multiple_of(k * rows + half + start, quarter), quarter)
            out[k * quarter : (k + 1) * quarter, :] = add_refs(mine_ref[here, :], got_ref[here, :])


def sum_second_kernel(info_ref, own_a, got_a, keep_b, got_b, keep_a, send_a, own_b, away_b):
    quarter = keep_a.shape[0]
    for out, other in ((keep_a, False), (send_a, True)):
        rows = bit_rows(info_ref, 0, quarter, other)
        out[...] = add_refs(own_a[rows, :], got_a[rows, :])
    own_b[...] = add_refs(keep_b[:quarter, :], got_b[:quarter, :])
    away_b[...] = add_refs(keep_b[quarter:, :], got_b[quarter:, :])


def sum_third_kernel(info_ref, keep_a, got_a, own_b, got_b, keep, send):
    first = info_ref[3] == 0
    a = add_refs(keep_a[...], got_a[...])
    b = add_refs(own_b[...], got_b[...])

    @pl.when(first)
    def _():
        keep[...] = a
        send[...] = b

    @pl.when(jnp.logical_not(first))
    def _():
        keep[...] = b
        send[...] = a


def sum_more_kernel(index, info_ref, keep_in, got, keep, send):
    half = keep.shape[0]
    for out, other in ((keep, False), (send, True)):
        rows = bit_rows(info_ref, index, half, other)
        out[...] = add_refs(keep_in[rows, :], got[rows, :])


def sum_join_kernel(index, info_ref, own, got, out):
    half = own.shape[0]
    out[bit_rows(info_ref, index, half), :] = own[...]
    out[bit_rows(info_ref, index, half, True), :] = got[...]


class SmallSum:
    def __init__(self, values):
        self.values = values
        self.moves = [swap_core, swap_y] + [lambda v, bit=bit: swap_dp(v, bit) for bit in dp_bits()]
        self.start()

    def start(self):
        self.got = self.moves.pop(0)(self.values)

    def step(self, *others):
        if self.got is None:
            return others
        self.values = self.values + after(self.got, *others)
        self.got = None
        if self.moves:
            self.start()
        return (self.values,)


class Sum:
    def __init__(self, info, mine, got):
        self.info = info
        self.inputs = (mine, got)
        self.rows, self.width = mine.shape[0] // 2, mine.shape[1]
        self.bits = dp_bits()

    def run(self, kernel, rows, args, scratch=()):
        outs = [((count, self.width), BF) for count in rows]
        return call(kernel, outs, (self.info, *args), scratch=scratch, smem=(0,), us=0.8)

    def start(self):
        half = self.rows // 2
        self.own_a, away_a, self.keep_b, send_b = self.run(sum_start_kernel, [half] * 4, self.inputs)
        self.got = (swap_y(away_a), swap_dp(send_b, self.bits[0]))
        return (away_a,)

    def second(self, *others):
        quarter = self.rows // 4
        got_a, got_b = (after(value, *others) for value in self.got)
        self.keep_a, send_a, self.own_b, away_b = self.run(
            sum_second_kernel, [quarter] * 4, (self.own_a, got_a, self.keep_b, got_b)
        )
        self.got = (swap_dp(send_a, self.bits[0]), swap_y(away_b))
        return (send_a,)

    def third(self, *others):
        quarter = self.rows // 4
        got_a, got_b = (after(value, *others) for value in self.got)
        self.keep, send = self.run(sum_third_kernel, [quarter] * 2, (self.keep_a, got_a, self.own_b, got_b))
        self.got = swap_dp(send, self.bits[1])
        self.count = quarter
        self.index = 2
        return (send,)

    def more(self, *others):
        got = after(self.got, *others)
        if self.index < len(self.bits):
            self.count //= 2
            index = self.index
            self.keep, send = self.run(
                lambda *refs: sum_more_kernel(index, *refs), [self.count] * 2, (self.keep, got)
            )
            self.got = swap_dp(send, self.bits[index])
            self.index += 1
            return (send,)
        self.block = add_low(self.keep, got)
        self.gather_start()
        return (self.block,)

    def gather_start(self):
        self.index -= 1
        if self.index >= 2:
            self.got = swap_dp(self.block, self.bits[self.index])
        else:
            self.near = swap_dp(self.block, self.bits[1])
            self.across = swap_dp(self.block, self.bits[0])

    def gather(self, *others):
        got = after(self.got, *others)
        index = self.index
        self.count *= 2
        (self.block,) = self.run(lambda *refs: sum_join_kernel(index, *refs), [self.count], (self.block, got))
        self.gather_start()
        return (self.block,)

    def finish(self, *others):
        near, across = together(self.near, self.across, *others)[:2]
        self.parts = (self.block, near, across, swap_dp(near, self.bits[0]))
        return (near,)


def halo(low, high):
    before = lax.ppermute(high, "mp", [(i, i + 1) for i in range(N_MP - 1)])
    after = lax.ppermute(low, "mp", [(i + 1, i) for i in range(N_MP - 1)])
    return before, after


def body(
    inputs,
    segments,
    cotangent,
    inner_first,
    outer_first,
    mixer_input,
    mixer_output,
    inner_second,
    outer_second,
    norm_params,
    conv_taps,
    state_maps,
    state_rates,
    inner_first_moment,
    outer_first_moment,
    mixer_input_moment,
    mixer_output_moment,
    inner_second_moment,
    outer_second_moment,
    norm_params_moment,
    conv_taps_moment,
    state_maps_moment,
    state_rates_moment,
):
    frames = inputs.shape[0]
    padded = -(-frames // ROW_CHUNK) * ROW_CHUNK
    more = padded - frames
    me = lax.axis_index("mp")
    own_states = HEADS // N_MP * STATE
    n_states = HEADS * STATE
    wide = 256
    bits = dp_bits()
    dp = lax.axis_index("dp")
    info = jnp.stack([me, me % 2] + [(dp // bit) % 2 for bit in bits])
    x_upper = dp % 2 == 1
    unit = 16 * lax.axis_size("dp")
    pack_rows = -(-(RATES_AT + 16) // unit) * unit
    tail_rows = -(-(2 * D + TILE_AT + STATE) // unit) * unit - 2 * D

    own_one = [inner_first.astype(BF), outer_first.astype(BF)]
    y_halves = [
        swap_y(jnp.where(x_upper, value[D // 2 :], value[: D // 2])) for value in own_one
    ]
    core_one = [swap_core(value) for value in own_one]
    own_two = [inner_second.astype(BF), outer_second.astype(BF)]
    maps_tile = jnp.transpose(state_maps, (2, 1, 0, 3)).reshape(STATE, wide)
    rates_row = jnp.tile(state_rates.reshape(1, own_states), (1, N_MP))
    rates_one = rates_row.astype(BF)
    rates_rest = rates_row - rates_one.astype(F32)
    rates_two = rates_rest.astype(BF)
    rates_three = (rates_rest - rates_two.astype(F32)).astype(BF)
    rates_tile = jnp.pad(
        jnp.concatenate([rates_one, rates_two, rates_three], axis=0), ((0, pack_rows - RATES_AT - 3), (0, 0))
    )
    own_mixer = jnp.concatenate(
        [
            mixer_input.reshape(D, wide).astype(BF),
            mixer_output[:, :wide].astype(BF),
            mixer_output[:, wide:].astype(BF),
            maps_tile.astype(BF),
            rates_tile,
        ],
        axis=0,
    )
    norm_rows = norm_params.reshape(10, D)
    x = jnp.pad(inputs, ((0, more), (0, 0)))
    cot = jnp.pad(cotangent, ((0, more), (0, 0)))
    taps = jnp.pad(conv_taps, ((0, 1), (0, 0)))
    past, future, bounds = call(
        lambda info_ref, *refs: place_kernel(info_ref, frames, *refs),
        [((padded, 128), jnp.int32), ((padded, 128), jnp.int32), ((8, 128), jnp.int32)],
        (info, segments),
        smem=(0,),
    )
    y_halves[0] = after(y_halves[0], own_mixer, *own_two, norm_rows, x, past)
    y_one = []
    for half in y_halves:
        across = swap_dp(half, 1)
        y_one.append(
            jnp.concatenate([jnp.where(x_upper, across, half), jnp.where(x_upper, half, across)], axis=0)
        )
    both_one = [swap_core(value) for value in y_one]
    one_refs = []
    for group in (own_one, y_one, core_one, both_one):
        one_refs.extend(group)
    own_mixer = after(own_mixer, y_halves[1])
    half = pack_rows // 2
    mixer_half = swap_y(jnp.where(x_upper, own_mixer[half:], own_mixer[:half]))
    core_mixer = swap_core(own_mixer)
    send_half = after(jnp.where(x_upper, own_two[1], own_two[0]), own_mixer)
    two_half = swap_y(send_half)
    core_two = [swap_core(after(value, mixer_half)) for value in own_two]
    mixer_across = swap_dp(mixer_half, 1)

    frame_shape = (padded, D)
    hidden_shape = (padded, FF)
    state_shape = (padded, n_states)
    edge = ((16, D), BF)
    frame_scratch = pltpu.VMEM((padded + 32, D), F32)
    map_scratch = pltpu.VMEM((n_states, D), BF)
    out_scratch = pltpu.VMEM((D, D), BF)

    act_one, gated_one, slope_one, stream_one = call(
        first_kernel,
        [(frame_shape, BF), (hidden_shape, BF), (hidden_shape, BF), (frame_shape, F32)],
        (after(x, send_half), norm_rows, *one_refs),
        us=6.6,
    )
    mixer_across = after(mixer_across, stream_one)
    y_mixer = jnp.concatenate(
        [jnp.where(x_upper, mixer_across, mixer_half), jnp.where(x_upper, mixer_half, mixer_across)], axis=0
    )
    wm = jnp.stack([own_mixer, y_mixer, core_mixer, swap_core(y_mixer)])
    two_half = after(two_half, stream_one, y_mixer)
    two_across = swap_dp(two_half, 1)
    act_two, signal, gate, driven, states_local, final = call(
        lambda *refs: mixer_in_kernel(frames, *refs),
        [(frame_shape, BF), (frame_shape, BF), (frame_shape, F32), (state_shape, F32), (state_shape, F32), ((8, n_states), F32)],
        (info, after(stream_one, two_half), norm_rows, wm, past),
        scratch=[map_scratch],
        smem=(0,),
        us=4.2,
    )
    finals = lax.all_gather(final, "mp", axis=0, tiled=True)
    states, carry_in, result, mixed, stream_two, act_three, low, high = call(
        lambda *refs: mixer_out_kernel(frames, *refs),
        [(state_shape, F32), ((8, n_states), F32), (frame_shape, F32), (frame_shape, BF), (frame_shape, F32), (frame_shape, F32), edge, edge],
        (info, states_local, finals, past, bounds, wm, gate, stream_one, norm_rows),
        scratch=[map_scratch, out_scratch],
        smem=(0,),
        us=2.1,
    )
    act_before, act_after = halo(low, high)
    two_across = after(two_across, stream_two)
    y_two = [jnp.where(x_upper, two_across, two_half), jnp.where(x_upper, two_half, two_across)]
    both_two = [swap_core(value) for value in y_two]
    two_refs = []
    for group in (own_two, y_two, core_two, both_two):
        two_refs.extend(group)
    layer_output, act_four, gated_four, grad_pre_four, back_four, grad_three, grad_conv, low, high, norm_high = call(
        lambda *refs: second_kernel(frames, *refs),
        [
            ((frames, D), BF), (frame_shape, BF), (hidden_shape, BF), (hidden_shape, BF), (frame_shape, BF),
            (frame_shape, F32), (frame_shape, F32), edge, edge, ((32, D), F32),
        ],
        (act_three, act_before, act_after, past, future, taps, stream_two, norm_rows, *two_refs, cot),
        scratch=[frame_scratch, pltpu.VMEM(frame_shape, F32), pltpu.VMEM(hidden_shape, BF), pltpu.VMEM(frame_shape, BF)],
        us=16.6,
    )
    grad_before, grad_after = halo(low, high)
    send_two = weight_grads(2, act_four, gated_four, grad_pre_four, back_four)
    keep_two = weight_grads(0, act_four, gated_four, grad_pre_four, back_four)
    got_two = swap_core(send_two)

    grad_two, back_two, grad_result, grad_gate, adjoint, first, taps_part, norm_two = call(
        lambda *refs: conv_back_kernel(frames, *refs),
        [
            (frame_shape, F32), (frame_shape, BF), (frame_shape, BF), (frame_shape, BF), (state_shape, F32),
            ((8, n_states), F32), ((8 * KSIZE, D), F32), ((16, D), F32),
        ],
        (
            info, act_three, act_before, act_after, grad_conv, grad_before, grad_after, past, future, taps,
            after(grad_three, keep_two, send_two), stream_two, norm_rows, wm, gate, result,
        ),
        scratch=[frame_scratch, frame_scratch, pltpu.VMEM(frame_shape, F32), map_scratch, out_scratch],
        smem=(0,),
        us=11.8,
    )
    firsts = lax.all_gather(first, "mp", axis=0, tiled=True)
    sum_two = Sum(info, keep_two, after(got_two, firsts))
    started = sum_two.start()
    grad_one, keep_mixer, send_mixer, rates_part, norm_one = call(
        lambda *refs: mixer_back_kernel(frames, *refs),
        [(frame_shape, F32), ((2 * tail_rows, D), BF), ((2 * tail_rows, D), BF), ((8, n_states), F32), ((16, D), F32)],
        (
            info, adjoint, firsts, past, future, bounds, states, carry_in, driven, wm, signal, grad_gate,
            act_two, stream_one, norm_rows, after(grad_two, *started), mixed, back_two, grad_result,
        ),
        scratch=[
            pltpu.VMEM(state_shape, BF), map_scratch, pltpu.VMEM(frame_shape, BF), pltpu.VMEM((N_MP, tail_rows, D), BF)
        ],
        smem=(0,),
        us=5.5,
    )
    got_mixer = swap_core(send_mixer)
    extra_bits = len(bits) - 2
    wide_shape = mixer_input.shape
    first_scale = 0.5 * math.sqrt(max(D, FF) / D)
    second_scale = 0.5 * math.sqrt(max(D, FF) / FF)
    made = {}

    def first_back(*others):
        made["pre"], made["back"], made["act"] = call(
            first_back_kernel,
            [(hidden_shape, BF), (frame_shape, BF), (frame_shape, F32)],
            (after(grad_one, *others), slope_one, *one_refs),
            us=5.4,
        )
        return (made["back"],)

    def first_send(*others):
        made["send"] = weight_grads(2, act_one, gated_one, made["pre"], after(made["back"], *others))
        made["got"] = swap_core(made["send"])
        return (made["send"],)

    def first_keep(*others):
        made["keep"] = weight_grads(0, act_one, gated_one, made["pre"], after(made["back"], *others))
        return (made["keep"],)

    def first_start(*others):
        made["o"] = Sum(info, made["keep"], after(made["got"], *others))
        return made["o"].start()

    def mixer_start(*others):
        made["m"] = Sum(info, keep_mixer, after(got_mixer, *others))
        return made["m"].start()

    made["t"] = sum_two

    def steps_of(chain, moments, scales, params):
        def step(name):
            return lambda *others: getattr(made[chain], name)(*others)

        def several(name):
            def run(*others):
                for _ in range(extra_bits - 1):
                    others = getattr(made[chain], name)(*others)
                return getattr(made[chain], name)(*others)

            return run

        def moment(*others):
            parts = tuple(after(v, *others) for v in made[chain].parts)
            left = (made["tx"].own, made["tx"].other) if chain == "m" else ()
            made[chain + "x"] = Muon(info, parts, moments, chain, left)
            return (made[chain + "x"].own,)

        def muon(name):
            return lambda *others: getattr(made[chain + "x"], name)(*others)

        def update(*others):
            factors = made["ox" if chain == "o" else "mx"].factors
            made[chain + "r"] = made[chain + "x"].update(scales, params, factors, *others)
            return (made[chain + "r"][0][2],)

        head = [
            step("second"), step("third"), several("more"), step("more"), several("gather"), step("finish"), moment
        ]
        middle = {"t": [], "o": ["exchange", "newton"], "m": ["exchange", "arrive", "newton", "share"]}[chain]
        return head + [muon(name) for name in middle] + [update]

    def input_step(*others):
        input_grad, small = call(
            lambda *refs: input_grad_kernel(frames, *refs),
            [((frames, D), F32), ((32, D), F32)],
            (x, after(made["act"], *others), norm_rows, grad_one, norm_one, norm_two, norm_high, taps_part, rates_part),
            scratch=[pltpu.VMEM(frame_shape, F32), pltpu.VMEM((16, D), F32)],
            us=2.4,
        )
        made["input_grad"], made["s"] = input_grad, SmallSum(small)
        return (small,)

    def small_step(*others):
        return made["s"].step(*others)

    def small_last(*others):
        while made["s"].got is not None:
            others = made["s"].step(*others)
        return others

    def small_params(*others):
        small = after(made["s"].values, *others)
        mixer = made["mx"]
        norm_sum = small[:10].reshape(norm_params.shape)
        taps_sum = small[10 : 10 + KSIZE]
        rates_sum = lax.dynamic_slice_in_dim(small[10 + KSIZE], me * own_states, own_states, 0).reshape(state_rates.shape)
        maps_sum = jnp.transpose(mixer.extra[0].reshape(STATE, 2, HEADS // N_MP, HD), (2, 1, 0, 3))
        tokens_all = frames * lax.axis_size("dp") * lax.axis_size("mp")
        small_results = []
        for factor, grad, moment, param in (
            (SMALL_FACTORS[0], norm_sum, norm_params_moment, norm_params),
            (SMALL_FACTORS[1], taps_sum, conv_taps_moment, conv_taps),
            (SMALL_FACTORS[2], maps_sum, state_maps_moment, state_maps),
            (SMALL_FACTORS[3], rates_sum, state_rates_moment, state_rates),
        ):
            moment_new = 0.5 * moment + grad
            small_results.extend((grad, moment_new, param - factor / math.sqrt(tokens_all) * moment_new))
        made["small"] = small_results
        made["in"] = [values[1].reshape(wide_shape) for values in (mixer.grads, mixer.news)]
        return (*small_results, *made["in"])

    chains = {
        "t": steps_of("t", (outer_second_moment, inner_second_moment), (second_scale, first_scale), (outer_second, inner_second)),
        "m": [mixer_start]
        + steps_of(
            "m", (mixer_output_moment, mixer_input_moment.reshape(D, wide)), (0.5, 0.5 * math.sqrt(2.0)),
            (mixer_output, mixer_input.reshape(D, wide)),
        ),
        "o": [first_back, first_send, first_keep, first_start]
        + steps_of("o", (outer_first_moment, inner_first_moment), (second_scale, first_scale), (outer_first, inner_first)),
        "s": [input_step] + [small_step] * 4 + [small_last],
        "p": [small_params],
    }
    started = (grad_one,)
    for name in ORDER:
        started = chains[name].pop(0)(*started)
    input_grad, small_results = made["input_grad"], made["small"]
    down_two, up_two = made["tr"]
    down_one, up_one = made["or"]
    out_triple, in_triple = made["mr"]
    in_triple = [*made["in"], in_triple[2].reshape(wide_shape)]
    results = [layer_output, input_grad]
    for triple in (up_one, down_one, in_triple, out_triple, up_two, down_two):
        results.extend(triple)
    results.extend(small_results)
    return tuple(results)


def solution(mesh):
    in_specs = (
        P(("dp", "mp"), None),
        P("dp", None),
        P(("dp", "mp"), None),
        P(None, "mp"),
        P("mp", None),
        P(None, None, "mp"),
        P("mp", None),
        P(None, "mp"),
        P("mp", None),
        P(),
        P(),
        P("mp", None, None, None),
        P("mp", None),
        P(None, "mp"),
        P("mp", None),
        P(None, None, "mp"),
        P("mp", None),
        P(None, "mp"),
        P("mp", None),
        P(),
        P(),
        P("mp", None, None, None),
        P("mp", None),
    )
    out_specs = (
        P(("dp", "mp"), None),
        P(("dp", "mp"), None),
        P(None, "mp"),
        P(None, "mp"),
        P(None, "mp"),
        P("mp", None),
        P("mp", None),
        P("mp", None),
        P(None, None, "mp"),
        P(None, None, "mp"),
        P(None, None, "mp"),
        P("mp", None),
        P("mp", None),
        P("mp", None),
        P(None, "mp"),
        P(None, "mp"),
        P(None, "mp"),
        P("mp", None),
        P("mp", None),
        P("mp", None),
        P(),
        P(),
        P(),
        P(),
        P(),
        P(),
        P("mp", None, None, None),
        P("mp", None, None, None),
        P("mp", None, None, None),
        P("mp", None),
        P("mp", None),
        P("mp", None),
    )
    return jax.shard_map(body, mesh=mesh, in_specs=in_specs, out_specs=out_specs, check_vma=False)
```

```python
import math

import jax
import jax.numpy as jnp
from jax import lax
from jax.experimental import pallas as pl
from jax.experimental.pallas import tpu as pltpu
from jax.sharding import PartitionSpec as P

D = 512
FF = 2048
HEADS = 8
STATE = 32
HD = 64
KSIZE = 15
MARGIN = (KSIZE - 1) // 2
NS_STEPS = 5
N_MP = 4
BF = jnp.bfloat16
F32 = jnp.float32

COEF_A = 3.4445
COEF_B = -4.775
COEF_C = 2.0315
NORM_EPS = 1e-05
SMALL_FACTORS = (0.2, 0.2, 0.2, 4.0)
VMEM_LIMIT = 24 * 1024 * 1024
ROW_CHUNK = 320
CONV_CHUNK = 64
MAPS_AT = D + 256
RATES_AT = MAPS_AT + STATE
SEGS = 6
SQUARES = (1, 3, 3, 3, 3)
ORDER = "otomtoomstomstomtostmsotmsommmsomoomopmotm"
OUT_AT = 256
TILE_AT = OUT_AT + 128
FLOPS_PER_US = 1.0e9


def dot(left, right, dims):
    return lax.dot_general(left, right, ((dims[0], dims[1]), ((), ())), preferred_element_type=F32)


def dot_nn(left, right):
    return dot(left, right, ((1,), (0,)))


def dot_tn(left, right):
    return dot(left, right, ((0,), (0,)))


def dot_nt(left, right):
    return dot(left, right, ((1,), (1,)))


def split_low(values):
    high = values.astype(BF)
    return high, (values - high.astype(F32)).astype(BF)


def dot3(left, right, kind):
    lh, ll = left
    rh, rl = right
    return kind(lh, rh) + (kind(lh, rl) + kind(ll, rh))


def swap_core(values):
    return lax.ppermute(values, "mp", [(i, i ^ 1) for i in range(N_MP)])


def swap_y(values):
    return lax.ppermute(values, "mp", [(i, i ^ 2) for i in range(N_MP)])


def swap_dp(values, bit):
    count = lax.axis_size("dp")
    return lax.ppermute(values, "dp", [(i, i ^ bit) for i in range(count)])


def dp_bits():
    count = lax.axis_size("dp")
    bits = []
    bit = 1
    while bit < count:
        bits.append(bit)
        bit *= 2
    return bits


def add_low(left, right):
    return (left.astype(F32) + right.astype(F32)).astype(BF)


def swish_parts(values):
    gate = 0.5 * jnp.tanh(0.5 * values) + 0.5
    active = values * gate
    return active, gate + active * (1.0 - gate)


def normed(values):
    middle = jnp.mean(values, axis=-1, keepdims=True)
    centred = values - middle
    spread = jnp.mean(centred * centred, axis=-1, keepdims=True)
    scale = lax.rsqrt(spread + NORM_EPS)
    return centred * scale, scale


def norm_forward(values, norm_ref, index):
    unit, _ = normed(values)
    return unit * norm_ref[2 * index : 2 * index + 1, :] + norm_ref[2 * index + 1 : 2 * index + 2, :]


def fold(values):
    return jnp.sum(values.reshape(values.shape[0] // 8, 8, values.shape[1]), axis=0)


def norm_backward(values, grad, norm_ref, index):
    unit, scale = normed(values)
    wide = grad * norm_ref[2 * index : 2 * index + 1, :]
    mean_one = jnp.mean(wide, axis=-1, keepdims=True)
    mean_two = jnp.mean(wide * unit, axis=-1, keepdims=True)
    return scale * (wide - mean_one - unit * mean_two), fold(grad * unit), fold(grad)


def for_rows(total, size, fn):
    def step(index, carry):
        fn(pl.ds(pl.multiple_of(index * size, size), size))
        return carry

    lax.fori_loop(0, total // size, step, 0)


def lanes(column, width):
    return jnp.concatenate([column] * (width // 128), axis=1)


def after(value, *others):
    return lax.optimization_barrier((value, *others))[0]


def together(*values):
    return lax.optimization_barrier(values)


def call(kernel, outs, args, scratch=(), smem=(), us=1.0):
    in_specs = [pl.BlockSpec(memory_space=pltpu.SMEM if i in smem else pltpu.VMEM) for i in range(len(args))]
    return pl.pallas_call(
        kernel,
        out_shape=tuple(jax.ShapeDtypeStruct(shape, dtype) for shape, dtype in outs),
        in_specs=in_specs,
        out_specs=tuple(pl.BlockSpec(memory_space=pltpu.VMEM) for _ in outs),
        scratch_shapes=list(scratch),
        compiler_params=pltpu.CompilerParams(vmem_limit_bytes=VMEM_LIMIT),
        cost_estimate=pl.CostEstimate(flops=int(us * FLOPS_PER_US), bytes_accessed=1 << 16, transcendentals=0),
    )(*args)


def block_place(block, me):
    mask = block ^ me
    return (mask & 1) * 2 + (mask >> 1)


def first_kernel(x_ref, norm_ref, u0, d0, u1, d1, u2, d2, u3, d3, act_ref, gated_ref, slope_ref, stream_ref):
    def chunk(rows):
        x = x_ref[rows, :].astype(F32)
        act = norm_forward(x, norm_ref, 0).astype(BF)
        act_ref[rows, :] = act
        total = jnp.zeros(x.shape, F32)
        for k, (up, down) in enumerate(((u0, d0), (u1, d1), (u2, d2), (u3, d3))):
            active, slope = swish_parts(dot_nn(act, up[...]))
            active = active.astype(BF)
            gated_ref[rows, k * D : (k + 1) * D] = active
            slope_ref[rows, k * D : (k + 1) * D] = slope.astype(BF)
            total = total + dot_nn(active, down[...])
        stream_ref[rows, :] = x + 0.5 * total

    for_rows(x_ref.shape[0], ROW_CHUNK, chunk)


def fill_maps(me, wm_ref, map_ref, side):
    map_ref[...] = jnp.zeros(map_ref.shape, BF)
    lane = lax.broadcasted_iota(jnp.int32, (STATE, 128), 1)
    for block in range(N_MP):
        tile = wm_ref[block_place(block, me), MAPS_AT : MAPS_AT + STATE, side * 128 : (side + 1) * 128]
        for j in range(2):
            head = 2 * block + j
            keep = jnp.where((lane >= HD) == (j == 1), tile.astype(F32), 0.0)
            map_ref[head * STATE : (head + 1) * STATE, block * 128 : (block + 1) * 128] = keep.astype(BF)


def rates_of(me, wm_ref):
    lane = lax.broadcasted_iota(jnp.int32, (1, HEADS * STATE), 1)
    own_states = HEADS // N_MP * STATE
    total = jnp.zeros((1, HEADS * STATE), F32)
    for block in range(N_MP):
        parts = wm_ref[block_place(block, me), RATES_AT : RATES_AT + 16, :].astype(F32)
        here = (lane >= block * own_states) & (lane < (block + 1) * own_states)
        total = jnp.where(here, parts[0:1] + parts[1:2] + parts[2:3], total)
    rate = jnp.exp(total)
    decays = jnp.exp(-rate)
    return rate, decays, jnp.sqrt(1.0 - decays * decays)


def no_start(bounds_ref, low, high):
    free = jnp.ones((1, 1), F32)
    for v in range(SEGS - 1):
        bound = bounds_ref[v : v + 1, :1]
        free = jnp.where((bound >= low) & (bound <= high), 0.0, free)
    return free


def place_kernel(info_ref, frames, segments_ref, past_ref, future_ref, bounds_ref):
    row = segments_ref[...]
    length = row.shape[1]
    frame = lax.broadcasted_iota(jnp.int32, past_ref.shape, 0)
    real = frame < frames
    frame = frame + info_ref[0] * frames
    begin = jnp.zeros(past_ref.shape, jnp.int32)
    end = jnp.full(past_ref.shape, length, jnp.int32)
    bounds_ref[...] = jnp.zeros(bounds_ref.shape, jnp.int32)
    for v in range(1, SEGS):
        bound = jnp.sum((row < v).astype(F32), axis=1, keepdims=True).astype(jnp.int32)
        bounds_ref[v - 1 : v, :] = jnp.broadcast_to(bound, (1, 128))
        begin = jnp.where(bound <= frame, jnp.maximum(begin, bound), begin)
        end = jnp.where(bound > frame, jnp.minimum(end, bound), end)
    past_ref[...] = jnp.where(real, frame - begin, -1)
    future_ref[...] = jnp.where(real, end - 1 - frame, -1)


def scan_steps(states_ref, reach, rate, backward):
    frames = states_ref.shape[0]
    wide = lanes(reach, states_ref.shape[1])
    states = states_ref[...]
    step = 1
    while step < frames:
        moved = pltpu.roll(states, frames - step if backward else step, 0)
        factor = jnp.exp(-float(step) * rate)
        states = states + jnp.where(wide >= step, moved * factor, 0.0)
        step *= 2
    states_ref[...] = states


def mixer_in_kernel(
    frames, info_ref, stream_ref, norm_ref, wm_ref, past_ref,
    act_ref, signal_ref, gate_ref, driven_ref, states_ref, final_ref, map_ref,
):
    me = info_ref[0]
    rate, _, gain = rates_of(me, wm_ref)
    fill_maps(me, wm_ref, map_ref, 0)

    def chunk(rows):
        act = norm_forward(stream_ref[rows, :], norm_ref, 1).astype(BF)
        act_ref[rows, :] = act
        for block in range(N_MP):
            both = dot_nn(act, wm_ref[block_place(block, me), :D, :])
            signal_ref[rows, block * 128 : (block + 1) * 128] = both[:, :128].astype(BF)
            gate_ref[rows, block * 128 : (block + 1) * 128] = both[:, 128:]
        driven = dot_nt(signal_ref[rows, :], map_ref[...]) * gain
        driven_ref[rows, :] = driven
        states_ref[rows, :] = driven

    for_rows(stream_ref.shape[0], ROW_CHUNK, chunk)
    local = lax.broadcasted_iota(jnp.int32, past_ref.shape, 0)
    scan_steps(states_ref, jnp.minimum(past_ref[...], local), rate, False)
    final_ref[...] = states_ref[frames - 8 : frames, :]


def fill_out(me, wm_ref, out_ref):
    for block in range(N_MP):
        for half in range(2):
            out_ref[block * 128 : (block + 1) * 128, half * 256 : (half + 1) * 256] = wm_ref[
                block_place(block, me), D + half * 128 : D + (half + 1) * 128, :
            ]


def mixer_out_kernel(
    frames, info_ref, states_in_ref, finals_ref, past_ref, bounds_ref, wm_ref, gate_ref, stream_ref, norm_ref,
    states_ref, carry_ref, result_ref, mixed_ref, stream_two_ref, act_ref, low_ref, high_ref, map_ref, out_ref,
):
    me = info_ref[0]
    fill_maps(me, wm_ref, map_ref, 1)
    fill_out(me, wm_ref, out_ref)
    rate, _, _ = rates_of(me, wm_ref)
    across = jnp.exp(-float(frames) * rate)
    carry = jnp.zeros(rate.shape, F32)
    mine = carry
    for k in range(N_MP):
        mine = jnp.where(me == k, carry, mine)
        whole = no_start(bounds_ref, k * frames, (k + 1) * frames - 1)
        carry = finals_ref[8 * k + 7 : 8 * k + 8, :] + whole * across * carry
    carry_ref[...] = jnp.broadcast_to(mine, carry_ref.shape)

    def chunk(rows):
        past = past_ref[rows, :]
        local = lax.broadcasted_iota(jnp.int32, past.shape, 0) + rows.start
        reach = lanes(jnp.where(past > local, local + 1, 0).astype(F32), rate.shape[1])
        states = states_in_ref[rows, :] + jnp.where(reach > 0.0, jnp.exp(-rate * reach) * mine, 0.0)
        states_ref[rows, :] = states
        result = dot_nn(states.astype(BF), map_ref[...])
        result_ref[rows, :] = result
        mixed = (result * swish_parts(gate_ref[rows, :])[0]).astype(BF)
        mixed_ref[rows, :] = mixed
        stream = stream_ref[rows, :] + dot_nn(mixed, out_ref[...])
        stream_two_ref[rows, :] = stream
        act_ref[rows, :] = norm_forward(stream, norm_ref, 2).astype(BF).astype(F32)

    for_rows(stream_ref.shape[0], ROW_CHUNK, chunk)
    low_ref[...] = act_ref[:16, :].astype(BF)
    high_ref[...] = act_ref[frames - 16 : frames, :].astype(BF)


def fill_frame(frames, frame_ref, own_ref, before_ref, after_ref):
    frame_ref[:8, :] = before_ref[8:, :].astype(F32)
    frame_ref[8 : 8 + frames, :] = own_ref[:frames, :]
    frame_ref[8 + frames : 24 + frames, :] = after_ref[...].astype(F32)


def open_taps(past, future, offset):
    shift = offset - MARGIN
    return past >= -shift if shift < 0 else future >= shift


def conv_rows(frame_ref, taps_ref, past_ref, future_ref, start, flip):
    rows = pl.ds(start, CONV_CHUNK)
    past, future = past_ref[rows, :], future_ref[rows, :]
    total = jnp.zeros((CONV_CHUNK, D), F32)
    block = frame_ref[pl.ds(start, CONV_CHUNK + 16), :]
    for offset in range(KSIZE):
        tap = KSIZE - 1 - offset if flip else offset
        here = block[offset + 1 : offset + 1 + CONV_CHUNK, :]
        term = here * taps_ref[tap : tap + 1, :]
        if offset != MARGIN:
            term = jnp.where(lanes(open_taps(past, future, offset), D), term, 0.0)
        total = total + term
    if flip:
        total = jnp.where(lanes(past >= 0, D), total, 0.0)
    return total


def second_kernel(
    frames, act_three_ref, before_ref, after_ref, past_ref, future_ref, taps_ref, stream_two_ref, norm_ref,
    u0, d0, u1, d1, u2, d2, u3, d3, cot_ref,
    output_ref, act_ref, gated_ref, grad_pre_ref, back_ref, grad_three_ref, grad_conv_ref, low_ref, high_ref, norm_grad_ref,
    frame_ref, pre_ref, slope_ref, out_ref,
):
    fill_frame(frames, frame_ref, act_three_ref, before_ref, after_ref)
    norm_grad_ref[...] = jnp.zeros(norm_grad_ref.shape, F32)
    weights = ((u0, d0), (u1, d1), (u2, d2), (u3, d3))

    def conv(index, carry):
        start = pl.multiple_of(index * CONV_CHUNK, CONV_CHUNK)
        pre_ref[pl.ds(start, CONV_CHUNK), :] = conv_rows(frame_ref, taps_ref, past_ref, future_ref, start, False)
        return carry

    lax.fori_loop(0, pre_ref.shape[0] // CONV_CHUNK, conv, 0)

    def chunk(rows):
        active, conv_slope = swish_parts(pre_ref[rows, :])
        stream_three = stream_two_ref[rows, :] + active
        act = norm_forward(stream_three, norm_ref, 3).astype(BF)
        act_ref[rows, :] = act
        total = jnp.zeros(active.shape, F32)
        for k, (up, down) in enumerate(weights):
            hidden, slope = swish_parts(dot_nn(act, up[...]))
            hidden = hidden.astype(BF)
            gated_ref[rows, k * D : (k + 1) * D] = hidden
            slope_ref[rows, k * D : (k + 1) * D] = slope.astype(BF)
            total = total + dot_nn(hidden, down[...])
        stream_four = stream_three + 0.5 * total
        out_ref[rows, :] = norm_forward(stream_four, norm_ref, 4).astype(BF)
        grad_four, gain, bias = norm_backward(stream_four, cot_ref[rows, :].astype(F32), norm_ref, 4)
        norm_grad_ref[16:24, :] += gain
        norm_grad_ref[24:32, :] += bias
        back = (0.5 * grad_four).astype(BF)
        back_ref[rows, :] = back
        grad_act = jnp.zeros(active.shape, F32)
        for k, (up, down) in enumerate(weights):
            grad_gated = dot_nt(back, down[...])
            grad_pre = (grad_gated * slope_ref[rows, k * D : (k + 1) * D].astype(F32)).astype(BF)
            grad_pre_ref[rows, k * D : (k + 1) * D] = grad_pre
            grad_act = grad_act + dot_nt(grad_pre, up[...])
        grad_part, gain, bias = norm_backward(stream_three, grad_act, norm_ref, 3)
        norm_grad_ref[:8, :] += gain
        norm_grad_ref[8:16, :] += bias
        grad_three = grad_four + grad_part
        grad_three_ref[rows, :] = grad_three
        grad_conv_ref[rows, :] = (grad_three * conv_slope).astype(BF).astype(F32)

    for_rows(pre_ref.shape[0], ROW_CHUNK, chunk)
    output_ref[...] = out_ref[:frames, :]
    low_ref[...] = grad_conv_ref[:16, :].astype(BF)
    high_ref[...] = grad_conv_ref[frames - 16 : frames, :].astype(BF)


def weight_grad_kernel(first, act_ref, gated_ref, grad_pre_ref, back_ref, out_ref):
    for k in range(2):
        columns = slice((first + k) * D, (first + k + 1) * D)
        out_ref[2 * k * D : (2 * k + 1) * D, :] = dot_tn(act_ref[...], grad_pre_ref[:, columns]).astype(BF)
        out_ref[(2 * k + 1) * D : (2 * k + 2) * D, :] = dot_tn(gated_ref[:, columns], back_ref[...]).astype(BF)


def weight_grads(first, act, gated, grad_pre, back):
    return call(
        lambda *refs: weight_grad_kernel(first, *refs), [((4 * D, D), BF)], (act, gated, grad_pre, back), us=2.0
    )[0]


def conv_back_kernel(
    frames, info_ref, act_three_ref, act_before_ref, act_after_ref, grad_conv_ref, before_ref, after_ref,
    past_ref, future_ref, taps_ref, grad_three_ref, stream_two_ref, norm_ref, wm_ref, gate_ref, result_ref,
    grad_two_ref, back_ref, grad_result_ref, grad_gate_ref, adjoint_ref, first_ref, taps_grad_ref, norm_grad_ref,
    act_frame_ref, frame_ref, grad_act_ref, map_ref, out_ref,
):
    me = info_ref[0]
    fill_frame(frames, act_frame_ref, act_three_ref, act_before_ref, act_after_ref)
    fill_frame(frames, frame_ref, grad_conv_ref, before_ref, after_ref)
    fill_maps(me, wm_ref, map_ref, 1)
    fill_out(me, wm_ref, out_ref)
    taps_grad_ref[...] = jnp.zeros(taps_grad_ref.shape, F32)
    norm_grad_ref[...] = jnp.zeros(norm_grad_ref.shape, F32)

    def conv(index, carry):
        start = pl.multiple_of(index * CONV_CHUNK, CONV_CHUNK)
        rows = pl.ds(start, CONV_CHUNK)
        grad_act_ref[rows, :] = conv_rows(frame_ref, taps_ref, past_ref, future_ref, start, True)
        past, future = past_ref[rows, :], future_ref[rows, :]
        block = act_frame_ref[pl.ds(start, CONV_CHUNK + 16), :]
        grad = grad_conv_ref[rows, :]
        for offset in range(KSIZE):
            term = grad * block[offset + 1 : offset + 1 + CONV_CHUNK, :]
            if offset != MARGIN:
                term = jnp.where(lanes(open_taps(past, future, offset), D), term, 0.0)
            taps_grad_ref[8 * offset : 8 * offset + 8, :] += fold(term)
        return carry

    lax.fori_loop(0, grad_act_ref.shape[0] // CONV_CHUNK, conv, 0)

    def chunk(rows):
        grad_part, gain, bias = norm_backward(stream_two_ref[rows, :], grad_act_ref[rows, :], norm_ref, 2)
        norm_grad_ref[:8, :] += gain
        norm_grad_ref[8:16, :] += bias
        grad_two = grad_three_ref[rows, :] + grad_part
        grad_two_ref[rows, :] = grad_two
        back = grad_two.astype(BF)
        back_ref[rows, :] = back
        grad_mixed = dot_nt(back, out_ref[...])
        active, slope = swish_parts(gate_ref[rows, :])
        grad_result = (grad_mixed * active).astype(BF)
        grad_result_ref[rows, :] = grad_result
        grad_gate_ref[rows, :] = (grad_mixed * result_ref[rows, :] * slope).astype(BF)
        adjoint_ref[rows, :] = dot_nt(grad_result, map_ref[...])

    for_rows(grad_act_ref.shape[0], ROW_CHUNK, chunk)
    local = lax.broadcasted_iota(jnp.int32, future_ref.shape, 0)
    reach = jnp.where(local < frames, jnp.minimum(future_ref[...], frames - 1 - local), 0)
    scan_steps(adjoint_ref, reach, rates_of(me, wm_ref)[0], True)
    first_ref[...] = adjoint_ref[:8, :]


def mixer_back_kernel(
    frames, info_ref, adjoint_in_ref, firsts_ref, past_ref, future_ref, bounds_ref, states_ref, carry_ref,
    driven_ref, wm_ref, signal_ref, grad_gate_ref, act_ref, stream_ref, norm_ref, grad_two_ref,
    mixed_ref, back_ref, grad_result_ref,
    grad_one_ref, keep_ref, send_ref, rates_ref, norm_grad_ref, low_ref, map_ref, grad_signal_ref, pack_ref,
):
    me = info_ref[0]
    rate, decays, gain = rates_of(me, wm_ref)
    fill_maps(me, wm_ref, map_ref, 0)
    norm_grad_ref[...] = jnp.zeros(norm_grad_ref.shape, F32)
    low_ref[...] = states_ref[...].astype(BF)
    out_grad = dot_tn(mixed_ref[...], back_ref[...])
    maps_out = dot_tn(low_ref[...], grad_result_ref[...])
    across = jnp.exp(-float(frames) * rate)
    carry = jnp.zeros(rate.shape, F32)
    mine = carry
    for k in reversed(range(N_MP)):
        mine = jnp.where(me == k, carry, mine)
        whole = no_start(bounds_ref, k * frames + 1, (k + 1) * frames) if k + 1 < N_MP else 0.0
        carry = firsts_ref[8 * k : 8 * k + 1, :] + whole * across * carry
    rows_all = adjoint_in_ref.shape[0]
    local = lax.broadcasted_iota(jnp.int32, future_ref.shape, 0)
    reach = jnp.where((local < frames) & (future_ref[...] > frames - 1 - local), frames - local, 0).astype(F32)
    reach = lanes(reach, rate.shape[1])
    adjoint = adjoint_in_ref[...] + jnp.where(reach > 0.0, jnp.exp(-rate * reach) * mine, 0.0)
    low_ref[...] = (adjoint * gain).astype(BF)
    earlier = pltpu.roll(states_ref[...], 1, 0)
    place = lax.broadcasted_iota(jnp.int32, earlier.shape, 0)
    earlier = jnp.where(place == 0, carry_ref[:1, :], earlier)
    open_past = lanes(past_ref[...], rate.shape[1]) >= 1
    decay_grad = jnp.sum(jnp.where(open_past, earlier * adjoint, 0.0), axis=0, keepdims=True)
    gain_grad = jnp.sum(adjoint * driven_ref[...], axis=0, keepdims=True) / gain
    decay_grad = decay_grad - gain_grad * decays / gain
    rates_ref[...] = jnp.broadcast_to(decay_grad * decays * -rate, rates_ref.shape)
    maps = dot_tn(low_ref[...], signal_ref[...])
    lane = lax.broadcasted_iota(jnp.int32, (STATE, 128), 1)
    for block in range(N_MP):
        place_k = block_place(block, me)
        columns = slice(block * 128, (block + 1) * 128)
        pack_ref[place_k, OUT_AT:TILE_AT, :] = out_grad[columns, :].astype(BF)
        pack_ref[place_k, TILE_AT:, :] = jnp.zeros((pack_ref.shape[1] - TILE_AT, D), BF)
        for side, grads in enumerate((maps, maps_out)):
            one = grads[2 * block * STATE : (2 * block + 1) * STATE, columns]
            two = grads[(2 * block + 1) * STATE : (2 * block + 2) * STATE, columns]
            pack_ref[place_k, TILE_AT : TILE_AT + STATE, side * 128 : (side + 1) * 128] = jnp.where(lane < HD, one, two).astype(BF)

    def chunk(rows):
        grad_signal_ref[rows, :] = dot_nn(low_ref[rows, :], map_ref[...]).astype(BF)
        grad_act = jnp.zeros((ROW_CHUNK, D), F32)
        for block in range(N_MP):
            columns = slice(block * 128, (block + 1) * 128)
            both = jnp.concatenate([grad_signal_ref[rows, columns], grad_gate_ref[rows, columns]], axis=1)
            grad_act = grad_act + dot_nt(both, wm_ref[block_place(block, me), :D, :])
        grad_part, gain_sum, bias_sum = norm_backward(stream_ref[rows, :], grad_act, norm_ref, 1)
        norm_grad_ref[:8, :] += gain_sum
        norm_grad_ref[8:16, :] += bias_sum
        grad_one_ref[rows, :] = grad_two_ref[rows, :] + grad_part

    for_rows(rows_all, ROW_CHUNK, chunk)
    for block in range(N_MP):
        columns = slice(block * 128, (block + 1) * 128)
        both = jnp.concatenate([grad_signal_ref[:, columns], grad_gate_ref[:, columns]], axis=1)
        grad = dot_tn(act_ref[...], both).astype(BF)
        for half in range(2):
            pack_ref[block_place(block, me), :OUT_AT, half * 256 : (half + 1) * 256] = grad[half * 256 : (half + 1) * 256, :]
    rows = pack_ref.shape[1]
    for k in range(2):
        keep_ref[k * rows : (k + 1) * rows, :] = pack_ref[k]
        send_ref[k * rows : (k + 1) * rows, :] = pack_ref[2 + k]


def first_back_kernel(grad_one_ref, slope_ref, u0, d0, u1, d1, u2, d2, u3, d3, grad_pre_ref, back_ref, grad_act_ref):
    def chunk(rows):
        back = (0.5 * grad_one_ref[rows, :]).astype(BF)
        back_ref[rows, :] = back
        grad_act = jnp.zeros((ROW_CHUNK, D), F32)
        for k, (up, down) in enumerate(((u0, d0), (u1, d1), (u2, d2), (u3, d3))):
            grad_gated = dot_nt(back, down[...])
            grad_pre = (grad_gated * slope_ref[rows, k * D : (k + 1) * D].astype(F32)).astype(BF)
            grad_pre_ref[rows, k * D : (k + 1) * D] = grad_pre
            grad_act = grad_act + dot_nt(grad_pre, up[...])
        grad_act_ref[rows, :] = grad_act

    for_rows(grad_one_ref.shape[0], ROW_CHUNK, chunk)


def input_grad_kernel(
    frames, x_ref, grad_act_ref, norm_ref, grad_one_ref, norm_one_ref, norm_two_ref, norm_high_ref, taps_ref, rates_ref,
    grad_ref, small_ref, sum_ref, norm_grad_ref,
):
    norm_grad_ref[...] = jnp.zeros(norm_grad_ref.shape, F32)

    def chunk(rows):
        grad_part, gain, bias = norm_backward(x_ref[rows, :].astype(F32), grad_act_ref[rows, :], norm_ref, 0)
        norm_grad_ref[:8, :] += gain
        norm_grad_ref[8:16, :] += bias
        sum_ref[rows, :] = grad_one_ref[rows, :] + grad_part

    for_rows(x_ref.shape[0], ROW_CHUNK, chunk)
    grad_ref[...] = sum_ref[:frames, :]
    small_ref[...] = jnp.zeros(small_ref.shape, F32)
    row = 0
    for ref in (norm_grad_ref, norm_one_ref, norm_two_ref, norm_high_ref, taps_ref):
        for part in range(ref.shape[0] // 8):
            small_ref[row : row + 1, :] = jnp.sum(ref[8 * part : 8 * part + 8, :], axis=0, keepdims=True)
            row += 1
    small_ref[row : row + 1, : HEADS * STATE] = rates_ref[:1, :]


def triangle():
    count = D // 128
    return [(i, j) for i in range(count) for j in range(i, count)]


def put_triangle(matrix, out_ref):
    for k, (i, j) in enumerate(triangle()):
        out_ref[k * 128 : (k + 1) * 128, :] = matrix[i * 128 : (i + 1) * 128, j * 128 : (j + 1) * 128]


def get_triangle(ref, out_ref, more_ref=None):
    for k, (i, j) in enumerate(triangle()):
        block = ref[k * 128 : (k + 1) * 128, :]
        if more_ref is not None:
            block = block + more_ref[k * 128 : (k + 1) * 128, :]
        out_ref[i * 128 : (i + 1) * 128, j * 128 : (j + 1) * 128] = block
        if i != j:
            out_ref[j * 128 : (j + 1) * 128, i * 128 : (i + 1) * 128] = block.T


def fill_block(info_ref, part_refs, block_ref):
    x, z = info_ref[2], info_ref[3]
    part = part_refs[0].shape[0]
    for ref, side, half in zip(part_refs, (z, 1 - z, z, 1 - z), (x, x, 1 - x, 1 - x)):
        block_ref[pl.ds(pl.multiple_of(side * 2 * part + half * part, part), part), :] = ref[...]


def put_grams(info_ref, pair, own_ref, other_ref):
    first_pair, second_pair = split_low(pair[0]), split_low(pair[1])
    gram_first = dot3(first_pair, first_pair, dot_tn)
    gram_second = dot3(second_pair, second_pair, dot_nt)
    is_zero = info_ref[1] == 0

    @pl.when(is_zero)
    def _():
        put_triangle(gram_first, own_ref)
        put_triangle(gram_second, other_ref)

    @pl.when(jnp.logical_not(is_zero))
    def _():
        put_triangle(gram_second, own_ref)
        put_triangle(gram_first, other_ref)


def moment_kernel(kind, info_ref, *refs):
    parts, moments, block_ref = refs[:4], refs[4:6], refs[-1]
    refs = refs[6:-1]
    if kind == "m":
        left_refs, refs = refs[:2], refs[2:]
    grads, news, own_ref, other_ref = refs[:2], refs[2:4], refs[4], refs[5]
    fill_block(info_ref, parts, block_ref)
    if kind == "m":
        values = [
            block_ref[OUT_AT:TILE_AT, :],
            jnp.concatenate([block_ref[:OUT_AT, :256], block_ref[:OUT_AT, 256:]], axis=0),
        ]
        refs[6][...] = block_ref[TILE_AT : TILE_AT + STATE, :256].astype(F32)
    else:
        values = [block_ref[D:, :], block_ref[:D, :]]
    pair = []
    for value, moment, grad_ref, new_ref in zip(values, moments, grads, news):
        grad = value.astype(F32)
        grad_ref[...] = grad
        new = 0.5 * moment[...] + grad
        new_ref[...] = new
        pair.append(new)
    if kind == "o":
        put_grams(info_ref, pair, own_ref, other_ref)
        return
    mine = info_ref[2] == (0 if kind == "t" else 1)

    @pl.when(mine)
    def _():
        put_grams(info_ref, pair, own_ref, other_ref)

    @pl.when(jnp.logical_not(mine))
    def _():
        for k, ref in enumerate((own_ref, other_ref)):
            ref[...] = left_refs[k][...] if kind == "m" else jnp.zeros(ref.shape, F32)


def update_kernel(scales, kind, info_ref, *refs):
    count = 2 if kind == "o" else 4
    factors, (first_new, second_new, first_ref, second_ref, first_out, second_out, full_ref) = refs[:count], refs[count:]
    is_zero = info_ref[1] == 0
    own, other = factors[0][...], factors[1][...]
    if kind != "o":
        mine = info_ref[2] == (0 if kind == "t" else 1)
        own, other = jnp.where(mine, own, factors[2][...]), jnp.where(mine, other, factors[3][...])
    get_triangle(jnp.where(is_zero, own, other), full_ref)
    first_out[...] = first_ref[...] - scales[0] * dot3(split_low(first_new[...]), split_low(full_ref[...]), dot_nn)
    get_triangle(jnp.where(is_zero, other, own), full_ref)
    second_out[...] = second_ref[...] - scales[1] * dot3(split_low(full_ref[...]), split_low(second_new[...]), dot_nn)


def newton_poly(a, squares):
    pair = split_low(a)
    square = dot_nn(pair[0], pair[0]) if squares == 1 else dot3(pair, pair, dot_nn)
    return (COEF_B * a + COEF_C * square).astype(BF), pair


def newton_gram(a, pair, poly):
    half = COEF_A * a + (dot_nn(pair[0], poly) + dot_nn(pair[1], poly))
    high, rest = split_low(half)
    return COEF_A * half + (dot_nn(poly, high) + dot_nn(poly, rest))


def newton_start(near_ref, far_ref, a_ref, q_ref):
    get_triangle(near_ref, a_ref, far_ref)
    rows = lax.broadcasted_iota(jnp.int32, (D, D), 0)
    columns = lax.broadcasted_iota(jnp.int32, (D, D), 1)
    gram = a_ref[...]
    trace = jnp.sum(jnp.where(rows == columns, gram, 0.0))
    inverse = 1.0 / (jnp.sqrt(jnp.full((1, 1), trace, F32)) + 1e-07)
    a = gram * (inverse * inverse)
    poly, pair = newton_poly(a, SQUARES[0])
    q_ref[...] = (jnp.where(rows == columns, COEF_A, 0.0) + poly.astype(F32)) * inverse
    a_ref[...] = newton_gram(a, pair, poly)


def newton_step(index, a_ref, q_ref, a_out, q_out):
    a, q = a_ref[...], q_ref[...]
    poly, pair = newton_poly(a, SQUARES[index])
    if index < NS_STEPS - 1:
        a_out[...] = newton_gram(a, pair, poly)
    high, rest = split_low(q)
    q_out[...] = COEF_A * q + (dot_nn(high, poly) + dot_nn(rest, poly))


def newton_kernel(near_ref, far_ref, out_ref, a_ref, q_ref):
    newton_start(near_ref, far_ref, a_ref, q_ref)
    for index in range(1, NS_STEPS):
        newton_step(index, a_ref, q_ref, a_ref, q_ref)
    put_triangle(q_ref[...], out_ref)


class Muon:
    def __init__(self, info, parts, moments, kind, left=()):
        self.info, self.kind = info, kind
        shapes = [(moment.shape, F32) for moment in moments]
        packed = ((len(triangle()) * 128, 128), F32)
        extra = [((STATE, 256), F32)] if kind == "m" else []
        outs = call(
            lambda *refs: moment_kernel(kind, *refs),
            shapes * 2 + [packed] * 2 + extra,
            (info, *parts, *moments, *left),
            scratch=[pltpu.VMEM((4 * parts[0].shape[0], D), BF)],
            smem=(0,),
            us=4.5,
        )
        self.grads, self.news, self.own, self.other, self.extra = outs[:2], outs[2:4], outs[4], outs[5], outs[6:]
        if kind != "t":
            self.got = swap_core(self.other)

    def exchange(self, *others):
        self.near = self.own + after(self.got, *others)
        self.far = swap_y(self.near)
        return (self.near,)

    def newton(self, *others):
        far = after(self.far, *others)
        (self.q,) = call(
            newton_kernel,
            [(self.near.shape, F32)],
            (self.near, far),
            scratch=[pltpu.VMEM((D, D), F32)] * 2,
            us=13.0,
        )
        return self.send()

    def arrive(self, *others):
        self.far = after(self.far, *others)
        return (self.far,)

    def send(self):
        self.factors = [self.q, swap_core(self.q)]
        if self.kind == "m":
            self.factors.append(swap_dp(self.q, 1))
        return (self.q,)

    def share(self, *others):
        self.factors[1:3] = together(self.factors[1], self.factors[2], *others)[:2]
        self.factors.append(swap_core(self.factors[2]))
        return (self.factors[2],)

    def update(self, scales, params, factors, *others):
        kind = self.kind
        news = call(
            lambda *refs: update_kernel(scales, kind, *refs),
            [(param.shape, F32) for param in params],
            (self.info, *factors[:-1], after(factors[-1], *others), *self.news, *params),
            scratch=[pltpu.VMEM((D, D), F32)],
            smem=(0,),
            us=4.5,
        )
        return [list(triple) for triple in zip(self.grads, self.news, news)]


def bit_rows(info_ref, index, half, other=False):
    bit = info_ref[2 + index]
    return pl.ds(pl.multiple_of((1 - bit if other else bit) * half, half), half)


def add_refs(one, two):
    return (one.astype(F32) + two.astype(F32)).astype(BF)


def sum_start_kernel(info_ref, mine_ref, got_ref, own_a, away_a, keep_b, send_b):
    half, rows = own_a.shape[0], mine_ref.shape[0] // 2
    own_a[...] = add_refs(mine_ref[:half, :], got_ref[:half, :])
    away_a[...] = add_refs(mine_ref[rows : rows + half, :], got_ref[rows : rows + half, :])
    quarter = half // 2
    for out, other in ((keep_b, False), (send_b, True)):
        start = bit_rows(info_ref, 0, quarter, other).start
        for k in range(2):
            here = pl.ds(pl.multiple_of(k * rows + half + start, quarter), quarter)
            out[k * quarter : (k + 1) * quarter, :] = add_refs(mine_ref[here, :], got_ref[here, :])


def sum_second_kernel(info_ref, own_a, got_a, keep_b, got_b, keep_a, send_a, own_b, away_b):
    quarter = keep_a.shape[0]
    for out, other in ((keep_a, False), (send_a, True)):
        rows = bit_rows(info_ref, 0, quarter, other)
        out[...] = add_refs(own_a[rows, :], got_a[rows, :])
    own_b[...] = add_refs(keep_b[:quarter, :], got_b[:quarter, :])
    away_b[...] = add_refs(keep_b[quarter:, :], got_b[quarter:, :])


def sum_third_kernel(info_ref, keep_a, got_a, own_b, got_b, keep, send):
    first = info_ref[3] == 0
    a = add_refs(keep_a[...], got_a[...])
    b = add_refs(own_b[...], got_b[...])

    @pl.when(first)
    def _():
        keep[...] = a
        send[...] = b

    @pl.when(jnp.logical_not(first))
    def _():
        keep[...] = b
        send[...] = a


def sum_more_kernel(index, info_ref, keep_in, got, keep, send):
    half = keep.shape[0]
    for out, other in ((keep, False), (send, True)):
        rows = bit_rows(info_ref, index, half, other)
        out[...] = add_refs(keep_in[rows, :], got[rows, :])


def sum_join_kernel(index, info_ref, own, got, out):
    half = own.shape[0]
    out[bit_rows(info_ref, index, half), :] = own[...]
    out[bit_rows(info_ref, index, half, True), :] = got[...]


class SmallSum:
    def __init__(self, values):
        self.values = values
        self.moves = [swap_core, swap_y] + [lambda v, bit=bit: swap_dp(v, bit) for bit in dp_bits()]
        self.start()

    def start(self):
        self.got = self.moves.pop(0)(self.values)

    def step(self, *others):
        if self.got is None:
            return others
        self.values = self.values + after(self.got, *others)
        self.got = None
        if self.moves:
            self.start()
        return (self.values,)


class Sum:
    def __init__(self, info, mine, got):
        self.info = info
        self.inputs = (mine, got)
        self.rows, self.width = mine.shape[0] // 2, mine.shape[1]
        self.bits = dp_bits()

    def run(self, kernel, rows, args, scratch=()):
        outs = [((count, self.width), BF) for count in rows]
        return call(kernel, outs, (self.info, *args), scratch=scratch, smem=(0,), us=0.8)

    def start(self):
        half = self.rows // 2
        self.own_a, away_a, self.keep_b, send_b = self.run(sum_start_kernel, [half] * 4, self.inputs)
        self.got = (swap_y(away_a), swap_dp(send_b, self.bits[0]))
        return (away_a,)

    def second(self, *others):
        quarter = self.rows // 4
        got_a, got_b = (after(value, *others) for value in self.got)
        self.keep_a, send_a, self.own_b, away_b = self.run(
            sum_second_kernel, [quarter] * 4, (self.own_a, got_a, self.keep_b, got_b)
        )
        self.got = (swap_dp(send_a, self.bits[0]), swap_y(away_b))
        return (send_a,)

    def third(self, *others):
        quarter = self.rows // 4
        got_a, got_b = (after(value, *others) for value in self.got)
        self.keep, send = self.run(sum_third_kernel, [quarter] * 2, (self.keep_a, got_a, self.own_b, got_b))
        self.got = swap_dp(send, self.bits[1])
        self.count = quarter
        self.index = 2
        return (send,)

    def more(self, *others):
        got = after(self.got, *others)
        if self.index < len(self.bits):
            self.count //= 2
            index = self.index
            self.keep, send = self.run(
                lambda *refs: sum_more_kernel(index, *refs), [self.count] * 2, (self.keep, got)
            )
            self.got = swap_dp(send, self.bits[index])
            self.index += 1
            return (send,)
        self.block = add_low(self.keep, got)
        self.gather_start()
        return (self.block,)

    def gather_start(self):
        self.index -= 1
        if self.index >= 2:
            self.got = swap_dp(self.block, self.bits[self.index])
        else:
            self.near = swap_dp(self.block, self.bits[1])
            self.across = swap_dp(self.block, self.bits[0])

    def gather(self, *others):
        got = after(self.got, *others)
        index = self.index
        self.count *= 2
        (self.block,) = self.run(lambda *refs: sum_join_kernel(index, *refs), [self.count], (self.block, got))
        self.gather_start()
        return (self.block,)

    def finish(self, *others):
        near, across = together(self.near, self.across, *others)[:2]
        self.parts = (self.block, near, across, swap_dp(near, self.bits[0]))
        return (near,)


def halo(low, high):
    before = lax.ppermute(high, "mp", [(i, i + 1) for i in range(N_MP - 1)])
    after = lax.ppermute(low, "mp", [(i + 1, i) for i in range(N_MP - 1)])
    return before, after


def body(
    inputs,
    segments,
    cotangent,
    inner_first,
    outer_first,
    mixer_input,
    mixer_output,
    inner_second,
    outer_second,
    norm_params,
    conv_taps,
    state_maps,
    state_rates,
    inner_first_moment,
    outer_first_moment,
    mixer_input_moment,
    mixer_output_moment,
    inner_second_moment,
    outer_second_moment,
    norm_params_moment,
    conv_taps_moment,
    state_maps_moment,
    state_rates_moment,
):
    frames = inputs.shape[0]
    padded = -(-frames // ROW_CHUNK) * ROW_CHUNK
    more = padded - frames
    me = lax.axis_index("mp")
    own_states = HEADS // N_MP * STATE
    n_states = HEADS * STATE
    wide = 256
    bits = dp_bits()
    dp = lax.axis_index("dp")
    info = jnp.stack([me, me % 2] + [(dp // bit) % 2 for bit in bits])
    x_upper = dp % 2 == 1
    unit = 16 * lax.axis_size("dp")
    pack_rows = -(-(RATES_AT + 16) // unit) * unit
    tail_rows = -(-(2 * D + TILE_AT + STATE) // unit) * unit - 2 * D

    own_one = [inner_first.astype(BF), outer_first.astype(BF)]
    y_halves = [
        swap_y(jnp.where(x_upper, value[D // 2 :], value[: D // 2])) for value in own_one
    ]
    core_one = [swap_core(value) for value in own_one]
    own_two = [inner_second.astype(BF), outer_second.astype(BF)]
    maps_tile = jnp.transpose(state_maps, (2, 1, 0, 3)).reshape(STATE, wide)
    rates_row = jnp.tile(state_rates.reshape(1, own_states), (1, N_MP))
    rates_one = rates_row.astype(BF)
    rates_rest = rates_row - rates_one.astype(F32)
    rates_two = rates_rest.astype(BF)
    rates_three = (rates_rest - rates_two.astype(F32)).astype(BF)
    rates_tile = jnp.pad(
        jnp.concatenate([rates_one, rates_two, rates_three], axis=0), ((0, pack_rows - RATES_AT - 3), (0, 0))
    )
    own_mixer = jnp.concatenate(
        [
            mixer_input.reshape(D, wide).astype(BF),
            mixer_output[:, :wide].astype(BF),
            mixer_output[:, wide:].astype(BF),
            maps_tile.astype(BF),
            rates_tile,
        ],
        axis=0,
    )
    norm_rows = norm_params.reshape(10, D)
    x = jnp.pad(inputs, ((0, more), (0, 0)))
    cot = jnp.pad(cotangent, ((0, more), (0, 0)))
    taps = jnp.pad(conv_taps, ((0, 1), (0, 0)))
    past, future, bounds = call(
        lambda info_ref, *refs: place_kernel(info_ref, frames, *refs),
        [((padded, 128), jnp.int32), ((padded, 128), jnp.int32), ((8, 128), jnp.int32)],
        (info, segments),
        smem=(0,),
    )
    y_halves[0] = after(y_halves[0], own_mixer, *own_two, norm_rows, x, past)
    y_one = []
    for half in y_halves:
        across = swap_dp(half, 1)
        y_one.append(
            jnp.concatenate([jnp.where(x_upper, across, half), jnp.where(x_upper, half, across)], axis=0)
        )
    both_one = [swap_core(value) for value in y_one]
    one_refs = []
    for group in (own_one, y_one, core_one, both_one):
        one_refs.extend(group)
    own_mixer = after(own_mixer, y_halves[1])
    half = pack_rows // 2
    mixer_half = swap_y(jnp.where(x_upper, own_mixer[half:], own_mixer[:half]))
    core_mixer = swap_core(own_mixer)
    send_half = after(jnp.where(x_upper, own_two[1], own_two[0]), own_mixer)
    two_half = swap_y(send_half)
    core_two = [swap_core(after(value, mixer_half)) for value in own_two]
    mixer_across = swap_dp(mixer_half, 1)

    frame_shape = (padded, D)
    hidden_shape = (padded, FF)
    state_shape = (padded, n_states)
    edge = ((16, D), BF)
    frame_scratch = pltpu.VMEM((padded + 32, D), F32)
    map_scratch = pltpu.VMEM((n_states, D), BF)
    out_scratch = pltpu.VMEM((D, D), BF)

    act_one, gated_one, slope_one, stream_one = call(
        first_kernel,
        [(frame_shape, BF), (hidden_shape, BF), (hidden_shape, BF), (frame_shape, F32)],
        (after(x, send_half), norm_rows, *one_refs),
        us=6.6,
    )
    mixer_across = after(mixer_across, stream_one)
    y_mixer = jnp.concatenate(
        [jnp.where(x_upper, mixer_across, mixer_half), jnp.where(x_upper, mixer_half, mixer_across)], axis=0
    )
    wm = jnp.stack([own_mixer, y_mixer, core_mixer, swap_core(y_mixer)])
    two_half = after(two_half, stream_one, y_mixer)
    two_across = swap_dp(two_half, 1)
    act_two, signal, gate, driven, states_local, final = call(
        lambda *refs: mixer_in_kernel(frames, *refs),
        [(frame_shape, BF), (frame_shape, BF), (frame_shape, F32), (state_shape, F32), (state_shape, F32), ((8, n_states), F32)],
        (info, after(stream_one, two_half), norm_rows, wm, past),
        scratch=[map_scratch],
        smem=(0,),
        us=4.2,
    )
    finals = lax.all_gather(final, "mp", axis=0, tiled=True)
    states, carry_in, result, mixed, stream_two, act_three, low, high = call(
        lambda *refs: mixer_out_kernel(frames, *refs),
        [(state_shape, F32), ((8, n_states), F32), (frame_shape, F32), (frame_shape, BF), (frame_shape, F32), (frame_shape, F32), edge, edge],
        (info, states_local, finals, past, bounds, wm, gate, stream_one, norm_rows),
        scratch=[map_scratch, out_scratch],
        smem=(0,),
        us=2.1,
    )
    act_before, act_after = halo(low, high)
    two_across = after(two_across, stream_two)
    y_two = [jnp.where(x_upper, two_across, two_half), jnp.where(x_upper, two_half, two_across)]
    both_two = [swap_core(value) for value in y_two]
    two_refs = []
    for group in (own_two, y_two, core_two, both_two):
        two_refs.extend(group)
    layer_output, act_four, gated_four, grad_pre_four, back_four, grad_three, grad_conv, low, high, norm_high = call(
        lambda *refs: second_kernel(frames, *refs),
        [
            ((frames, D), BF), (frame_shape, BF), (hidden_shape, BF), (hidden_shape, BF), (frame_shape, BF),
            (frame_shape, F32), (frame_shape, F32), edge, edge, ((32, D), F32),
        ],
        (act_three, act_before, act_after, past, future, taps, stream_two, norm_rows, *two_refs, cot),
        scratch=[frame_scratch, pltpu.VMEM(frame_shape, F32), pltpu.VMEM(hidden_shape, BF), pltpu.VMEM(frame_shape, BF)],
        us=16.6,
    )
    grad_before, grad_after = halo(low, high)
    send_two = weight_grads(2, act_four, gated_four, grad_pre_four, back_four)
    keep_two = weight_grads(0, act_four, gated_four, grad_pre_four, back_four)
    got_two = swap_core(send_two)

    grad_two, back_two, grad_result, grad_gate, adjoint, first, taps_part, norm_two = call(
        lambda *refs: conv_back_kernel(frames, *refs),
        [
            (frame_shape, F32), (frame_shape, BF), (frame_shape, BF), (frame_shape, BF), (state_shape, F32),
            ((8, n_states), F32), ((8 * KSIZE, D), F32), ((16, D), F32),
        ],
        (
            info, act_three, act_before, act_after, grad_conv, grad_before, grad_after, past, future, taps,
            after(grad_three, keep_two, send_two), stream_two, norm_rows, wm, gate, result,
        ),
        scratch=[frame_scratch, frame_scratch, pltpu.VMEM(frame_shape, F32), map_scratch, out_scratch],
        smem=(0,),
        us=11.8,
    )
    firsts = lax.all_gather(first, "mp", axis=0, tiled=True)
    sum_two = Sum(info, keep_two, after(got_two, firsts))
    started = sum_two.start()
    grad_one, keep_mixer, send_mixer, rates_part, norm_one = call(
        lambda *refs: mixer_back_kernel(frames, *refs),
        [(frame_shape, F32), ((2 * tail_rows, D), BF), ((2 * tail_rows, D), BF), ((8, n_states), F32), ((16, D), F32)],
        (
            info, adjoint, firsts, past, future, bounds, states, carry_in, driven, wm, signal, grad_gate,
            act_two, stream_one, norm_rows, after(grad_two, *started), mixed, back_two, grad_result,
        ),
        scratch=[
            pltpu.VMEM(state_shape, BF), map_scratch, pltpu.VMEM(frame_shape, BF), pltpu.VMEM((N_MP, tail_rows, D), BF)
        ],
        smem=(0,),
        us=5.5,
    )
    got_mixer = swap_core(send_mixer)
    extra_bits = len(bits) - 2
    wide_shape = mixer_input.shape
    first_scale = 0.5 * math.sqrt(max(D, FF) / D)
    second_scale = 0.5 * math.sqrt(max(D, FF) / FF)
    made = {}

    def first_back(*others):
        made["pre"], made["back"], made["act"] = call(
            first_back_kernel,
            [(hidden_shape, BF), (frame_shape, BF), (frame_shape, F32)],
            (after(grad_one, *others), slope_one, *one_refs),
            us=5.4,
        )
        return (made["back"],)

    def first_send(*others):
        made["send"] = weight_grads(2, act_one, gated_one, made["pre"], after(made["back"], *others))
        made["got"] = swap_core(made["send"])
        return (made["send"],)

    def first_keep(*others):
        made["keep"] = weight_grads(0, act_one, gated_one, made["pre"], after(made["back"], *others))
        return (made["keep"],)

    def first_start(*others):
        made["o"] = Sum(info, made["keep"], after(made["got"], *others))
        return made["o"].start()

    def mixer_start(*others):
        made["m"] = Sum(info, keep_mixer, after(got_mixer, *others))
        return made["m"].start()

    made["t"] = sum_two

    def steps_of(chain, moments, scales, params):
        def step(name):
            return lambda *others: getattr(made[chain], name)(*others)

        def several(name):
            def run(*others):
                for _ in range(extra_bits - 1):
                    others = getattr(made[chain], name)(*others)
                return getattr(made[chain], name)(*others)

            return run

        def moment(*others):
            parts = tuple(after(v, *others) for v in made[chain].parts)
            left = (made["tx"].own, made["tx"].other) if chain == "m" else ()
            made[chain + "x"] = Muon(info, parts, moments, chain, left)
            return (made[chain + "x"].own,)

        def muon(name):
            return lambda *others: getattr(made[chain + "x"], name)(*others)

        def update(*others):
            factors = made["ox" if chain == "o" else "mx"].factors
            made[chain + "r"] = made[chain + "x"].update(scales, params, factors, *others)
            return (made[chain + "r"][0][2],)

        head = [
            step("second"), step("third"), several("more"), step("more"), several("gather"), step("finish"), moment
        ]
        middle = {"t": [], "o": ["exchange", "newton"], "m": ["exchange", "arrive", "newton", "share"]}[chain]
        return head + [muon(name) for name in middle] + [update]

    def input_step(*others):
        input_grad, small = call(
            lambda *refs: input_grad_kernel(frames, *refs),
            [((frames, D), F32), ((32, D), F32)],
            (x, after(made["act"], *others), norm_rows, grad_one, norm_one, norm_two, norm_high, taps_part, rates_part),
            scratch=[pltpu.VMEM(frame_shape, F32), pltpu.VMEM((16, D), F32)],
            us=2.4,
        )
        made["input_grad"], made["s"] = input_grad, SmallSum(small)
        return (small,)

    def small_step(*others):
        return made["s"].step(*others)

    def small_last(*others):
        while made["s"].got is not None:
            others = made["s"].step(*others)
        return others

    def small_params(*others):
        small = after(made["s"].values, *others)
        mixer = made["mx"]
        norm_sum = small[:10].reshape(norm_params.shape)
        taps_sum = small[10 : 10 + KSIZE]
        rates_sum = lax.dynamic_slice_in_dim(small[10 + KSIZE], me * own_states, own_states, 0).reshape(state_rates.shape)
        maps_sum = jnp.transpose(mixer.extra[0].reshape(STATE, 2, HEADS // N_MP, HD), (2, 1, 0, 3))
        tokens_all = frames * lax.axis_size("dp") * lax.axis_size("mp")
        small_results = []
        for factor, grad, moment, param in (
            (SMALL_FACTORS[0], norm_sum, norm_params_moment, norm_params),
            (SMALL_FACTORS[1], taps_sum, conv_taps_moment, conv_taps),
            (SMALL_FACTORS[2], maps_sum, state_maps_moment, state_maps),
            (SMALL_FACTORS[3], rates_sum, state_rates_moment, state_rates),
        ):
            moment_new = 0.5 * moment + grad
            small_results.extend((grad, moment_new, param - factor / math.sqrt(tokens_all) * moment_new))
        made["small"] = small_results
        made["in"] = [values[1].reshape(wide_shape) for values in (mixer.grads, mixer.news)]
        return (*small_results, *made["in"])

    chains = {
        "t": steps_of("t", (outer_second_moment, inner_second_moment), (second_scale, first_scale), (outer_second, inner_second)),
        "m": [mixer_start]
        + steps_of(
            "m", (mixer_output_moment, mixer_input_moment.reshape(D, wide)), (0.5, 0.5 * math.sqrt(2.0)),
            (mixer_output, mixer_input.reshape(D, wide)),
        ),
        "o": [first_back, first_send, first_keep, first_start]
        + steps_of("o", (outer_first_moment, inner_first_moment), (second_scale, first_scale), (outer_first, inner_first)),
        "s": [input_step] + [small_step] * 4 + [small_last],
        "p": [small_params],
    }
    started = (grad_one,)
    for name in ORDER:
        started = chains[name].pop(0)(*started)
    input_grad, small_results = made["input_grad"], made["small"]
    down_two, up_two = made["tr"]
    down_one, up_one = made["or"]
    out_triple, in_triple = made["mr"]
    in_triple = [*made["in"], in_triple[2].reshape(wide_shape)]
    results = [layer_output, input_grad]
    for triple in (up_one, down_one, in_triple, out_triple, up_two, down_two):
        results.extend(triple)
    results.extend(small_results)
    return tuple(results)


def solution(mesh):
    in_specs = (
        P(("dp", "mp"), None),
        P("dp", None),
        P(("dp", "mp"), None),
        P(None, "mp"),
        P("mp", None),
        P(None, None, "mp"),
        P("mp", None),
        P(None, "mp"),
        P("mp", None),
        P(),
        P(),
        P("mp", None, None, None),
        P("mp", None),
        P(None, "mp"),
        P("mp", None),
        P(None, None, "mp"),
        P("mp", None),
        P(None, "mp"),
        P("mp", None),
        P(),
        P(),
        P("mp", None, None, None),
        P("mp", None),
    )
    out_specs = (
        P(("dp", "mp"), None),
        P(("dp", "mp"), None),
        P(None, "mp"),
        P(None, "mp"),
        P(None, "mp"),
        P("mp", None),
        P("mp", None),
        P("mp", None),
        P(None, None, "mp"),
        P(None, None, "mp"),
        P(None, None, "mp"),
        P("mp", None),
        P("mp", None),
        P("mp", None),
        P(None, "mp"),
        P(None, "mp"),
        P(None, "mp"),
        P("mp", None),
        P("mp", None),
        P("mp", None),
        P(),
        P(),
        P(),
        P(),
        P(),
        P(),
        P("mp", None, None, None),
        P("mp", None, None, None),
        P("mp", None, None, None),
        P("mp", None),
        P("mp", None),
        P("mp", None),
    )
    return jax.shard_map(body, mesh=mesh, in_specs=in_specs, out_specs=out_specs, check_vma=False)
```
